128 devices in a mesh: ctx: 32 (over x_lo, z, y), fsdp: 4 (over x_hi, core).
Axes of the slice: x: 4 (x_hi: 2, x_lo: 2; x = x_hi * 2 + x_lo), y: 4, z: 4, core: 2. Of those that a mesh axis runs over, the one named last changes fastest.
Arguments:
- hidden_in: bfloat16 [4, 4096, 1024], P('fsdp', 'ctx'), may hold values from -6 to 6
- positions: int32 [4, 4096], P('fsdp', 'ctx'), may hold values from 0 to 4095, as said below
- out_grad: bfloat16 [4, 4096, 1024], P('fsdp', 'ctx'), may hold values from -6 to 6
- ln1_gain: bfloat16 [1024], P('fsdp'), may hold values from 0.099609375 to 1.8984375
- ln1_bias: bfloat16 [1024], P('fsdp'), may hold values from -3 to 3
- qkv_weight: bfloat16 [1024, 3072], P('fsdp'), may hold values from -0.1875 to 0.1875
- qkv_bias: bfloat16 [3072], P('fsdp'), may hold values from -3 to 3
- out_weight: bfloat16 [1024, 1024], P('fsdp'), may hold values from -4 to 4
- out_bias: bfloat16 [1024], P('fsdp'), may hold values from -3 to 3
- ln2_gain: bfloat16 [1024], P('fsdp'), may hold values from 0.099609375 to 1.8984375
- ln2_bias: bfloat16 [1024], P('fsdp'), may hold values from -3 to 3
- fc1_weight: bfloat16 [1024, 4096], P('fsdp'), may hold values from -0.1875 to 0.1875
- fc1_bias: bfloat16 [4096], P('fsdp'), may hold values from -3 to 3
- fc2_weight: bfloat16 [4096, 1024], P('fsdp'), may hold values from -0.1875 to 0.1875
- fc2_bias: bfloat16 [1024], P('fsdp'), may hold values from -3 to 3
Outputs:
- block_out: bfloat16 [4, 4096, 1024], P('fsdp', 'ctx')
- input_grad: bfloat16 [4, 4096, 1024], P('fsdp', 'ctx')
- ln1_gain_grad: float32 [1024], P('fsdp')
- ln1_bias_grad: float32 [1024], P('fsdp')
- qkv_weight_grad: float32 [1024, 3072], P('fsdp')
- qkv_bias_grad: float32 [3072], P('fsdp')
- out_weight_grad: float32 [1024, 1024], P('fsdp')
- out_bias_grad: float32 [1024], P('fsdp')
- ln2_gain_grad: float32 [1024], P('fsdp')
- ln2_bias_grad: float32 [1024], P('fsdp')
- fc1_weight_grad: float32 [1024, 4096], P('fsdp')
- fc1_bias_grad: float32 [4096], P('fsdp')
- fc2_weight_grad: float32 [4096, 1024], P('fsdp')
- fc2_bias_grad: float32 [1024], P('fsdp')
The draws below stay inside these ranges and needn't reach their ends.
Inputs may be any that keep to these rules, and one draw needn't show every extreme that they name: Each sequence's positions are a permutation of 0 to 4095. The rows of a device are two runs of 64 ascending consecutive positions. Counting runs of 64 positions, device i along ctx holds either runs 2i and 2i + 1, or runs i and 63 - i; which of the two is drawn for each sequence.
All inputs are finite; a program needn't handle non-finite values.
Results may differ from the reference program's by a relative error of at most 0.025.
Values may be sent and summed in bfloat16 or wider, within the bound.
No kernel may reach another device: no remote copies, remote signals or barrier semaphores. Data moves between devices by JAX's collectives and lax.ppermute only.
A program may use at most 192 MiB of HBM per device.

```python
import jax
import jax.numpy as jnp
from jax import lax

D = 1024
H = 16
HD = 64
ROT = 16
FF = 4096
TOK_DEV = 128
SEQS = 4
LEN = 4096


def draw_positions(key, part):
    key = jax.random.fold_in(key, 11)
    half_run = TOK_DEV // 2
    groups = LEN // TOK_DEV
    orders = jax.random.randint(key, (SEQS, 1, 1), 0, 2)
    device = jnp.arange(groups, dtype=jnp.int32).reshape(1, groups, 1)
    within = jnp.arange(TOK_DEV, dtype=jnp.int32).reshape(1, 1, TOK_DEV)
    upper = within // half_run
    drawn = 2 * device + upper
    folded = jnp.where(upper == 0, device, 2 * groups - 1 - device)
    run_index = jnp.where(orders == 1, folded, drawn)
    return (run_index * half_run + within % half_run).reshape(SEQS, LEN).astype(jnp.int32)


def block_scale(own_key, dims, shards, low, largest):
    loudness = 1.0
    for position, parts in shards:
        heights = jax.random.uniform(jax.random.fold_in(jax.random.fold_in(own_key, 6), position), (parts,), jnp.float32, low / len(shards), largest / len(shards))
        loudness = loudness * jnp.repeat(jnp.exp(heights), dims[position] // parts).reshape((-1,) + (1,) * (len(dims) - 1 - position))
    return loudness


def bell_draw(stream_key, shape, deviation, reach, cuts=(), held_as=jnp.bfloat16):
    drawn = deviation * jax.random.normal(stream_key, shape, jnp.float32)
    if cuts:
        drawn = drawn * block_scale(stream_key, shape, cuts, -0.22, 0.18)
    return jnp.clip(drawn, -reach, reach).astype(held_as)


def setup_inputs(seed: int = 0) -> dict:
    seeds = jax.random.split(jax.random.key(seed), 16)
    return {
        "hidden_in": bell_draw(seeds[0], (SEQS, LEN, D), 1.0, 6.0, ((0, 4), (1, 32))),
        "positions": draw_positions(jax.random.fold_in(seeds[15], 71), 0),
        "out_grad": bell_draw(seeds[2], (SEQS, LEN, D), 1.0, 6.0, ((0, 4), (1, 32))),
        "ln1_gain": jnp.clip(1.0 + 0.18 * jax.random.normal(seeds[3], (D,), jnp.float32), 0.099609375, 1.8984375).astype(jnp.bfloat16),
        "ln1_bias": bell_draw(seeds[4], (D,), 0.3, 3.0, ((0, 4),)),
        "qkv_weight": bell_draw(seeds[5], (D, 3 * D), D ** -0.5, 0.1875, ((0, 4),)),
        "qkv_bias": bell_draw(seeds[6], (3 * D,), 0.3, 3.0, ((0, 4),)),
        "out_weight": bell_draw(seeds[7], (D, D), (max(1, 8 * D // LEN)) ** -0.5, 4.0, ((0, 4),)),
        "out_bias": bell_draw(seeds[8], (D,), 0.3, 3.0, ((0, 4),)),
        "ln2_gain": jnp.clip(1.0 + 0.18 * jax.random.normal(seeds[9], (D,), jnp.float32), 0.099609375, 1.8984375).astype(jnp.bfloat16),
        "ln2_bias": bell_draw(seeds[10], (D,), 0.3, 3.0, ((0, 4),)),
        "fc1_weight": bell_draw(seeds[11], (D, FF), D ** -0.5, 0.1875, ((0, 4),)),
        "fc1_bias": bell_draw(seeds[12], (FF,), 0.3, 3.0, ((0, 4),)),
        "fc2_weight": bell_draw(seeds[13], (FF, D), (FF // 4) ** -0.5, 0.1875, ((0, 4),)),
        "fc2_bias": bell_draw(seeds[14], (D,), 0.3, 3.0, ((0, 4),)),
    }


@jax.custom_vjp
def low(v):
    return lax.optimization_barrier(v.astype(jnp.bfloat16)).astype(jnp.float32)

@jax.custom_vjp
def low_back(v):
    return v

def low_keep(v):
    return (low(v), None)

def low_pass(kept, grad):
    return (grad,)

def back_keep(v):
    return (v, None)

def back_low(kept, grad):
    return (low(grad),)
low.defvjp(low_keep, low_pass)
low_back.defvjp(back_keep, back_low)
norm_eps = 1e-05
exact_mode = lax.Precision.HIGHEST

def layer_norm(values, gain):
    average = lax.optimization_barrier(jnp.mean(values, axis=-1, keepdims=True))
    centred = values - average
    variance = lax.optimization_barrier(jnp.mean(centred * centred, axis=-1, keepdims=True))
    return centred * lax.rsqrt(variance + norm_eps) * gain

def rotate(values, cosines, sine_part):
    half_rot = ROT // 2
    lower_half = values[..., :half_rot]
    upper_half = values[..., half_rot:ROT]
    return jnp.concatenate([lower_half * cosines - upper_half * sine_part, upper_half * cosines + lower_half * sine_part, values[..., ROT:]], axis=-1)

def angles(places):
    frequency = 10000.0 ** (-2.0 * jnp.arange(ROT // 2, dtype=jnp.float32) / ROT)
    phases = places.astype(jnp.float32)[:, None] * frequency[None, :]
    return (jnp.cos(phases)[:, None, :], jnp.sin(phases)[:, None, :])

def attend_block(queries, key_rows, value_rows, query_places, key_places):
    scores = jnp.einsum('qhd,khd->hqk', queries, key_rows, precision=exact_mode)
    allowed = key_places[None, None, :] <= query_places[None, :, None]
    scores = low_back(jnp.where(allowed, scores, -1e+30))
    row_top = lax.optimization_barrier(jnp.max(scores, axis=-1, keepdims=True))
    unnormed = jnp.exp(scores - row_top)
    probabilities = unnormed / lax.optimization_barrier(jnp.sum(unnormed, axis=-1, keepdims=True))
    return jnp.einsum('hqk,khd->qhd', low(probabilities), value_rows, precision=exact_mode)

def forward(weights, inputs, places):
    gain_one, shift_one, w_qkv, b_qkv, w_out, b_out, gain_two, shift_two, w_up, b_up, w_down, b_down = weights
    length = inputs.shape[0]
    model_width = inputs.shape[1]
    attn_in = low(layer_norm(inputs, gain_one) + shift_one)
    projected = low_back(jnp.dot(attn_in, w_qkv, precision=exact_mode) + b_qkv)
    cosines, sine_part = angles(places)
    score_scale = HD ** (-0.5)
    queries = low(rotate(projected[:, :model_width].reshape(length, H, HD), cosines, sine_part) * score_scale)
    key_rows = low(rotate(projected[:, model_width:2 * model_width].reshape(length, H, HD), cosines, sine_part))
    value_rows = low(projected[:, 2 * model_width:].reshape(length, H, HD))
    block_len = min(512, length)
    block_count = length // block_len
    head_out = lax.map(jax.checkpoint(lambda pieces: attend_block(pieces[0], key_rows, value_rows, pieces[1], places)), (queries.reshape(block_count, block_len, H, HD), places.reshape(block_count, block_len)))
    head_out = low(low_back(head_out.reshape(length, model_width)))
    attn_out = jnp.dot(head_out, w_out, precision=exact_mode) + b_out
    mlp_in = low(layer_norm(inputs, gain_two) + shift_two)
    pre_act = low_back(jnp.dot(mlp_in, w_up, precision=exact_mode) + b_up)
    activated = low(jax.nn.gelu(pre_act, approximate=False))
    return inputs + attn_out + jnp.dot(activated, w_down, precision=exact_mode) + b_down

def reference(hidden_in, positions, out_grad, ln1_gain, ln1_bias, qkv_weight, qkv_bias, out_weight, out_bias, ln2_gain, ln2_bias, fc1_weight, fc1_bias, fc2_weight, fc2_bias):
    weights = tuple((weight_arg.astype(jnp.float32) for weight_arg in (ln1_gain, ln1_bias, qkv_weight, qkv_bias, out_weight, out_bias, ln2_gain, ln2_bias, fc1_weight, fc1_bias, fc2_weight, fc2_bias)))

    def per_sequence(grad_sums, pieces):
        inputs, places, out_cot = pieces
        block_out, pullback = jax.vjp(lambda params, values: forward(params, values, places), weights, inputs.astype(jnp.float32))
        grad_terms, input_grad = pullback(out_cot.astype(jnp.float32))
        grad_sums = jax.tree.map(jnp.add, grad_sums, grad_terms)
        return (grad_sums, (block_out.astype(jnp.bfloat16), input_grad.astype(jnp.bfloat16)))
    initial = jax.tree.map(jnp.zeros_like, weights)
    grad_sums, (block_outs, input_grads) = lax.scan(per_sequence, initial, (hidden_in, positions, out_grad))
    return (block_outs, input_grads, grad_sums[0], grad_sums[1], grad_sums[2], grad_sums[3], grad_sums[4], grad_sums[5], grad_sums[6], grad_sums[7], grad_sums[8], grad_sums[9], grad_sums[10], grad_sums[11])
```

```python
import jax
import jax.numpy as jnp
from jax import lax
from jax.experimental import pallas as pl
from jax.experimental.pallas import tpu as pltpu
from jax.sharding import PartitionSpec as P

H = 16
HD = 64
ROT = 16
RUN = 64
NORM_EPS = 1e-05
BF = jnp.bfloat16
F32 = jnp.float32
NEG = -1e30

QT = 256
KT = 512


def mm(a, b):
    return jnp.dot(a, b, preferred_element_type=F32)


def contract_rows(a, b):
    return lax.dot_general(a, b, (((0,), (0,)), ((), ())), preferred_element_type=F32)


def contract_cols(a, b):
    return lax.dot_general(a, b, (((1,), (1,)), ((), ())), preferred_element_type=F32)


def swap_xh(v):
    return lax.ppermute(v, "fsdp", [(i, i ^ 2) for i in range(4)])


def swap_core(v):
    return lax.ppermute(v, "fsdp", [(i, i ^ 1) for i in range(4)])


def attention_kernel(scal, recv, out, kv, qx, yx, dkv, oq, sbuf, dbuf):
    folded = scal[0]
    odd = scal[1]
    lane = lax.broadcasted_iota(jnp.int32, (RUN, 2 * HD), 1)
    low_half = lane < HD
    n_src = recv.shape[0]
    tiles = qx.shape[0]
    per_tile = QT // RUN

    def runs(c):
        turned = jnp.logical_and(folded == 1, c % 2 == 1)
        even = jnp.where(folded == 1, jnp.where(turned, 2 * n_src - 1 - c, c), 2 * c)
        other = jnp.where(folded == 1, jnp.where(turned, c, 2 * n_src - 1 - c), 2 * c + 1)
        return even, other

    def sort_in(c, carry):
        even, other = runs(c)
        kv[pl.ds(pl.multiple_of(even * RUN, RUN), RUN), :] = recv[c, 0:RUN, :]
        kv[pl.ds(pl.multiple_of(other * RUN, RUN), RUN), :] = recv[c, RUN : 2 * RUN, :]
        rank = jnp.where(odd == 1, other, even) // 2
        tile = rank // per_tile
        place = pl.multiple_of((rank % per_tile) * RUN, RUN)
        qd = recv[c, 2 * RUN : 3 * RUN, :]
        zero = jnp.zeros_like(qd)
        q_only = jnp.where(low_half, qd, zero)
        d_only = jnp.where(low_half, zero, qd)
        qx[tile, pl.ds(place, RUN), :] = q_only
        qx[tile, pl.ds(QT + place, RUN), :] = d_only
        yx[tile, pl.ds(place, RUN), :] = d_only
        yx[tile, pl.ds(QT + place, RUN), :] = q_only
        return carry

    lax.fori_loop(0, n_src, sort_in, 0)
    dkv[...] = jnp.zeros_like(dkv)

    row = lax.broadcasted_iota(jnp.int32, (QT, KT), 0)
    col = lax.broadcasted_iota(jnp.int32, (QT, KT), 1)
    row_place = (2 * (row // RUN) + odd) * RUN + row % RUN
    allowed = col <= row_place

    def fold(v, op):
        parts = [v[:, i * 128 : (i + 1) * 128] for i in range(KT // 128)]
        total = parts[0]
        for part in parts[1:]:
            total = op(total, part)
        return total

    def tile_step(j, carry):
        x = qx[j]
        y = yx[j]

        def products(k):
            keys = kv[pl.ds(pl.multiple_of(k * KT, KT), KT), :]
            both = contract_cols(x, keys)
            return both[:QT], both[QT:]

        def pass_one(k, top):
            s, d = products(k)
            sbuf[k] = s
            dbuf[k] = d
            return jnp.maximum(top, fold(s, jnp.maximum))

        top = lax.fori_loop(0, j, pass_one, jnp.full((QT, 128), NEG, F32))
        s, d = products(j)
        s = jnp.where(allowed, s, NEG)
        sbuf[j] = s
        dbuf[j] = d
        top = jnp.maximum(top, fold(s, jnp.maximum))
        top = jnp.max(top, axis=1, keepdims=True)

        def pass_two(k, sums):
            total, weighted = sums
            e = jnp.exp(sbuf[k] - top)
            sbuf[k] = e
            return total + fold(e, jnp.add), weighted + fold(e * dbuf[k], jnp.add)

        zero = jnp.zeros((QT, 128), F32)
        total, weighted = lax.fori_loop(0, j + 1, pass_two, (zero, zero))
        scale = 1.0 / jnp.sum(total, axis=1, keepdims=True)
        delta = jnp.sum(weighted, axis=1, keepdims=True) * scale

        def pass_three(k, acc):
            rows = pl.ds(pl.multiple_of(k * KT, KT), KT)
            p = sbuf[k] * scale
            ds = p * (dbuf[k] - delta)
            a = jnp.concatenate([p.astype(BF), ds.astype(BF)], axis=0)
            dkv[rows, :] += contract_rows(a, y)
            return acc + mm(a, kv[rows, :])

        acc = lax.fori_loop(0, j + 1, pass_three, jnp.zeros((2 * QT, 2 * HD), F32))
        wide = lax.broadcasted_iota(jnp.int32, (QT, 2 * HD), 1) < HD
        oq[pl.ds(pl.multiple_of(j * QT, QT), QT), :] = jnp.where(wide, acc[QT:], acc[:QT]).astype(BF)
        return carry

    lax.fori_loop(0, tiles, tile_step, 0)

    def sort_out(c, carry):
        even, other = runs(c)
        out[c, 0:RUN, :] = dkv[pl.ds(pl.multiple_of(even * RUN, RUN), RUN), :].astype(BF)
        out[c, RUN : 2 * RUN, :] = dkv[pl.ds(pl.multiple_of(other * RUN, RUN), RUN), :].astype(BF)
        rank = jnp.where(odd == 1, other, even) // 2
        out[c, 2 * RUN : 3 * RUN, :] = oq[pl.ds(pl.multiple_of(rank * RUN, RUN), RUN), :]
        return carry

    lax.fori_loop(0, n_src, sort_out, 0)


def attention(scal, recv):
    n_src = recv.shape[0]
    keys = n_src * 2 * RUN
    queries = n_src * RUN
    tiles = queries // QT
    return pl.pallas_call(
        attention_kernel,
        out_shape=jax.ShapeDtypeStruct(recv.shape, BF),
        in_specs=[pl.BlockSpec(memory_space=pltpu.SMEM), pl.BlockSpec(memory_space=pltpu.VMEM)],
        out_specs=pl.BlockSpec(memory_space=pltpu.VMEM),
        scratch_shapes=[
            pltpu.VMEM((keys, 2 * HD), BF),
            pltpu.VMEM((tiles, 2 * QT, 2 * HD), BF),
            pltpu.VMEM((tiles, 2 * QT, 2 * HD), BF),
            pltpu.VMEM((keys, 2 * HD), F32),
            pltpu.VMEM((queries, 2 * HD), BF),
            pltpu.VMEM((keys // KT, QT, KT), F32),
            pltpu.VMEM((keys // KT, QT, KT), F32),
        ],
        compiler_params=pltpu.CompilerParams(vmem_limit_bytes=40 * 1024 * 1024),
        cost_estimate=pl.CostEstimate(
            flops=14 * HD * queries * keys // 2,
            bytes_accessed=4 * recv.size,
            transcendentals=queries * keys // 2,
        ),
        name="attention",
    )(scal, recv)


def pick(stacked, index):
    return lax.dynamic_index_in_dim(stacked, index, 0, keepdims=False)


def on_device(
    hidden_in,
    positions,
    out_grad,
    ln1_gain,
    ln1_bias,
    qkv_weight,
    qkv_bias,
    out_weight,
    out_bias,
    ln2_gain,
    ln2_bias,
    fc1_weight,
    fc1_bias,
    fc2_weight,
    fc2_bias,
):
    n_fs = 4
    n_ctx = lax.axis_size("ctx")
    ctx = lax.axis_index("ctx")
    me = lax.axis_index("fsdp")
    t = hidden_in.shape[1]
    d = hidden_in.shape[2]
    dq = d // n_fs
    heads = H // n_fs
    ff = fc1_weight.shape[1] // n_fs
    tok = n_fs * t

    run_a = positions[0, 0] // RUN
    run_b = positions[0, RUN] // RUN
    flip = run_a % 2 == 1

    def turned(v):
        return jnp.where(flip, jnp.concatenate([v[RUN:], v[:RUN]], 0), v)

    x_own = turned(hidden_in[0])
    cot_own = turned(out_grad[0])
    folded_own = (run_a + run_b == 2 * n_ctx - 1).astype(BF)

    short = jnp.concatenate(
        [ln1_gain, ln1_bias, ln2_gain, ln2_bias, out_bias, fc2_bias, qkv_bias, jnp.full((dq,), folded_own)]
    )
    short = jnp.pad(short.reshape(-1, dq), ((0, 6), (0, d - dq)))
    message = jnp.concatenate([x_own, cot_own, short], 0)
    pair = jnp.stack([message, swap_xh(message)])
    everyone = jnp.concatenate([pair, swap_core(pair)], 0)

    w_qkv_parts = qkv_weight.reshape(dq, 3, n_fs, dq).transpose(2, 0, 1, 3).reshape(n_fs, dq, 3 * dq)
    w_qkv = lax.all_to_all(w_qkv_parts, "fsdp", 0, 0).reshape(d, 3 * dq)
    w_up_parts = fc1_weight.reshape(dq, n_fs, ff).transpose(1, 0, 2)
    w_up = lax.all_to_all(w_up_parts, "fsdp", 0, 0).reshape(d, ff)

    inputs = everyone[:, :t].reshape(tok, d).astype(F32)
    cot = everyone[:, t : 2 * t].reshape(tok, d)
    short_rel = everyone[:, 2 * t : 2 * t + 10, :dq]

    def rel_of(owner):
        diff = jnp.bitwise_xor(me, owner)
        return (diff % 2) * 2 + diff // 2

    short_abs = jnp.stack([pick(short_rel, rel_of(o)) for o in range(n_fs)]).astype(F32)
    gain_one, shift_one, gain_two, shift_two, b_out, b_down = (
        short_abs[:, i].reshape(1, d) for i in range(6)
    )
    b_qkv = short_abs[:, 6:9].reshape(3, n_fs, dq)
    b_qkv = lax.dynamic_index_in_dim(b_qkv, me, 1, keepdims=False).reshape(1, 3 * dq)
    folded = short_rel[:, 9, 0] > 0.5

    average = jnp.mean(inputs, axis=-1, keepdims=True)
    centred = inputs - average
    variance = jnp.mean(centred * centred, axis=-1, keepdims=True)
    rstd = lax.rsqrt(variance + NORM_EPS)
    xhat = centred * rstd
    attn_in = (xhat * gain_one + shift_one).astype(BF)
    mlp_in = (xhat * gain_two + shift_two).astype(BF)

    half = ROT // 2
    back = ctx % 2 == 1
    even_run = jnp.where(folded, jnp.where(back, 2 * n_ctx - 1 - ctx, ctx), 2 * ctx)
    odd_run = jnp.where(folded, jnp.where(back, ctx, 2 * n_ctx - 1 - ctx), 2 * ctx + 1)
    starts = jnp.stack([even_run, odd_run], 1) * RUN
    places = (starts[:, :, None] + jnp.arange(RUN)[None, None, :]).reshape(tok).astype(F32)
    frequency = 10000.0 ** (-2.0 * jnp.arange(half, dtype=F32) / ROT)
    phases = places[:, None] * frequency[None, :]
    cosines, sines = jnp.cos(phases), jnp.sin(phases)
    rest = jnp.zeros((tok, HD - ROT), F32)
    cos_row = jnp.tile(jnp.concatenate([cosines, cosines, rest + 1.0], 1), (1, heads))
    sin_up = jnp.tile(jnp.concatenate([-sines, jnp.zeros_like(sines), rest], 1), (1, heads))
    sin_down = jnp.tile(jnp.concatenate([jnp.zeros_like(sines), sines, rest], 1), (1, heads))

    def rotate(v, sign):
        ahead = jnp.concatenate([v[:, half:], v[:, :half]], 1)
        behind = jnp.concatenate([v[:, -half:], v[:, :-half]], 1)
        return v * cos_row + (ahead * sin_up + behind * sin_down) * sign

    score_scale = HD ** (-0.5)
    projected = mm(attn_in, w_qkv) + b_qkv
    queries = (rotate(projected[:, :dq], 1.0) * score_scale).astype(BF)
    keys = rotate(projected[:, dq : 2 * dq], 1.0).astype(BF)
    values = projected[:, 2 * dq :].astype(BF)
    d_heads = contract_cols(cot, out_weight).astype(BF)

    def by_head(a, b):
        both = jnp.concatenate(
            [a.reshape(n_fs, t, heads, HD), b.reshape(n_fs, t, heads, HD)], -1
        )
        return both.transpose(0, 2, 1, 3)

    kv_send = by_head(keys, values)
    qd_send = by_head(queries, d_heads).reshape(n_fs, heads, 2, RUN, 2 * HD)
    send = jnp.concatenate(
        [jnp.broadcast_to(kv_send[:, :, None], (n_fs, heads, 2, t, 2 * HD)), qd_send], 3
    ).reshape(n_ctx, t + RUN, 2 * HD)
    recv = lax.all_to_all(send, "ctx", 0, 0)
    my_folded = pick(folded, ctx // (2 * heads)).astype(jnp.int32)
    scal = jnp.stack([my_folded, ctx % 2]).astype(jnp.int32)
    grads = attention(scal, recv)
    home = lax.all_to_all(grads, "ctx", 0, 0).reshape(n_fs, heads, 2, t + RUN, 2 * HD)

    pre_act = mm(mlp_in, w_up) + fc1_bias.astype(F32)[None]
    act_float, pull_act = jax.vjp(lambda v: jax.nn.gelu(v, approximate=False), pre_act)
    activated = act_float.astype(BF)
    d_pre = pull_act(contract_cols(cot, fc2_weight))[0].astype(BF)
    mlp_part = mm(activated, fc2_weight)
    fc2_grad = contract_rows(activated, cot).astype(BF)
    fc1_grad = contract_rows(mlp_in, d_pre).astype(BF)
    fc1_bias_grad = jnp.sum(d_pre, axis=0, dtype=F32)
    d_norm_two = contract_cols(d_pre, w_up)
    cot_sum = jnp.sum(cot.astype(F32), axis=0)

    def by_owner(g):
        n = g.shape[1]
        return g.reshape(n_fs, n_ctx, dq // n_ctx, n).transpose(1, 0, 2, 3).reshape(n_fs * n_ctx, dq // n_ctx, n)

    def reduce_all(parts):
        got = lax.all_to_all(parts, ("ctx", "fsdp"), 0, 0)
        return jnp.sum(got.reshape((n_ctx, n_fs) + got.shape[1:]).astype(F32), axis=0)

    def reduce_ctx(parts):
        return jnp.sum(lax.all_to_all(parts, "ctx", 0, 0).astype(F32), axis=0)

    def give_back(share):
        return lax.all_to_all(jnp.broadcast_to(share[None], (n_ctx,) + share.shape), "ctx", 0, 0)

    fc1_share = reduce_all(by_owner(fc1_grad))
    fc2_share = reduce_ctx(fc2_grad.reshape(n_ctx, ff // n_ctx, d))
    mlp_share = jnp.concatenate([fc1_share.reshape(-1, ff), fc2_share], 0).astype(BF)
    mlp_all = give_back(mlp_share)
    rows = dq // n_ctx
    fc1_out = (
        mlp_all[:, : n_fs * rows].reshape(n_ctx, n_fs, rows, ff).transpose(0, 2, 1, 3).reshape(dq, n_fs * ff).astype(F32)
    )
    fc2_out = mlp_all[:, n_fs * rows :].reshape(ff, d).astype(F32)

    dkv = jnp.sum(home[:, :, :, :t].astype(F32), axis=2)
    oq = home[:, :, :, t:].reshape(n_fs, heads, t, 2 * HD)

    def from_heads(v):
        return v.transpose(0, 2, 1, 3).reshape(tok, heads * HD)

    head_out = from_heads(oq[..., HD:])
    d_queries = from_heads(oq[..., :HD]).astype(F32)
    d_keys = from_heads(dkv[..., :HD])
    d_values = from_heads(dkv[..., HD:])
    d_projected = jnp.concatenate(
        [rotate_back(d_queries, cos_row, sin_up, sin_down, half) * score_scale,
         rotate_back(d_keys, cos_row, sin_up, sin_down, half), d_values], 1
    ).astype(BF)
    qkv_grad = contract_rows(attn_in, d_projected).astype(BF)
    qkv_bias_grad = jnp.sum(d_projected, axis=0, dtype=F32)
    out_weight_grad = contract_rows(head_out, cot).astype(BF)
    d_norm_one = contract_cols(d_projected, w_qkv)

    def scatter_fsdp(parts):
        parts = parts.reshape(2, 2, t, d)
        here = parts[0] + swap_core(parts[1].astype(BF)).astype(F32)
        return here[0] + swap_xh(here[1].astype(BF)).astype(F32)

    x_float = x_own.astype(F32)
    block = scatter_fsdp(mlp_part + mm(head_out, out_weight))
    block_out = turned((x_float + block + b_out + b_down).astype(BF))

    u = scatter_fsdp(d_norm_one * gain_one + d_norm_two * gain_two)
    xhat_own, rstd_own = xhat[:t], rstd[:t]
    dx = rstd_own * (
        u - jnp.mean(u, axis=-1, keepdims=True) - xhat_own * jnp.mean(u * xhat_own, axis=-1, keepdims=True)
    )
    input_grad = turned((cot_own.astype(F32) + dx).astype(BF))

    def split_owner(v):
        return v.reshape(n_fs, n_ctx, rows).transpose(1, 0, 2)

    def split_ctx(v):
        return jnp.broadcast_to(v.reshape(n_ctx, 1, -1), (n_ctx, n_fs, v.shape[0] // n_ctx))

    smalls = jnp.concatenate(
        [
            split_owner(jnp.sum(d_norm_one * xhat, 0)),
            split_owner(jnp.sum(d_norm_one, 0)),
            split_owner(jnp.sum(d_norm_two * xhat, 0)),
            split_owner(jnp.sum(d_norm_two, 0)),
            split_owner(cot_sum),
            split_ctx(qkv_bias_grad),
            split_ctx(fc1_bias_grad),
        ],
        -1,
    )
    used = smalls.shape[-1]
    smalls = jnp.pad(
        smalls.reshape(n_ctx * n_fs, 1, used), ((0, 0), (0, rows - 1), (0, 128 - used))
    ).astype(BF)
    qkv_share = reduce_all(jnp.concatenate([by_owner(qkv_grad), smalls], 2))
    out_share = reduce_ctx(out_weight_grad.reshape(n_ctx, rows, d))
    out_share = out_share.reshape(rows, n_fs, dq).transpose(1, 0, 2)
    attn_share = jnp.concatenate([qkv_share, out_share], 2).astype(BF)
    attn_all = give_back(attn_share)
    qkv_out = (
        attn_all[..., : 3 * dq].reshape(n_ctx, n_fs, rows, 3, dq).transpose(0, 2, 3, 1, 4).reshape(dq, 3 * d).astype(F32)
    )
    out_out = attn_all[..., 3 * dq + 128 :].transpose(0, 2, 1, 3).reshape(dq, d).astype(F32)
    short_all = attn_all[:, :, 0, 3 * dq : 3 * dq + 128].astype(F32)

    def whole(v):
        return v.reshape(-1)

    summed = jnp.sum(short_all[..., : 4 * rows], axis=1)
    gains = [whole(summed[:, i * rows : (i + 1) * rows]) for i in range(4)]
    mine = lax.dynamic_index_in_dim(short_all, me, 1, keepdims=False)
    bias_common = whole(mine[:, 4 * rows : 5 * rows])
    at = 5 * rows
    n_qb = 3 * dq // n_ctx
    qb = short_all[..., at : at + n_qb].transpose(1, 0, 2).reshape(n_fs, 3, dq).transpose(1, 0, 2).reshape(3 * d)
    qkv_bias_out = lax.dynamic_slice(qb, (me * 3 * dq,), (3 * dq,))
    fc1_bias_out = whole(mine[:, at + n_qb : at + n_qb + ff // n_ctx])

    return (
        block_out[None],
        input_grad[None],
        gains[0],
        gains[1],
        qkv_out,
        qkv_bias_out,
        out_out,
        bias_common,
        gains[2],
        gains[3],
        fc1_out,
        fc1_bias_out,
        fc2_out,
        bias_common,
    )


def rotate_back(v, cos_row, sin_up, sin_down, half):
    ahead = jnp.concatenate([v[:, half:], v[:, :half]], 1)
    behind = jnp.concatenate([v[:, -half:], v[:, :-half]], 1)
    return v * cos_row - (ahead * sin_up + behind * sin_down)


def solution(mesh):
    token = P("fsdp", "ctx", None)
    placed = (
        token,
        P("fsdp", "ctx"),
        token,
        P("fsdp"),
        P("fsdp"),
        P("fsdp", None),
        P("fsdp"),
        P("fsdp", None),
        P("fsdp"),
        P("fsdp"),
        P("fsdp"),
        P("fsdp", None),
        P("fsdp"),
        P("fsdp", None),
        P("fsdp"),
    )
    return jax.shard_map(
        on_device,
        mesh=mesh,
        in_specs=placed,
        out_specs=(
            token,
            token,
            P("fsdp"),
            P("fsdp"),
            P("fsdp", None),
            P("fsdp"),
            P("fsdp", None),
            P("fsdp"),
            P("fsdp"),
            P("fsdp"),
            P("fsdp", None),
            P("fsdp"),
            P("fsdp", None),
            P("fsdp"),
        ),
        check_vma=False,
    )
```

```python
import jax
import jax.numpy as jnp
from jax import lax
from jax.experimental import pallas as pl
from jax.experimental.pallas import tpu as pltpu
from jax.sharding import PartitionSpec as P

H = 16
HD = 64
ROT = 16
RUN = 64
RUNS = 64
NORM_EPS = 1e-05
BF = jnp.bfloat16
F32 = jnp.float32
NEG = -1e30

QT = 256
KT = 512


def mm(a, b):
    return jnp.dot(a, b, preferred_element_type=F32)


def contract_rows(a, b):
    return lax.dot_general(a, b, (((0,), (0,)), ((), ())), preferred_element_type=F32)


def contract_cols(a, b):
    return lax.dot_general(a, b, (((1,), (1,)), ((), ())), preferred_element_type=F32)


def swap_xh(v):
    return lax.ppermute(v, "fsdp", [(i, i ^ 2) for i in range(4)])


def swap_core(v):
    return lax.ppermute(v, "fsdp", [(i, i ^ 1) for i in range(4)])


def attention_kernel(scal, recv, out, kv, qx, yx, dkv, oq, sbuf, dbuf):
    folded = scal[0]
    odd = scal[1]
    lane = lax.broadcasted_iota(jnp.int32, (RUN, 2 * HD), 1)
    low_half = lane < HD
    n_src = recv.shape[0]
    tiles = qx.shape[0]
    per_tile = QT // RUN

    def runs(c):
        turned = jnp.logical_and(folded == 1, c % 2 == 1)
        even = jnp.where(folded == 1, jnp.where(turned, 2 * n_src - 1 - c, c), 2 * c)
        other = jnp.where(folded == 1, jnp.where(turned, c, 2 * n_src - 1 - c), 2 * c + 1)
        return even, other

    def sort_in(c, carry):
        even, other = runs(c)
        kv[pl.ds(pl.multiple_of(even * RUN, RUN), RUN), :] = recv[c, 0:RUN, :]
        kv[pl.ds(pl.multiple_of(other * RUN, RUN), RUN), :] = recv[c, RUN : 2 * RUN, :]
        rank = jnp.where(odd == 1, other, even) // 2
        tile = rank // per_tile
        place = pl.multiple_of((rank % per_tile) * RUN, RUN)
        qd = recv[c, 2 * RUN : 3 * RUN, :]
        zero = jnp.zeros_like(qd)
        q_only = jnp.where(low_half, qd, zero)
        d_only = jnp.where(low_half, zero, qd)
        qx[tile, pl.ds(place, RUN), :] = q_only
        qx[tile, pl.ds(QT + place, RUN), :] = d_only
        yx[tile, pl.ds(place, RUN), :] = d_only
        yx[tile, pl.ds(QT + place, RUN), :] = q_only
        return carry

    lax.fori_loop(0, n_src, sort_in, 0)
    dkv[...] = jnp.zeros_like(dkv)

    row = lax.broadcasted_iota(jnp.int32, (QT, KT), 0)
    col = lax.broadcasted_iota(jnp.int32, (QT, KT), 1)
    row_place = (2 * (row // RUN) + odd) * RUN + row % RUN
    allowed = col <= row_place

    def fold(v, op):
        parts = [v[:, i * 128 : (i + 1) * 128] for i in range(KT // 128)]
        total = parts[0]
        for part in parts[1:]:
            total = op(total, part)
        return total

    def tile_step(j, carry):
        x = qx[j]
        y = yx[j]

        def products(k):
            keys = kv[pl.ds(pl.multiple_of(k * KT, KT), KT), :]
            both = contract_cols(x, keys)
            return both[:QT], both[QT:]

        def pass_one(k, top):
            s, d = products(k)
            sbuf[k] = s
            dbuf[k] = d
            return jnp.maximum(top, fold(s, jnp.maximum))

        top = lax.fori_loop(0, j, pass_one, jnp.full((QT, 128), NEG, F32))
        s, d = products(j)
        s = jnp.where(allowed, s, NEG)
        sbuf[j] = s
        dbuf[j] = d
        top = jnp.maximum(top, fold(s, jnp.maximum))
        top = jnp.max(top, axis=1, keepdims=True)

        def pass_two(k, sums):
            total, weighted = sums
            e = jnp.exp(sbuf[k] - top)
            sbuf[k] = e
            return total + fold(e, jnp.add), weighted + fold(e * dbuf[k], jnp.add)

        zero = jnp.zeros((QT, 128), F32)
        total, weighted = lax.fori_loop(0, j + 1, pass_two, (zero, zero))
        scale = 1.0 / jnp.sum(total, axis=1, keepdims=True)
        delta = jnp.sum(weighted, axis=1, keepdims=True) * scale

        def pass_three(k, acc):
            rows = pl.ds(pl.multiple_of(k * KT, KT), KT)
            p = sbuf[k] * scale
            ds = p * (dbuf[k] - delta)
            a = jnp.concatenate([p.astype(BF), ds.astype(BF)], axis=0)
            dkv[rows, :] += contract_rows(a, y)
            return acc + mm(a, kv[rows, :])

        acc = lax.fori_loop(0, j + 1, pass_three, jnp.zeros((2 * QT, 2 * HD), F32))
        wide = lax.broadcasted_iota(jnp.int32, (QT, 2 * HD), 1) < HD
        oq[pl.ds(pl.multiple_of(j * QT, QT), QT), :] = jnp.where(wide, acc[QT:], acc[:QT]).astype(BF)
        return carry

    lax.fori_loop(0, tiles, tile_step, 0)

    def sort_out(c, carry):
        even, other = runs(c)
        out[c, 0:RUN, :] = dkv[pl.ds(pl.multiple_of(even * RUN, RUN), RUN), :].astype(BF)
        out[c, RUN : 2 * RUN, :] = dkv[pl.ds(pl.multiple_of(other * RUN, RUN), RUN), :].astype(BF)
        rank = jnp.where(odd == 1, other, even) // 2
        out[c, 2 * RUN : 3 * RUN, :] = oq[pl.ds(pl.multiple_of(rank * RUN, RUN), RUN), :]
        return carry

    lax.fori_loop(0, n_src, sort_out, 0)


def attention(scal, recv):
    n_src = recv.shape[0]
    keys = n_src * 2 * RUN
    queries = n_src * RUN
    tiles = queries // QT
    return pl.pallas_call(
        attention_kernel,
        out_shape=jax.ShapeDtypeStruct(recv.shape, BF),
        in_specs=[pl.BlockSpec(memory_space=pltpu.SMEM), pl.BlockSpec(memory_space=pltpu.VMEM)],
        out_specs=pl.BlockSpec(memory_space=pltpu.VMEM),
        scratch_shapes=[
            pltpu.VMEM((keys, 2 * HD), BF),
            pltpu.VMEM((tiles, 2 * QT, 2 * HD), BF),
            pltpu.VMEM((tiles, 2 * QT, 2 * HD), BF),
            pltpu.VMEM((keys, 2 * HD), F32),
            pltpu.VMEM((queries, 2 * HD), BF),
            pltpu.VMEM((keys // KT, QT, KT), F32),
            pltpu.VMEM((keys // KT, QT, KT), F32),
        ],
        compiler_params=pltpu.CompilerParams(vmem_limit_bytes=40 * 1024 * 1024),
        cost_estimate=pl.CostEstimate(
            flops=14 * HD * queries * keys // 2,
            bytes_accessed=4 * recv.size,
            transcendentals=queries * keys // 2,
        ),
        name="attention",
    )(scal, recv)


def full_spec(v):
    zeros = (0,) * len(v.shape)
    return pl.BlockSpec(v.shape, lambda i: zeros)


def whole_call(body, out_shape, n_smem, args, name, flops=0):
    smem = [pl.BlockSpec(memory_space=pltpu.SMEM)] * n_smem
    return pl.pallas_call(
        body,
        grid=(1,),
        out_shape=out_shape,
        in_specs=smem + [full_spec(v) for v in args[n_smem:]],
        out_specs=jax.tree.map(full_spec, out_shape),
        compiler_params=pltpu.CompilerParams(vmem_limit_bytes=56 * 1024 * 1024),
        cost_estimate=pl.CostEstimate(
            flops=flops,
            bytes_accessed=sum(v.size * v.dtype.itemsize for v in args)
            + sum(v.size * v.dtype.itemsize for v in jax.tree.leaves(out_shape)),
            transcendentals=0,
        ),
        name=name,
    )(*args)


def shaped(shape, dtype):
    return jax.ShapeDtypeStruct(shape, dtype)


def message_kernel(places, x, g, l1g, l1b, l2g, l2b, ob, f2b, qb, x_out, g_out):
    run = places[0] // RUN
    flip = run % 2 == 1
    t, d = x.shape

    @pl.when(flip)
    def _():
        for src, dst in ((x, x_out), (g, g_out)):
            dst[0:RUN, :] = src[RUN:t, :]
            dst[RUN:t, :] = src[0:RUN, :]

    @pl.when(jnp.logical_not(flip))
    def _():
        x_out[0:t, :] = x[...]
        g_out[...] = g[...]

    n = l1g.shape[0]
    both = run + places[RUN] // RUN
    row = lax.broadcasted_iota(jnp.int32, (16, n), 0)
    short = jnp.where(jnp.logical_and(row == 9, both == RUNS - 1), 1.0, 0.0)
    lines = [ref[...].astype(F32).reshape(1, n) for ref in (l1g, l1b, l2g, l2b, ob, f2b)]
    bias = qb[...].astype(F32).reshape(1, 3 * n)
    lines += [bias[:, i * n : (i + 1) * n] for i in range(3)]
    for i, line in enumerate(lines):
        short = jnp.where(row == i, line, short)
    x_out[t:, 0:n] = short.astype(BF)
    x_out[t:, n:] = jnp.zeros((16, d - n), BF)


def columns_kernel(w, out):
    n_fs, _, width = out.shape
    part = width // 3
    for g in range(n_fs):
        for k in range(3):
            out[g, :, k * part : (k + 1) * part] = w[:, (k * n_fs + g) * part : (k * n_fs + g + 1) * part]


def project_kernel(me, x0, x1, x2, x3, g0, g1, g2, g3, w, wo, tables, send, attn_in, mlp_in, xhat, cot, short_out):
    t = g0.shape[0]
    d = g0.shape[1]
    dq = w.shape[1] // 3
    n_fs = d // dq
    blocks = (x0, x1, x2, x3)
    cots = (g0, g1, g2, g3)
    f = me[0]
    shorts = [ref[t : t + 16, :].astype(F32) for ref in blocks]
    owners = [f, f ^ 2, f ^ 1, f ^ 3]
    by_owner = []
    for o in range(n_fs):
        total = shorts[0]
        for r in range(1, n_fs):
            total = jnp.where(owners[r] == o, shorts[r], total)
        by_owner.append(total[:, :dq])
    short = jnp.concatenate(by_owner, axis=1)
    short_out[...] = short
    gain_one, shift_one, gain_two, shift_two = (short[i : i + 1] for i in range(4))
    biases = []
    for kind in range(3):
        total = jnp.zeros((1, dq), F32)
        for b in range(3 * n_fs):
            o, i = divmod(b, 3)
            total = jnp.where(kind * n_fs + f == b, by_owner[o][6 + i : 7 + i], total)
        biases.append(total)

    for r in range(n_fs):
        rows = slice(r * t, (r + 1) * t)
        v = blocks[r][0:t, :].astype(F32)
        centred = v - jnp.mean(v, axis=1, keepdims=True)
        variance = jnp.mean(centred * centred, axis=1, keepdims=True)
        hat = centred * lax.rsqrt(variance + NORM_EPS)
        xhat[rows, :] = hat
        attn_in[rows, :] = (hat * gain_one + shift_one).astype(BF)
        mlp_in[rows, :] = (hat * gain_two + shift_two).astype(BF)
        cot[rows, :] = cots[r][...]

    a = attn_in[...]
    q_all = mm(a, w[:, :dq]) + biases[0]
    k_all = mm(a, w[:, dq : 2 * dq]) + biases[1]
    v_all = mm(a, w[:, 2 * dq :]) + biases[2]
    dh_all = contract_cols(cot[...], wo[...])
    low = lax.broadcasted_iota(jnp.int32, (t, 2 * HD), 1) < HD
    for r in range(n_fs):
        rows = slice(r * t, (r + 1) * t)
        is_folded = shorts[r][9:10, 0:1] > 0.5
        cos, up, down = (jnp.where(is_folded, tables[3 + i], tables[i]) for i in range(3))

        def turn(v):
            return v * cos + pltpu.roll(v, 2 * HD - ROT // 2, 1) * up + pltpu.roll(v, ROT // 2, 1) * down

        for b in range(dq // (2 * HD)):
            cols = slice(b * 2 * HD, (b + 1) * 2 * HD)
            q = turn(q_all[rows, cols]) * (HD ** (-0.5))
            k = turn(k_all[rows, cols])
            v = v_all[rows, cols]
            dh = dh_all[rows, cols]
            for side in range(2):
                if side == 0:
                    kv = jnp.where(low, k, pltpu.roll(v, HD, 1)).astype(BF)
                    qd = jnp.where(low, q, pltpu.roll(dh, HD, 1)).astype(BF)
                else:
                    kv = jnp.where(low, pltpu.roll(k, HD, 1), v).astype(BF)
                    qd = jnp.where(low, pltpu.roll(q, HD, 1), dh).astype(BF)
                at = r * 8 + (2 * b + side) * 2
                for half in range(2):
                    send[at + half, 0:t, :] = kv
                    send[at + half, t : t + RUN, :] = qd[half * RUN : (half + 1) * RUN]


def finish_kernel(folded, home, tables, attn_in, cot, w, xhat, early, payload, d_norm, head_out, d_proj):
    t = home.shape[1] - RUN
    dq = head_out.shape[1]
    n_fs = home.shape[0] // 8
    low = lax.broadcasted_iota(jnp.int32, (t, 2 * HD), 1) < HD
    for r in range(n_fs):
        rows = slice(r * t, (r + 1) * t)
        is_folded = folded[r] == 1
        cos, up, down = (jnp.where(is_folded, tables[3 + i], tables[i]) for i in range(3))

        def turn_back(v):
            return v * cos - (pltpu.roll(v, 2 * HD - ROT // 2, 1) * up + pltpu.roll(v, ROT // 2, 1) * down)

        for b in range(dq // (2 * HD)):
            cols = slice(b * 2 * HD, (b + 1) * 2 * HD)
            dkv, qo = [], []
            for side in range(2):
                at = r * 8 + (2 * b + side) * 2
                dkv.append(home[at, 0:t, :].astype(F32) + home[at + 1, 0:t, :].astype(F32))
                qo.append(jnp.concatenate([home[at, t : t + RUN, :], home[at + 1, t : t + RUN, :]], 0).astype(F32))
            d_q = jnp.where(low, qo[0], pltpu.roll(qo[1], HD, 1))
            o = jnp.where(low, pltpu.roll(qo[0], HD, 1), qo[1])
            d_k = jnp.where(low, dkv[0], pltpu.roll(dkv[1], HD, 1))
            d_v = jnp.where(low, pltpu.roll(dkv[0], HD, 1), dkv[1])
            head_out[rows, cols] = o.astype(BF)
            d_proj[rows, cols] = (turn_back(d_q) * (HD ** (-0.5))).astype(BF)
            d_proj[rows, dq + b * 2 * HD : dq + (b + 1) * 2 * HD] = turn_back(d_k).astype(BF)
            d_proj[rows, 2 * dq + b * 2 * HD : 2 * dq + (b + 1) * 2 * HD] = d_v.astype(BF)

    n_ctx, _, rows, _ = payload.shape
    d = attn_in.shape[1]
    width = d_proj.shape[1]
    dp = d_proj[...]
    c = contract_cols(dp, w[...])
    d_norm[...] = c
    gain = jnp.sum(c * xhat[...], axis=0, keepdims=True)
    shift = jnp.sum(c, axis=0, keepdims=True)
    bias = jnp.sum(dp.astype(F32), axis=0, keepdims=True)
    last = width + 128
    payload[:, :, :, width:last] = jnp.zeros((n_ctx, n_fs, rows, 128), BF)
    first = lax.broadcasted_iota(jnp.int32, (rows, 128), 0) == 0

    def put(b, f, v):
        payload[b, f, :, width:last] = jnp.where(first, v, 0.0).astype(BF)

    for f in range(n_fs):
        grad = contract_rows(attn_in[:, f * dq : (f + 1) * dq], dp)
        payload[:, f, :, 0:width] = grad.reshape(n_ctx, rows, width).astype(BF)
        grad = contract_rows(head_out[...], cot[:, f * dq : (f + 1) * dq])
        payload[:, f, :, last:] = grad.reshape(n_ctx, rows, dq).astype(BF)
        mine = [gain, shift, early[0:1, :], early[1:2, :], early[2:3, :]]
        for i, v in enumerate(mine):
            for half in range(2):
                at = f * dq + half * 128
                put(2 * i + half, f, v[:, at : at + 128])
        for i in range(6):
            put(10 + i, f, bias[:, i * 128 : (i + 1) * 128])
        for i in range(8):
            put(16 + i, f, early[3:4, i * 128 : (i + 1) * 128])


def expand_attn_kernel(share, qkv, out):
    n_ctx = share.shape[0]
    dq = out.shape[0]
    rows = dq // n_ctx

    def step(c, carry):
        at = pl.ds(pl.multiple_of(c * rows, rows), rows)
        for f in range(4):
            v = share[c, f].astype(F32)
            for kind in range(3):
                qkv[at, (kind * 4 + f) * dq : (kind * 4 + f + 1) * dq] = v[:, kind * dq : (kind + 1) * dq]
            out[at, f * dq : (f + 1) * dq] = v[:, 3 * dq + 128 :]
        return carry

    lax.fori_loop(0, n_ctx, step, 0)


def expand_mlp_kernel(place_a, place_b, order, up, down, up_out, down_out):
    n_ctx = up.shape[0]
    ff = down_out.shape[1]
    rows = up_out.shape[0] // n_ctx

    def step(c, carry):
        v = up[place_a[c]].astype(F32)
        at = pl.ds(pl.multiple_of(c * rows, rows), rows)
        for f in range(4):
            up_out[at, f * ff : (f + 1) * ff] = v[f * rows : (f + 1) * rows]
        down_out[pl.ds(pl.multiple_of(c * 4 * rows, 4 * rows), 4 * rows), :] = down[place_b[c]].astype(F32)
        return carry

    lax.fori_loop(0, n_ctx, step, 0)


def pick(stacked, index):
    return lax.dynamic_index_in_dim(stacked, index, 0, keepdims=False)


def on_device(
    hidden_in,
    positions,
    out_grad,
    ln1_gain,
    ln1_bias,
    qkv_weight,
    qkv_bias,
    out_weight,
    out_bias,
    ln2_gain,
    ln2_bias,
    fc1_weight,
    fc1_bias,
    fc2_weight,
    fc2_bias,
):
    n_fs = 4
    n_ctx = 32
    ctx = lax.axis_index("ctx")
    me = lax.axis_index("fsdp")
    t = hidden_in.shape[1]
    d = hidden_in.shape[2]
    dq = d // n_fs
    ff = fc1_weight.shape[1] // n_fs
    tok = n_fs * t
    rows = dq // n_ctx
    me_one = me.astype(jnp.int32).reshape(1)

    flip = (positions[0, 0] // RUN) % 2 == 1

    def turned(v):
        return jnp.where(flip, jnp.concatenate([v[RUN:], v[:RUN]], 0), v)

    x_msg, cot_msg = whole_call(
        message_kernel,
        (shaped((t + 16, d), BF), shaped((t, d), BF)),
        1,
        (positions[0], hidden_in[0], out_grad[0], ln1_gain, ln1_bias, ln2_gain, ln2_bias, out_bias, fc2_bias, qkv_bias),
        "message",
    )
    x_xh = swap_xh(x_msg)
    cot_xh = swap_xh(cot_msg)
    x_all = [x_msg, x_xh, swap_core(x_msg), swap_core(x_xh)]
    cot_all = [cot_msg, cot_xh, swap_core(cot_msg), swap_core(cot_xh)]

    (qkv_columns,) = whole_call(columns_kernel, (shaped((n_fs, dq, 3 * dq), BF),), 0, (qkv_weight,), "columns")
    w_qkv = lax.all_to_all(qkv_columns, "fsdp", 0, 0).reshape(d, 3 * dq)
    w_qkv, up_own = lax.optimization_barrier((w_qkv, fc1_weight))

    def cross(v):
        return lax.ppermute(v, ("ctx", "fsdp"), [(i, i ^ (16 * n_fs + 2)) for i in range(n_ctx * n_fs)])

    def up_columns(diff):
        return lax.dynamic_slice(up_own, (0, (me ^ diff) * ff), (dq, ff))

    across = [cross(up_columns(2)), cross(up_columns(3))]
    up_rel = [up_columns(0), across[0], swap_core(up_columns(1)), swap_core(across[1])]
    up_rel = jnp.stack(up_rel)

    def rel_of(owner):
        diff = jnp.bitwise_xor(me, owner)
        return (diff % 2) * 2 + diff // 2

    w_up = jnp.concatenate([pick(up_rel, rel_of(o)) for o in range(n_fs)], 0)

    half = ROT // 2
    lane = jnp.arange(2 * HD) % HD
    turning = lane < ROT
    frequency = jnp.where(turning, 10000.0 ** (-2.0 * (lane % half).astype(F32) / ROT), 0.0)
    back = ctx % 2 == 1
    tables = []
    for even_run, odd_run in (
        (2 * ctx, 2 * ctx + 1),
        (jnp.where(back, 2 * n_ctx - 1 - ctx, ctx), jnp.where(back, ctx, 2 * n_ctx - 1 - ctx)),
    ):
        places = jnp.concatenate([even_run * RUN + jnp.arange(RUN), odd_run * RUN + jnp.arange(RUN)])
        phases = places.astype(F32)[:, None] * frequency[None, :]
        sines = jnp.sin(phases)
        tables += [jnp.cos(phases), jnp.where(lane < half, -sines, 0.0), jnp.where((lane >= half) & turning, sines, 0.0)]
    tables = jnp.stack(tables)

    send, attn_in, mlp_in, xhat, cot, short_all = whole_call(
        project_kernel,
        (
            shaped((n_ctx, t + RUN, 2 * HD), BF),
            shaped((tok, d), BF),
            shaped((tok, d), BF),
            shaped((tok, d), F32),
            shaped((tok, d), BF),
            shaped((16, d), F32),
        ),
        1,
        (me_one, *x_all, *cot_all, w_qkv, out_weight, tables),
        "project",
        flops=2 * tok * d * 4 * dq,
    )
    gain_one, gain_two = short_all[0:1], short_all[2:3]
    both_bias = short_all[4:5] + short_all[5:6]
    folded = jnp.stack([v[t + 9, 0] for v in x_all]) > 0.5
    folded = folded.astype(jnp.int32)

    recv = lax.all_to_all(send, "ctx", 0, 0)

    pre_act = mm(mlp_in, w_up) + fc1_bias.astype(F32)[None]
    act_float, pull_act = jax.vjp(lambda v: jax.nn.gelu(v, approximate=False), pre_act)
    activated = act_float.astype(BF)
    d_pre = pull_act(contract_cols(cot, fc2_weight))[0].astype(BF)
    fc2_grad = contract_rows(activated, cot).astype(BF)
    fc1_grad = contract_rows(mlp_in, d_pre).astype(BF)
    xl, z, y = ctx // 16, (ctx // 4) % 4, ctx % 4
    spot = {"xl": xl, "z": z, "y": y}

    def shift(v, axis, by):
        size, stride = {"y": (4, 1), "z": (4, 4), "xl": (2, 16)}[axis]
        perm = []
        for i in range(n_ctx):
            p = (i // stride) % size
            perm.append((i, i + ((p + by) % size - p) * stride))
        return lax.ppermute(v, "ctx", perm)

    def blocks_of(v, axis, dim):
        size = v.shape[dim]
        return [
            lax.dynamic_index_in_dim(v, (spot[axis] + s) % size, dim, keepdims=False) for s in range(size)
        ]

    def exchange(parts, axis):
        return [parts[0]] + [shift(p, axis, s + 1) for s, p in enumerate(parts[1:])]

    def add_up(parts):
        total = parts[0].astype(F32)
        for p in parts[1:]:
            total = total + p.astype(F32)
        return total.astype(BF)

    up_parts = blocks_of(fc1_grad.reshape(n_fs, 2, 4, 4, rows, ff), "y", 3)
    down_parts = blocks_of(fc2_grad.reshape(2, 4, 4, ff // n_ctx, d), "z", 1)
    recv, up_parts, down_parts = lax.optimization_barrier((recv, up_parts, down_parts))
    up_parts = exchange(up_parts, "y")
    down_parts = exchange(down_parts, "z")

    my_folded = pick(folded, ctx // 8)
    grads = attention(jnp.stack([my_folded, ctx % 2]).astype(jnp.int32), recv)
    home = lax.all_to_all(grads, "ctx", 0, 0)

    up_sum = add_up(exchange(blocks_of(add_up(up_parts), "z", 2), "z"))
    down_sum = add_up(exchange(blocks_of(add_up(down_parts), "y", 1), "y"))
    up_sum = add_up(exchange(blocks_of(up_sum, "xl", 1), "xl"))
    down_share = add_up(exchange(blocks_of(down_sum, "xl", 0), "xl"))

    def to_owner(pieces):
        for_core = jnp.stack([pick(pieces, me ^ 1), pick(pieces, me ^ 3)])
        from_core = swap_core(for_core)
        from_xh = swap_xh(jnp.stack([pick(pieces, me ^ 2), from_core[1]]))
        rel = jnp.stack([pick(pieces, me), from_xh[0], from_core[0], from_xh[1]])
        return jnp.stack([pick(rel, rel_of(o)) for o in range(n_fs)])

    up_share = to_owner(up_sum).reshape(n_fs * rows, ff)

    mlp_part = mm(activated, fc2_weight)
    d_norm_two = contract_cols(d_pre, w_up)
    early = jnp.stack(
        [
            jnp.sum(d_norm_two * xhat, 0),
            jnp.sum(d_norm_two, 0),
            jnp.sum(cot.astype(F32), 0),
            jnp.sum(d_pre, 0, dtype=F32),
        ]
    )
    def spread(v, axes):
        v = v[None]
        for axis, size in axes:
            v = jnp.concatenate([v] + [shift(v, axis, s) for s in range(1, size)], 0)
        return v

    owner = jnp.arange(n_ctx)
    dxl, dz, dy = xl ^ (owner // 16), (z - (owner // 4) % 4) % 4, (y - owner % 4) % 4
    up_spread = spread(up_share, (("xl", 2), ("y", 4), ("z", 4)))
    down_spread = spread(down_share, (("xl", 2), ("z", 4), ("y", 4)))
    place_a = (dz * 8 + dy * 2 + dxl).astype(jnp.int32)
    place_b = (dy * 8 + dz * 2 + dxl).astype(jnp.int32)
    fc1_out, fc2_out = whole_call(
        expand_mlp_kernel,
        (shaped((dq, n_fs * ff), F32), shaped((ff, d), F32)),
        3,
        (place_a, place_b, me_one, up_spread, down_spread),
        "expand_mlp",
    )

    payload, d_norm_one, head_out, _ = whole_call(
        finish_kernel,
        (
            shaped((n_ctx, n_fs, rows, 4 * dq + 128), BF),
            shaped((tok, d), F32),
            shaped((tok, dq), BF),
            shaped((tok, 3 * dq), BF),
        ),
        1,
        (folded, home, tables, attn_in, cot, w_qkv, xhat, early),
        "finish",
        flops=2 * tok * d * 7 * dq,
    )
    got = lax.all_to_all(payload, "ctx", 0, 0)
    share = jnp.sum(got.astype(F32), 0).astype(BF)
    qkv_share = to_owner(share[..., : 3 * dq + 128])
    attn_share = jnp.concatenate([qkv_share, share[..., 3 * dq + 128 :]], 2)
    attn_all = lax.all_to_all(
        jnp.broadcast_to(attn_share[None], (n_ctx,) + attn_share.shape), "ctx", 0, 0
    )
    qkv_out, out_out = whole_call(
        expand_attn_kernel,
        (shaped((dq, 3 * d), F32), shaped((dq, d), F32)),
        0,
        (attn_all,),
        "expand_attn",
    )
    lines = attn_all[:, :, 0, 3 * dq : 3 * dq + 128].astype(F32)
    vectors = jnp.sum(lines[:8], 1).reshape(4, dq)
    mine = lax.dynamic_index_in_dim(lines, me, 1, keepdims=False)
    bias_common = mine[8:10].reshape(dq)
    qkv_bias_all = lines[10:16].reshape(3, 2, n_fs, 128).transpose(0, 2, 1, 3).reshape(3 * d)
    qkv_bias_out = lax.dynamic_slice(qkv_bias_all, (me * 3 * dq,), (3 * dq,))
    fc1_bias_out = mine[16:24].reshape(ff)

    def scatter_fsdp(parts):
        parts = parts.reshape(2, 2, t, d)
        here = parts[0] + swap_core(parts[1].astype(BF)).astype(F32)
        return here[0] + swap_xh(here[1].astype(BF)).astype(F32)

    block = scatter_fsdp(mlp_part + mm(head_out, out_weight))
    block_out = turned((x_msg[:t].astype(F32) + block + both_bias).astype(BF))

    u = scatter_fsdp(d_norm_one * gain_one + d_norm_two * gain_two)
    x_float = x_msg[:t].astype(F32)
    centred = x_float - jnp.mean(x_float, axis=-1, keepdims=True)
    rstd_own = lax.rsqrt(jnp.mean(centred * centred, axis=-1, keepdims=True) + NORM_EPS)
    xhat_own = centred * rstd_own
    dx = rstd_own * (
        u - jnp.mean(u, axis=-1, keepdims=True) - xhat_own * jnp.mean(u * xhat_own, axis=-1, keepdims=True)
    )
    input_grad = turned((cot_msg.astype(F32) + dx).astype(BF))

    return (
        block_out[None],
        input_grad[None],
        vectors[0],
        vectors[1],
        qkv_out,
        qkv_bias_out,
        out_out,
        bias_common,
        vectors[2],
        vectors[3],
        fc1_out,
        fc1_bias_out,
        fc2_out,
        bias_common,
    )


def solution(mesh):
    token = P("fsdp", "ctx", None)
    placed = (
        token,
        P("fsdp", "ctx"),
        token,
        P("fsdp"),
        P("fsdp"),
        P("fsdp", None),
        P("fsdp"),
        P("fsdp", None),
        P("fsdp"),
        P("fsdp"),
        P("fsdp"),
        P("fsdp", None),
        P("fsdp"),
        P("fsdp", None),
        P("fsdp"),
    )
    return jax.shard_map(
        on_device,
        mesh=mesh,
        in_specs=placed,
        out_specs=(
            token,
            token,
            P("fsdp"),
            P("fsdp"),
            P("fsdp", None),
            P("fsdp"),
            P("fsdp", None),
            P("fsdp"),
            P("fsdp"),
            P("fsdp"),
            P("fsdp", None),
            P("fsdp"),
            P("fsdp", None),
            P("fsdp"),
        ),
        check_vma=False,
    )
```

```python
import jax
import jax.numpy as jnp
from jax import lax
from jax.experimental import pallas as pl
from jax.experimental.pallas import tpu as pltpu
from jax.sharding import PartitionSpec as P

H = 16
HD = 64
ROT = 16
RUN = 64
RUNS = 64
NORM_EPS = 1e-05
BF = jnp.bfloat16
F32 = jnp.float32
NEG = -1e30

QT = 512
KT = 1024


def mm(a, b):
    return jnp.dot(a, b, preferred_element_type=F32)


def contract_rows(a, b):
    return lax.dot_general(a, b, (((0,), (0,)), ((), ())), preferred_element_type=F32)


def contract_cols(a, b):
    return lax.dot_general(a, b, (((1,), (1,)), ((), ())), preferred_element_type=F32)


def swap_xh(v):
    return lax.ppermute(v, "fsdp", [(i, i ^ 2) for i in range(4)])


def swap_core(v):
    return lax.ppermute(v, "fsdp", [(i, i ^ 1) for i in range(4)])


def attention_kernel(scal, recv, out, kv, qx, yx, dkv, oq, sbuf, dbuf):
    folded = scal[0]
    odd = scal[1]
    lane = lax.broadcasted_iota(jnp.int32, (RUN, 2 * HD), 1)
    low_half = lane < HD
    n_src = recv.shape[0]
    tiles = qx.shape[0]
    per_tile = QT // RUN

    def runs(c):
        turned = jnp.logical_and(folded == 1, c % 2 == 1)
        even = jnp.where(folded == 1, jnp.where(turned, 2 * n_src - 1 - c, c), 2 * c)
        other = jnp.where(folded == 1, jnp.where(turned, c, 2 * n_src - 1 - c), 2 * c + 1)
        return even, other

    def sort_in(c, carry):
        even, other = runs(c)
        kv[pl.ds(pl.multiple_of(even * RUN, RUN), RUN), :] = recv[c, 0:RUN, :]
        kv[pl.ds(pl.multiple_of(other * RUN, RUN), RUN), :] = recv[c, RUN : 2 * RUN, :]
        rank = jnp.where(odd == 1, other, even) // 2
        tile = rank // per_tile
        place = pl.multiple_of((rank % per_tile) * RUN, RUN)
        qd = recv[c, 2 * RUN : 3 * RUN, :]
        zero = jnp.zeros_like(qd)
        q_only = jnp.where(low_half, qd, zero)
        d_only = jnp.where(low_half, zero, qd)
        qx[tile, pl.ds(place, RUN), :] = q_only
        qx[tile, pl.ds(QT + place, RUN), :] = d_only
        yx[tile, pl.ds(place, RUN), :] = d_only
        yx[tile, pl.ds(QT + place, RUN), :] = q_only
        return carry

    lax.fori_loop(0, n_src, sort_in, 0)
    dkv[...] = jnp.zeros_like(dkv)

    row = lax.broadcasted_iota(jnp.int32, (QT, KT), 0)
    col = lax.broadcasted_iota(jnp.int32, (QT, KT), 1)
    row_place = (2 * (row // RUN) + odd) * RUN + row % RUN
    allowed = col <= row_place

    def fold(v, op):
        parts = [v[:, i * 128 : (i + 1) * 128] for i in range(KT // 128)]
        total = parts[0]
        for part in parts[1:]:
            total = op(total, part)
        return total

    def tile_step(j, carry):
        x = qx[j]
        y = yx[j]

        def products(k):
            keys = kv[pl.ds(pl.multiple_of(k * KT, KT), KT), :]
            both = contract_cols(x, keys)
            return both[:QT], both[QT:]

        def pass_one(k, top):
            s, d = products(k)
            sbuf[k] = s
            dbuf[k] = d
            return jnp.maximum(top, fold(s, jnp.maximum))

        top = lax.fori_loop(0, j, pass_one, jnp.full((QT, 128), NEG, F32), unroll=2 if j else 1)
        s, d = products(j)
        s = jnp.where(allowed, s, NEG)
        sbuf[j] = s
        dbuf[j] = d
        top = jnp.maximum(top, fold(s, jnp.maximum))
        top = jnp.max(top, axis=1, keepdims=True)

        def pass_two(k, sums):
            total, weighted = sums
            e = jnp.exp(sbuf[k] - top)
            sbuf[k] = e
            return total + fold(e, jnp.add), weighted + fold(e * dbuf[k], jnp.add)

        zero = jnp.zeros((QT, 128), F32)
        total, weighted = lax.fori_loop(0, j + 1, pass_two, (zero, zero), unroll=2)
        scale = 1.0 / jnp.sum(total, axis=1, keepdims=True)
        delta = jnp.sum(weighted, axis=1, keepdims=True) * scale

        def pass_three(k, acc):
            rows = pl.ds(pl.multiple_of(k * KT, KT), KT)
            p = sbuf[k] * scale
            ds = p * (dbuf[k] - delta)
            a = jnp.concatenate([p.astype(BF), ds.astype(BF)], axis=0)
            dkv[rows, :] += contract_rows(a, y)
            return acc + mm(a, kv[rows, :])

        acc = lax.fori_loop(0, j + 1, pass_three, jnp.zeros((2 * QT, 2 * HD), F32), unroll=2)
        wide = lax.broadcasted_iota(jnp.int32, (QT, 2 * HD), 1) < HD
        oq[pl.ds(j * QT, QT), :] = jnp.where(wide, acc[QT:], acc[:QT]).astype(BF)
        return carry

    for j in range(tiles):
        tile_step(j, 0)

    def sort_out(c, carry):
        even, other = runs(c)
        out[c, 0:RUN, :] = dkv[pl.ds(pl.multiple_of(even * RUN, RUN), RUN), :].astype(BF)
        out[c, RUN : 2 * RUN, :] = dkv[pl.ds(pl.multiple_of(other * RUN, RUN), RUN), :].astype(BF)
        rank = jnp.where(odd == 1, other, even) // 2
        out[c, 2 * RUN : 3 * RUN, :] = oq[pl.ds(pl.multiple_of(rank * RUN, RUN), RUN), :]
        return carry

    lax.fori_loop(0, n_src, sort_out, 0)


def attention(scal, recv):
    n_src = recv.shape[0]
    keys = n_src * 2 * RUN
    queries = n_src * RUN
    tiles = queries // QT
    return pl.pallas_call(
        attention_kernel,
        out_shape=jax.ShapeDtypeStruct(recv.shape, BF),
        in_specs=[pl.BlockSpec(memory_space=pltpu.SMEM), pl.BlockSpec(memory_space=pltpu.VMEM)],
        out_specs=pl.BlockSpec(memory_space=pltpu.VMEM),
        scratch_shapes=[
            pltpu.VMEM((keys, 2 * HD), BF),
            pltpu.VMEM((tiles, 2 * QT, 2 * HD), BF),
            pltpu.VMEM((tiles, 2 * QT, 2 * HD), BF),
            pltpu.VMEM((keys, 2 * HD), F32),
            pltpu.VMEM((queries, 2 * HD), BF),
            pltpu.VMEM((keys // KT, QT, KT), F32),
            pltpu.VMEM((keys // KT, QT, KT), F32),
        ],
        compiler_params=pltpu.CompilerParams(vmem_limit_bytes=60 * 1024 * 1024),
        cost_estimate=pl.CostEstimate(
            flops=14 * HD * queries * keys // 2,
            bytes_accessed=4 * recv.size,
            transcendentals=queries * keys // 2,
        ),
        name="attention",
    )(scal, recv)


def full_spec(v):
    zeros = (0,) * len(v.shape)
    return pl.BlockSpec(v.shape, lambda i: zeros)


def whole_call(body, out_shape, n_smem, args, name, flops=0):
    smem = [pl.BlockSpec(memory_space=pltpu.SMEM)] * n_smem
    return pl.pallas_call(
        body,
        grid=(1,),
        out_shape=out_shape,
        in_specs=smem + [full_spec(v) for v in args[n_smem:]],
        out_specs=jax.tree.map(full_spec, out_shape),
        compiler_params=pltpu.CompilerParams(vmem_limit_bytes=60 * 1024 * 1024),
        cost_estimate=pl.CostEstimate(
            flops=flops,
            bytes_accessed=sum(v.size * v.dtype.itemsize for v in args)
            + sum(v.size * v.dtype.itemsize for v in jax.tree.leaves(out_shape)),
            transcendentals=0,
        ),
        name=name,
    )(*args)


def shaped(shape, dtype):
    return jax.ShapeDtypeStruct(shape, dtype)


def message_kernel(places, x, g, l1g, l1b, l2g, l2b, ob, f2b, qb, x_out, g_out):
    run = places[0] // RUN
    flip = run % 2 == 1
    t, d = x.shape

    @pl.when(flip)
    def _():
        for src, dst in ((x, x_out), (g, g_out)):
            dst[0:RUN, :] = src[RUN:t, :]
            dst[RUN:t, :] = src[0:RUN, :]

    @pl.when(jnp.logical_not(flip))
    def _():
        x_out[0:t, :] = x[...]
        g_out[...] = g[...]

    n = l1g.shape[0]
    both = run + places[RUN] // RUN
    row = lax.broadcasted_iota(jnp.int32, (16, n), 0)
    short = jnp.where(jnp.logical_and(row == 9, both == RUNS - 1), 1.0, 0.0)
    lines = [ref[...].astype(F32).reshape(1, n) for ref in (l1g, l1b, l2g, l2b, ob, f2b)]
    bias = qb[...].astype(F32).reshape(1, 3 * n)
    lines += [bias[:, i * n : (i + 1) * n] for i in range(3)]
    for i, line in enumerate(lines):
        short = jnp.where(row == i, line, short)
    x_out[t:, 0:n] = short.astype(BF)
    x_out[t:, n:] = jnp.zeros((16, d - n), BF)


def columns_kernel(w, out):
    n_fs, _, width = out.shape
    part = width // 3
    for g in range(n_fs):
        for k in range(3):
            out[g, :, k * part : (k + 1) * part] = w[:, (k * n_fs + g) * part : (k * n_fs + g + 1) * part]


def project_kernel(me, x0, x1, x2, x3, g0, g1, g2, g3, w, wo, tables, send, attn_in, mlp_in, xhat, cot, short_out, flags):
    t = g0.shape[0]
    d = g0.shape[1]
    dq = w.shape[1] // 3
    n_fs = d // dq
    blocks = (x0, x1, x2, x3)
    cots = (g0, g1, g2, g3)
    f = me[0]
    shorts = [ref[t : t + 16, :].astype(F32) for ref in blocks]
    owners = [f, f ^ 2, f ^ 1, f ^ 3]
    by_owner = []
    for o in range(n_fs):
        total = shorts[0]
        for r in range(1, n_fs):
            total = jnp.where(owners[r] == o, shorts[r], total)
        by_owner.append(total[:, :dq])
    short = jnp.concatenate(by_owner, axis=1)
    short_out[...] = short
    for r in range(n_fs):
        flags[r] = jnp.broadcast_to(shorts[r][9:10, 0:128], (8, 128))
    gain_one, shift_one, gain_two, shift_two = (short[i : i + 1] for i in range(4))
    biases = []
    for kind in range(3):
        total = jnp.zeros((1, dq), F32)
        for b in range(3 * n_fs):
            o, i = divmod(b, 3)
            total = jnp.where(kind * n_fs + f == b, by_owner[o][6 + i : 7 + i], total)
        biases.append(total)

    for r in range(n_fs):
        rows = slice(r * t, (r + 1) * t)
        v = blocks[r][0:t, :].astype(F32)
        centred = v - jnp.mean(v, axis=1, keepdims=True)
        variance = jnp.mean(centred * centred, axis=1, keepdims=True)
        hat = centred * lax.rsqrt(variance + NORM_EPS)
        xhat[rows, :] = hat
        attn_in[rows, :] = (hat * gain_one + shift_one).astype(BF)
        mlp_in[rows, :] = (hat * gain_two + shift_two).astype(BF)
        cot[rows, :] = cots[r][...]

    a = attn_in[...]
    q_all = mm(a, w[:, :dq]) + biases[0]
    k_all = mm(a, w[:, dq : 2 * dq]) + biases[1]
    v_all = mm(a, w[:, 2 * dq :]) + biases[2]
    dh_all = contract_cols(cot[...], wo[...])
    low = lax.broadcasted_iota(jnp.int32, (t, 2 * HD), 1) < HD
    for r in range(n_fs):
        rows = slice(r * t, (r + 1) * t)
        is_folded = shorts[r][9:10, 0:1] > 0.5
        cos, up, down = (jnp.where(is_folded, tables[3 + i], tables[i]) for i in range(3))

        def turn(v):
            return v * cos + pltpu.roll(v, 2 * HD - ROT // 2, 1) * up + pltpu.roll(v, ROT // 2, 1) * down

        for b in range(dq // (2 * HD)):
            cols = slice(b * 2 * HD, (b + 1) * 2 * HD)
            q = turn(q_all[rows, cols]) * (HD ** (-0.5))
            k = turn(k_all[rows, cols])
            v = v_all[rows, cols]
            dh = dh_all[rows, cols]
            for side in range(2):
                if side == 0:
                    kv = jnp.where(low, k, pltpu.roll(v, HD, 1)).astype(BF)
                    qd = jnp.where(low, q, pltpu.roll(dh, HD, 1)).astype(BF)
                else:
                    kv = jnp.where(low, pltpu.roll(k, HD, 1), v).astype(BF)
                    qd = jnp.where(low, pltpu.roll(q, HD, 1), dh).astype(BF)
                at = r * 8 + (2 * b + side) * 2
                for half in range(2):
                    send[at + half, 0:t, :] = kv
                    send[at + half, t : t + RUN, :] = qd[half * RUN : (half + 1) * RUN]


def finish_kernel(folded, home, tables, attn_in, cot, w, xhat, early, fc1, payload, d_norm, head_out, d_proj):
    t = home.shape[1] - RUN
    dq = head_out.shape[1]
    n_fs = home.shape[0] // 8
    low = lax.broadcasted_iota(jnp.int32, (t, 2 * HD), 1) < HD
    for r in range(n_fs):
        rows = slice(r * t, (r + 1) * t)
        is_folded = folded[r] == 1
        cos, up, down = (jnp.where(is_folded, tables[3 + i], tables[i]) for i in range(3))

        def turn_back(v):
            return v * cos - (pltpu.roll(v, 2 * HD - ROT // 2, 1) * up + pltpu.roll(v, ROT // 2, 1) * down)

        for b in range(dq // (2 * HD)):
            cols = slice(b * 2 * HD, (b + 1) * 2 * HD)
            dkv, qo = [], []
            for side in range(2):
                at = r * 8 + (2 * b + side) * 2
                dkv.append(home[at, 0:t, :].astype(F32) + home[at + 1, 0:t, :].astype(F32))
                qo.append(jnp.concatenate([home[at, t : t + RUN, :], home[at + 1, t : t + RUN, :]], 0).astype(F32))
            d_q = jnp.where(low, qo[0], pltpu.roll(qo[1], HD, 1))
            o = jnp.where(low, pltpu.roll(qo[0], HD, 1), qo[1])
            d_k = jnp.where(low, dkv[0], pltpu.roll(dkv[1], HD, 1))
            d_v = jnp.where(low, pltpu.roll(dkv[0], HD, 1), dkv[1])
            head_out[rows, cols] = o.astype(BF)
            d_proj[rows, cols] = (turn_back(d_q) * (HD ** (-0.5))).astype(BF)
            d_proj[rows, dq + b * 2 * HD : dq + (b + 1) * 2 * HD] = turn_back(d_k).astype(BF)
            d_proj[rows, 2 * dq + b * 2 * HD : 2 * dq + (b + 1) * 2 * HD] = d_v.astype(BF)

    n_ctx, _, rows, _ = payload.shape
    d = attn_in.shape[1]
    width = d_proj.shape[1]
    dp = d_proj[...]
    c = contract_cols(dp, w[...])
    d_norm[...] = c
    gain = jnp.sum(c * xhat[...], axis=0, keepdims=True)
    shift = jnp.sum(c, axis=0, keepdims=True)
    bias = jnp.sum(dp.astype(F32), axis=0, keepdims=True)
    last = width + 128
    payload[:, :, :, width:last] = jnp.zeros((n_ctx, n_fs, rows, 128), BF)
    first = lax.broadcasted_iota(jnp.int32, (rows, 128), 0) == 0

    def put(b, f, v):
        payload[b, f, :, width:last] = jnp.where(first, v, 0.0).astype(BF)

    for f in range(n_fs):
        grad = contract_rows(attn_in[:, f * dq : (f + 1) * dq], dp)
        payload[:, f, :, 0:width] = grad.reshape(n_ctx, rows, width).astype(BF)
        grad = contract_rows(head_out[...], cot[:, f * dq : (f + 1) * dq])
        payload[:, f, :, last : last + dq] = grad.reshape(n_ctx, rows, dq).astype(BF)
        payload[:, f, :, last + dq :] = fc1[f]
        mine = [gain, shift, early[0:1, :], early[1:2, :], early[2:3, :]]
        for i, v in enumerate(mine):
            for half in range(2):
                at = f * dq + half * 128
                put(2 * i + half, f, v[:, at : at + 128])
        for i in range(6):
            put(10 + i, f, bias[:, i * 128 : (i + 1) * 128])
        for i in range(8):
            put(16 + i, f, early[3:4, i * 128 : (i + 1) * 128])


def expand_kernel(place, *refs):
    firsts, seconds = refs[:4], refs[4:8]
    qkv, out, up, down, l1g, l1b, l2g, l2b, common, common_again, qb, f1b, lines = refs[8:]
    n_ctx = lines.shape[0]
    dq = out.shape[0]
    ff = down.shape[1]
    rows = dq // n_ctx
    me, xl, z, y = (place[i] for i in range(4))
    width = 3 * dq + 128 + dq
    for p in range(4):
        for b in range(4):
            for e in range(2):
                c = (xl ^ e) * 16 + ((z - p) % 4) * 4 + (y - b) % 4
                at = pl.ds(pl.multiple_of(c * rows, rows), rows)
                v = firsts[p][b * 2 + e].astype(F32)
                for f in range(4):
                    part = v[f * rows : (f + 1) * rows]
                    for kind in range(3):
                        qkv[at, (kind * 4 + f) * dq : (kind * 4 + f + 1) * dq] = part[:, kind * dq : (kind + 1) * dq]
                    lines[c, f : f + 1, :] = part[0:1, 3 * dq : 3 * dq + 128]
                    out[at, f * dq : (f + 1) * dq] = part[:, 3 * dq + 128 : width]
                half = 2 * rows
                low = pl.ds(pl.multiple_of(c * 4 * rows, 4 * rows), half)
                for i in range(2):
                    down[low, i * 512 : (i + 1) * 512] = v[i * half : (i + 1) * half, width:]
                c = (xl ^ e) * 16 + ((z - b) % 4) * 4 + (y - p) % 4
                at = pl.ds(pl.multiple_of(c * rows, rows), rows)
                v = seconds[p][b * 2 + e].astype(F32)
                for f in range(4):
                    up[at, f * ff : (f + 1) * ff] = v[f * rows : (f + 1) * rows, 0:ff]
                high = pl.ds(pl.multiple_of(c * 4 * rows + half, half), half)
                for i in range(2):
                    down[high, i * 512 : (i + 1) * 512] = v[i * half : (i + 1) * half, ff:]

    def line(b, f):
        return lines[b, pl.ds(f, 1), :]

    for i, ref in enumerate((l1g, l1b, l2g, l2b)):
        for half in range(2):
            total = line(2 * i + half, 0)
            for f in range(1, 4):
                total = total + line(2 * i + half, f)
            ref[half * 128 : (half + 1) * 128] = total.reshape(128)
    for half in range(2):
        v = line(8 + half, me).reshape(128)
        common[half * 128 : (half + 1) * 128] = v
        common_again[half * 128 : (half + 1) * 128] = v
    for i in range(3):
        b = 3 * me + i
        for half in range(2):
            at = (2 * i + half) * 128
            qb[at : at + 128] = line(10 + 2 * (b // 4) + half, b % 4).reshape(128)
    for i in range(8):
        f1b[i * 128 : (i + 1) * 128] = line(16 + i, me).reshape(128)


def pick(stacked, index):
    return lax.dynamic_index_in_dim(stacked, index, 0, keepdims=False)


def on_device(
    hidden_in,
    positions,
    out_grad,
    ln1_gain,
    ln1_bias,
    qkv_weight,
    qkv_bias,
    out_weight,
    out_bias,
    ln2_gain,
    ln2_bias,
    fc1_weight,
    fc1_bias,
    fc2_weight,
    fc2_bias,
):
    n_fs = 4
    n_ctx = 32
    ctx = lax.axis_index("ctx")
    me = lax.axis_index("fsdp")
    t = hidden_in.shape[1]
    d = hidden_in.shape[2]
    dq = d // n_fs
    ff = fc1_weight.shape[1] // n_fs
    tok = n_fs * t
    rows = dq // n_ctx
    me_one = me.astype(jnp.int32).reshape(1)

    flip = (positions[0, 0] // RUN) % 2 == 1

    def turned(v):
        return jnp.where(flip, jnp.concatenate([v[RUN:], v[:RUN]], 0), v)

    x_msg, cot_msg = whole_call(
        message_kernel,
        (shaped((t + 16, d), BF), shaped((t, d), BF)),
        1,
        (positions[0], hidden_in[0], out_grad[0], ln1_gain, ln1_bias, ln2_gain, ln2_bias, out_bias, fc2_bias, qkv_bias),
        "message",
    )
    x_xh = swap_xh(x_msg)
    cot_xh = swap_xh(cot_msg)
    x_all = [x_msg, x_xh, swap_core(x_msg), swap_core(x_xh)]
    cot_all = [cot_msg, cot_xh, swap_core(cot_msg), swap_core(cot_xh)]

    (qkv_columns,) = whole_call(columns_kernel, (shaped((n_fs, dq, 3 * dq), BF),), 0, (qkv_weight,), "columns")
    w_qkv = lax.all_to_all(qkv_columns, "fsdp", 0, 0).reshape(d, 3 * dq)
    w_qkv, up_own = lax.optimization_barrier((w_qkv, fc1_weight))

    def cross(v):
        return lax.ppermute(v, ("ctx", "fsdp"), [(i, i ^ (16 * n_fs + 2)) for i in range(n_ctx * n_fs)])

    def up_columns(diff):
        return lax.dynamic_slice(up_own, (0, (me ^ diff) * ff), (dq, ff))

    across = [cross(up_columns(2)), cross(up_columns(3))]
    def rel_of(owner):
        diff = jnp.bitwise_xor(me, owner)
        return (diff % 2) * 2 + diff // 2

    half = ROT // 2
    lane = jnp.arange(2 * HD) % HD
    turning = lane < ROT
    frequency = jnp.where(turning, 10000.0 ** (-2.0 * (lane % half).astype(F32) / ROT), 0.0)
    back = ctx % 2 == 1
    tables = []
    for even_run, odd_run in (
        (2 * ctx, 2 * ctx + 1),
        (jnp.where(back, 2 * n_ctx - 1 - ctx, ctx), jnp.where(back, ctx, 2 * n_ctx - 1 - ctx)),
    ):
        places = jnp.concatenate([even_run * RUN + jnp.arange(RUN), odd_run * RUN + jnp.arange(RUN)])
        phases = places.astype(F32)[:, None] * frequency[None, :]
        sines = jnp.sin(phases)
        tables += [jnp.cos(phases), jnp.where(lane < half, -sines, 0.0), jnp.where((lane >= half) & turning, sines, 0.0)]
    tables = jnp.stack(tables)

    send, attn_in, mlp_in, xhat, cot, short_all, flags = whole_call(
        project_kernel,
        (
            shaped((n_ctx, t + RUN, 2 * HD), BF),
            shaped((tok, d), BF),
            shaped((tok, d), BF),
            shaped((tok, d), F32),
            shaped((tok, d), BF),
            shaped((16, d), F32),
            shaped((n_fs, 8, 128), F32),
        ),
        1,
        (me_one, *x_all, *cot_all, w_qkv, out_weight, tables),
        "project",
        flops=2 * tok * d * 4 * dq,
    )
    gain_one, gain_two = short_all[0:1], short_all[2:3]
    both_bias = short_all[4:5] + short_all[5:6]
    folded = (flags[:, 0, 0] > 0.5).astype(jnp.int32)

    my_folded = pick(folded, ctx // 8)
    scal = jnp.stack([my_folded, ctx % 2]).astype(jnp.int32)
    across, _ = lax.optimization_barrier((across, send))
    up_rel = jnp.stack([up_columns(0), across[0], swap_core(up_columns(1)), swap_core(across[1])])
    w_up = jnp.concatenate([pick(up_rel, rel_of(o)) for o in range(n_fs)], 0)
    recv = lax.all_to_all(send, "ctx", 0, 0)

    pre_act = mm(mlp_in, w_up) + fc1_bias.astype(F32)[None]
    act_float, pull_act = jax.vjp(lambda v: jax.nn.gelu(v, approximate=False), pre_act)
    activated = act_float.astype(BF)
    d_pre = pull_act(contract_cols(cot, fc2_weight))[0].astype(BF)
    fc2_grad = contract_rows(activated, cot).astype(BF)
    fc1_grad = contract_rows(mlp_in, d_pre).astype(BF)
    xl, z, y = ctx // 16, (ctx // 4) % 4, ctx % 4
    spot = {"xl": xl, "z": z, "y": y}

    def shift(v, axis, by):
        size, stride = {"y": (4, 1), "z": (4, 4), "xl": (2, 16)}[axis]
        perm = []
        for i in range(n_ctx):
            p = (i // stride) % size
            perm.append((i, i + ((p + by) % size - p) * stride))
        return lax.ppermute(v, "ctx", perm)

    recv, fc2_grad, scal = lax.optimization_barrier((recv, fc2_grad, scal))
    down_got = lax.all_to_all(fc2_grad.reshape(n_ctx, ff // n_ctx, d), "ctx", 0, 0)

    grads = attention(scal, recv)
    grads, down_got = lax.optimization_barrier((grads, down_got))
    home = lax.all_to_all(grads, "ctx", 0, 0)
    down_share = jnp.sum(down_got.astype(F32), 0).astype(BF)

    mlp_part = mm(activated, fc2_weight)
    d_norm_two = contract_cols(d_pre, w_up)
    early = jnp.stack(
        [
            jnp.sum(d_norm_two * xhat, 0),
            jnp.sum(d_norm_two, 0),
            jnp.sum(cot.astype(F32), 0),
            jnp.sum(d_pre, 0, dtype=F32),
        ]
    )
    payload, d_norm_one, head_out, _ = whole_call(
        finish_kernel,
        (
            shaped((n_ctx, n_fs, rows, 4 * dq + 128 + ff), BF),
            shaped((tok, d), F32),
            shaped((tok, dq), BF),
            shaped((tok, 3 * dq), BF),
        ),
        1,
        (folded, home, tables, attn_in, cot, w_qkv, xhat, early, fc1_grad.reshape(n_fs, n_ctx, rows, ff)),
        "finish",
        flops=2 * tok * d * 7 * dq,
    )
    def to_owner(pieces):
        for_core = jnp.stack([pick(pieces, me ^ 1), pick(pieces, me ^ 3)])
        from_core = swap_core(for_core)
        from_xh = swap_xh(jnp.stack([pick(pieces, me ^ 2), from_core[1]]))
        rel = jnp.stack([pick(pieces, me), from_xh[0], from_core[0], from_xh[1]])
        return jnp.stack([pick(rel, rel_of(o)) for o in range(n_fs)])

    got = lax.all_to_all(payload, "ctx", 0, 0)

    def scatter_fsdp(parts):
        parts = parts.reshape(2, 2, t, d)
        here = parts[0] + swap_core(parts[1].astype(BF)).astype(F32)
        return here[0] + swap_xh(here[1].astype(BF)).astype(F32)

    block = scatter_fsdp(mlp_part + mm(head_out, out_weight))

    u = scatter_fsdp(d_norm_one * gain_one + d_norm_two * gain_two)
    got, block, u = lax.optimization_barrier((got, block, u))
    share = jnp.sum(got.astype(F32), 0).astype(BF)
    width = 3 * dq + 128
    owned = to_owner(jnp.concatenate([share[..., :width], share[..., width + dq :]], 2))
    first = jnp.concatenate([owned[..., :width], share[..., width : width + dq]], 2).reshape(n_fs * rows, width + dq)
    second = owned[..., width:].reshape(n_fs * rows, ff)
    down_halves = down_share.reshape(2, 2 * rows, 2, d // 2).transpose(0, 2, 1, 3).reshape(2, 4 * rows, d // 2)
    first = jnp.concatenate([first, down_halves[0]], 1)
    second = jnp.concatenate([second, down_halves[1]], 1)

    def joined(parts):
        v = jnp.concatenate([p[None] for p in parts], 0)
        return v.reshape((-1,) + v.shape[2:])

    def around(v, axis):
        return [v] + [shift(v, axis, s) for s in range(1, 4)]

    both = jnp.concatenate([first, second], 1)
    both = jnp.stack([both, shift(both, "xl", 1)])
    cut = first.shape[1]
    near = (around(both[..., :cut], "y"), around(both[..., cut:], "z"))
    near = lax.optimization_barrier(near)
    firsts = around(joined(near[0]), "z")
    seconds = around(joined(near[1]), "y")

    place = jnp.stack([me, xl, z, y]).astype(jnp.int32)
    grads_out = whole_call(
        expand_kernel,
        (shaped((dq, 3 * d), F32), shaped((dq, d), F32), shaped((dq, n_fs * ff), F32), shaped((ff, d), F32))
        + (shaped((dq,), F32),) * 6
        + (shaped((3 * dq,), F32), shaped((ff,), F32), shaped((n_ctx, n_fs, 128), F32)),
        1,
        (place, *firsts, *seconds),
        "expand",
    )
    qkv_out, out_out, fc1_out, fc2_out, l1g, l1b, l2g, l2b, out_bias_out, fc2_bias_out, qkv_bias_out, fc1_bias_out, _ = (
        grads_out
    )

    x_float = x_msg[:t].astype(F32)
    block_out = turned((x_float + block + both_bias).astype(BF))
    centred = x_float - jnp.mean(x_float, axis=-1, keepdims=True)
    rstd_own = lax.rsqrt(jnp.mean(centred * centred, axis=-1, keepdims=True) + NORM_EPS)
    xhat_own = centred * rstd_own
    dx = rstd_own * (
        u - jnp.mean(u, axis=-1, keepdims=True) - xhat_own * jnp.mean(u * xhat_own, axis=-1, keepdims=True)
    )
    input_grad = turned((cot_msg.astype(F32) + dx).astype(BF))

    return (
        block_out[None],
        input_grad[None],
        l1g,
        l1b,
        qkv_out,
        qkv_bias_out,
        out_out,
        out_bias_out,
        l2g,
        l2b,
        fc1_out,
        fc1_bias_out,
        fc2_out,
        fc2_bias_out,
    )


def solution(mesh):
    token = P("fsdp", "ctx", None)
    placed = (
        token,
        P("fsdp", "ctx"),
        token,
        P("fsdp"),
        P("fsdp"),
        P("fsdp", None),
        P("fsdp"),
        P("fsdp", None),
        P("fsdp"),
        P("fsdp"),
        P("fsdp"),
        P("fsdp", None),
        P("fsdp"),
        P("fsdp", None),
        P("fsdp"),
    )
    return jax.shard_map(
        on_device,
        mesh=mesh,
        in_specs=placed,
        out_specs=(
            token,
            token,
            P("fsdp"),
            P("fsdp"),
            P("fsdp", None),
            P("fsdp"),
            P("fsdp", None),
            P("fsdp"),
            P("fsdp"),
            P("fsdp"),
            P("fsdp", None),
            P("fsdp"),
            P("fsdp", None),
            P("fsdp"),
        ),
        check_vma=False,
    )
```

```python
import jax
import jax.numpy as jnp
from jax import lax
from jax.experimental import pallas as pl
from jax.experimental.pallas import tpu as pltpu
from jax.sharding import PartitionSpec as P

H = 16
HD = 64
ROT = 16
RUN = 64
RUNS = 64
NORM_EPS = 1e-05
BF = jnp.bfloat16
F32 = jnp.float32
NEG = -1e30

QT = 512
KT = 1024


def mm(a, b):
    return jnp.dot(a, b, preferred_element_type=F32)


def contract_rows(a, b):
    return lax.dot_general(a, b, (((0,), (0,)), ((), ())), preferred_element_type=F32)


def contract_cols(a, b):
    return lax.dot_general(a, b, (((1,), (1,)), ((), ())), preferred_element_type=F32)


def swap_xh(v):
    return lax.ppermute(v, "fsdp", [(i, i ^ 2) for i in range(4)])


def swap_core(v):
    return lax.ppermute(v, "fsdp", [(i, i ^ 1) for i in range(4)])


def attention_kernel(scal, recv, out, kv, qx, yx, dkv, oq, sbuf, dbuf):
    folded = scal[0]
    odd = scal[1]
    lane = lax.broadcasted_iota(jnp.int32, (RUN, 2 * HD), 1)
    low_half = lane < HD
    n_src = recv.shape[0]
    tiles = qx.shape[0]
    per_tile = QT // RUN

    def runs(c):
        turned = jnp.logical_and(folded == 1, c % 2 == 1)
        even = jnp.where(folded == 1, jnp.where(turned, 2 * n_src - 1 - c, c), 2 * c)
        other = jnp.where(folded == 1, jnp.where(turned, c, 2 * n_src - 1 - c), 2 * c + 1)
        return even, other

    def sort_in(c, carry):
        even, other = runs(c)
        kv[pl.ds(pl.multiple_of(even * RUN, RUN), RUN), :] = recv[c, 0:RUN, :]
        kv[pl.ds(pl.multiple_of(other * RUN, RUN), RUN), :] = recv[c, RUN : 2 * RUN, :]
        rank = jnp.where(odd == 1, other, even) // 2
        tile = rank // per_tile
        place = pl.multiple_of((rank % per_tile) * RUN, RUN)
        qd = recv[c, 2 * RUN : 3 * RUN, :]
        zero = jnp.zeros_like(qd)
        q_only = jnp.where(low_half, qd, zero)
        d_only = jnp.where(low_half, zero, qd)
        qx[tile, pl.ds(place, RUN), :] = q_only
        qx[tile, pl.ds(QT + place, RUN), :] = d_only
        yx[tile, pl.ds(place, RUN), :] = d_only
        yx[tile, pl.ds(QT + place, RUN), :] = q_only
        return carry

    lax.fori_loop(0, n_src, sort_in, 0)
    dkv[...] = jnp.zeros_like(dkv)

    row = lax.broadcasted_iota(jnp.int32, (QT, KT), 0)
    col = lax.broadcasted_iota(jnp.int32, (QT, KT), 1)
    row_place = (2 * (row // RUN) + odd) * RUN + row % RUN
    allowed = col <= row_place

    def fold(v, op):
        parts = [v[:, i * 128 : (i + 1) * 128] for i in range(KT // 128)]
        total = parts[0]
        for part in parts[1:]:
            total = op(total, part)
        return total

    def tile_step(j, carry):
        x = qx[j]
        y = yx[j]

        def products(k):
            keys = kv[pl.ds(pl.multiple_of(k * KT, KT), KT), :]
            both = contract_cols(x, keys)
            return both[:QT], both[QT:]

        def pass_one(k, top):
            s, d = products(k)
            sbuf[k] = s
            dbuf[k] = d
            return jnp.maximum(top, fold(s, jnp.maximum))

        top = lax.fori_loop(0, j, pass_one, jnp.full((QT, 128), NEG, F32), unroll=2 if j else 1)
        s, d = products(j)
        s = jnp.where(allowed, s, NEG)
        sbuf[j] = s
        dbuf[j] = d
        top = jnp.maximum(top, fold(s, jnp.maximum))
        top = jnp.max(top, axis=1, keepdims=True)

        def pass_two(k, sums):
            total, weighted = sums
            e = jnp.exp(sbuf[k] - top)
            sbuf[k] = e
            return total + fold(e, jnp.add), weighted + fold(e * dbuf[k], jnp.add)

        zero = jnp.zeros((QT, 128), F32)
        total, weighted = lax.fori_loop(0, j + 1, pass_two, (zero, zero), unroll=2)
        scale = 1.0 / jnp.sum(total, axis=1, keepdims=True)
        delta = jnp.sum(weighted, axis=1, keepdims=True) * scale

        def pass_three(k, acc):
            rows = pl.ds(pl.multiple_of(k * KT, KT), KT)
            p = sbuf[k] * scale
            ds = p * (dbuf[k] - delta)
            a = jnp.concatenate([p.astype(BF), ds.astype(BF)], axis=0)
            dkv[rows, :] += contract_rows(a, y)
            return acc + mm(a, kv[rows, :])

        acc = lax.fori_loop(0, j + 1, pass_three, jnp.zeros((2 * QT, 2 * HD), F32), unroll=2)
        wide = lax.broadcasted_iota(jnp.int32, (QT, 2 * HD), 1) < HD
        oq[pl.ds(j * QT, QT), :] = jnp.where(wide, acc[QT:], acc[:QT]).astype(BF)
        return carry

    for j in range(tiles):
        tile_step(j, 0)

    def sort_out(c, carry):
        even, other = runs(c)
        out[c, 0:RUN, :] = dkv[pl.ds(pl.multiple_of(even * RUN, RUN), RUN), :].astype(BF)
        out[c, RUN : 2 * RUN, :] = dkv[pl.ds(pl.multiple_of(other * RUN, RUN), RUN), :].astype(BF)
        rank = jnp.where(odd == 1, other, even) // 2
        out[c, 2 * RUN : 3 * RUN, :] = oq[pl.ds(pl.multiple_of(rank * RUN, RUN), RUN), :]
        return carry

    lax.fori_loop(0, n_src, sort_out, 0)


def attention(scal, recv):
    n_src = recv.shape[0]
    keys = n_src * 2 * RUN
    queries = n_src * RUN
    tiles = queries // QT
    return pl.pallas_call(
        attention_kernel,
        out_shape=jax.ShapeDtypeStruct(recv.shape, BF),
        in_specs=[pl.BlockSpec(memory_space=pltpu.SMEM), pl.BlockSpec(memory_space=pltpu.VMEM)],
        out_specs=pl.BlockSpec(memory_space=pltpu.VMEM),
        scratch_shapes=[
            pltpu.VMEM((keys, 2 * HD), BF),
            pltpu.VMEM((tiles, 2 * QT, 2 * HD), BF),
            pltpu.VMEM((tiles, 2 * QT, 2 * HD), BF),
            pltpu.VMEM((keys, 2 * HD), F32),
            pltpu.VMEM((queries, 2 * HD), BF),
            pltpu.VMEM((keys // KT, QT, KT), F32),
            pltpu.VMEM((keys // KT, QT, KT), F32),
        ],
        compiler_params=pltpu.CompilerParams(vmem_limit_bytes=60 * 1024 * 1024),
        cost_estimate=pl.CostEstimate(
            flops=14 * HD * queries * keys // 2,
            bytes_accessed=4 * recv.size,
            transcendentals=queries * keys // 2,
        ),
        name="attention",
    )(scal, recv)


def full_spec(v):
    zeros = (0,) * len(v.shape)
    return pl.BlockSpec(v.shape, lambda i: zeros)


def whole_call(body, out_shape, n_smem, args, name, flops=0):
    smem = [pl.BlockSpec(memory_space=pltpu.SMEM)] * n_smem
    return pl.pallas_call(
        body,
        grid=(1,),
        out_shape=out_shape,
        in_specs=smem + [full_spec(v) for v in args[n_smem:]],
        out_specs=jax.tree.map(full_spec, out_shape),
        compiler_params=pltpu.CompilerParams(vmem_limit_bytes=60 * 1024 * 1024),
        cost_estimate=pl.CostEstimate(
            flops=flops,
            bytes_accessed=sum(v.size * v.dtype.itemsize for v in args)
            + sum(v.size * v.dtype.itemsize for v in jax.tree.leaves(out_shape)),
            transcendentals=0,
        ),
        name=name,
    )(*args)


def shaped(shape, dtype):
    return jax.ShapeDtypeStruct(shape, dtype)


def message_kernel(places, x, g, l1g, l1b, l2g, l2b, ob, f2b, qb, x_out, g_out):
    run = places[0] // RUN
    flip = run % 2 == 1
    t, d = x.shape

    @pl.when(flip)
    def _():
        for src, dst in ((x, x_out), (g, g_out)):
            dst[0:RUN, :] = src[RUN:t, :]
            dst[RUN:t, :] = src[0:RUN, :]

    @pl.when(jnp.logical_not(flip))
    def _():
        x_out[0:t, :] = x[...]
        g_out[...] = g[...]

    n = l1g.shape[0]
    both = run + places[RUN] // RUN
    row = lax.broadcasted_iota(jnp.int32, (16, n), 0)
    short = jnp.where(jnp.logical_and(row == 9, both == RUNS - 1), 1.0, 0.0)
    lines = [ref[...].astype(F32).reshape(1, n) for ref in (l1g, l1b, l2g, l2b, ob, f2b)]
    bias = qb[...].astype(F32).reshape(1, 3 * n)
    lines += [bias[:, i * n : (i + 1) * n] for i in range(3)]
    for i, line in enumerate(lines):
        short = jnp.where(row == i, line, short)
    x_out[t:, 0:n] = short.astype(BF)
    x_out[t:, n:] = jnp.zeros((16, d - n), BF)


def columns_kernel(w, out):
    n_fs, _, width = out.shape
    part = width // 3
    for g in range(n_fs):
        for k in range(3):
            out[g, :, k * part : (k + 1) * part] = w[:, (k * n_fs + g) * part : (k * n_fs + g + 1) * part]


def project_kernel(me, x0, x1, x2, x3, g0, g1, g2, g3, w, wo, tables, send, attn_in, mlp_in, xhat, cot, short_out, flags):
    t = g0.shape[0]
    d = g0.shape[1]
    dq = w.shape[1] // 3
    n_fs = d // dq
    blocks = (x0, x1, x2, x3)
    cots = (g0, g1, g2, g3)
    f = me[0]
    shorts = [ref[t : t + 16, :].astype(F32) for ref in blocks]
    owners = [f, f ^ 2, f ^ 1, f ^ 3]
    by_owner = []
    for o in range(n_fs):
        total = shorts[0]
        for r in range(1, n_fs):
            total = jnp.where(owners[r] == o, shorts[r], total)
        by_owner.append(total[:, :dq])
    short = jnp.concatenate(by_owner, axis=1)
    short_out[...] = short
    for r in range(n_fs):
        flags[r] = jnp.broadcast_to(shorts[r][9:10, 0:128], (8, 128))
    gain_one, shift_one, gain_two, shift_two = (short[i : i + 1] for i in range(4))
    biases = []
    for kind in range(3):
        total = jnp.zeros((1, dq), F32)
        for b in range(3 * n_fs):
            o, i = divmod(b, 3)
            total = jnp.where(kind * n_fs + f == b, by_owner[o][6 + i : 7 + i], total)
        biases.append(total)

    for r in range(n_fs):
        rows = slice(r * t, (r + 1) * t)
        v = blocks[r][0:t, :].astype(F32)
        centred = v - jnp.mean(v, axis=1, keepdims=True)
        variance = jnp.mean(centred * centred, axis=1, keepdims=True)
        hat = centred * lax.rsqrt(variance + NORM_EPS)
        xhat[rows, :] = hat
        attn_in[rows, :] = (hat * gain_one + shift_one).astype(BF)
        mlp_in[rows, :] = (hat * gain_two + shift_two).astype(BF)
        cot[rows, :] = cots[r][...]

    a = attn_in[...]
    q_all = mm(a, w[:, :dq]) + biases[0]
    k_all = mm(a, w[:, dq : 2 * dq]) + biases[1]
    v_all = mm(a, w[:, 2 * dq :]) + biases[2]
    dh_all = contract_cols(cot[...], wo[...])
    low = lax.broadcasted_iota(jnp.int32, (t, 2 * HD), 1) < HD
    for r in range(n_fs):
        rows = slice(r * t, (r + 1) * t)
        is_folded = shorts[r][9:10, 0:1] > 0.5
        cos, up, down = (jnp.where(is_folded, tables[3 + i], tables[i]) for i in range(3))

        def turn(v):
            return v * cos + pltpu.roll(v, 2 * HD - ROT // 2, 1) * up + pltpu.roll(v, ROT // 2, 1) * down

        for b in range(dq // (2 * HD)):
            cols = slice(b * 2 * HD, (b + 1) * 2 * HD)
            q = turn(q_all[rows, cols]) * (HD ** (-0.5))
            k = turn(k_all[rows, cols])
            v = v_all[rows, cols]
            dh = dh_all[rows, cols]
            for side in range(2):
                if side == 0:
                    kv = jnp.where(low, k, pltpu.roll(v, HD, 1)).astype(BF)
                    qd = jnp.where(low, q, pltpu.roll(dh, HD, 1)).astype(BF)
                else:
                    kv = jnp.where(low, pltpu.roll(k, HD, 1), v).astype(BF)
                    qd = jnp.where(low, pltpu.roll(q, HD, 1), dh).astype(BF)
                at = r * 8 + (2 * b + side) * 2
                for half in range(2):
                    send[at + half, 0:t, :] = kv
                    send[at + half, t : t + RUN, :] = qd[half * RUN : (half + 1) * RUN]


def finish_kernel(folded, home, tables, attn_in, cot, w, xhat, early, fc1, payload, d_norm, head_out, d_proj):
    t = home.shape[1] - RUN
    dq = head_out.shape[1]
    n_fs = home.shape[0] // 8
    low = lax.broadcasted_iota(jnp.int32, (t, 2 * HD), 1) < HD
    for r in range(n_fs):
        rows = slice(r * t, (r + 1) * t)
        is_folded = folded[r] == 1
        cos, up, down = (jnp.where(is_folded, tables[3 + i], tables[i]) for i in range(3))

        def turn_back(v):
            return v * cos - (pltpu.roll(v, 2 * HD - ROT // 2, 1) * up + pltpu.roll(v, ROT // 2, 1) * down)

        for b in range(dq // (2 * HD)):
            cols = slice(b * 2 * HD, (b + 1) * 2 * HD)
            dkv, qo = [], []
            for side in range(2):
                at = r * 8 + (2 * b + side) * 2
                dkv.append(home[at, 0:t, :].astype(F32) + home[at + 1, 0:t, :].astype(F32))
                qo.append(jnp.concatenate([home[at, t : t + RUN, :], home[at + 1, t : t + RUN, :]], 0).astype(F32))
            d_q = jnp.where(low, qo[0], pltpu.roll(qo[1], HD, 1))
            o = jnp.where(low, pltpu.roll(qo[0], HD, 1), qo[1])
            d_k = jnp.where(low, dkv[0], pltpu.roll(dkv[1], HD, 1))
            d_v = jnp.where(low, pltpu.roll(dkv[0], HD, 1), dkv[1])
            head_out[rows, cols] = o.astype(BF)
            d_proj[rows, cols] = (turn_back(d_q) * (HD ** (-0.5))).astype(BF)
            d_proj[rows, dq + b * 2 * HD : dq + (b + 1) * 2 * HD] = turn_back(d_k).astype(BF)
            d_proj[rows, 2 * dq + b * 2 * HD : 2 * dq + (b + 1) * 2 * HD] = d_v.astype(BF)

    n_ctx, _, rows, _ = payload.shape
    d = attn_in.shape[1]
    width = d_proj.shape[1]
    dp = d_proj[...]
    c = contract_cols(dp, w[...])
    d_norm[...] = c
    gain = jnp.sum(c * xhat[...], axis=0, keepdims=True)
    shift = jnp.sum(c, axis=0, keepdims=True)
    bias = jnp.sum(dp.astype(F32), axis=0, keepdims=True)
    last = width + 128
    payload[:, :, :, width:last] = jnp.zeros((n_ctx, n_fs, rows, 128), BF)
    first = lax.broadcasted_iota(jnp.int32, (rows, 128), 0) == 0

    def put(b, f, v):
        payload[b, f, :, width:last] = jnp.where(first, v, 0.0).astype(BF)

    for f in range(n_fs):
        grad = contract_rows(attn_in[:, f * dq : (f + 1) * dq], dp)
        payload[:, f, :, 0:width] = grad.reshape(n_ctx, rows, width).astype(BF)
        grad = contract_rows(head_out[...], cot[:, f * dq : (f + 1) * dq])
        payload[:, f, :, last : last + dq] = grad.reshape(n_ctx, rows, dq).astype(BF)
        payload[:, f, :, last + dq :] = fc1[f]
        mine = [gain, shift, early[0:1, :], early[1:2, :], early[2:3, :]]
        for i, v in enumerate(mine):
            for half in range(2):
                at = f * dq + half * 128
                put(2 * i + half, f, v[:, at : at + 128])
        for i in range(6):
            put(10 + i, f, bias[:, i * 128 : (i + 1) * 128])
        for i in range(8):
            put(16 + i, f, early[3:4, i * 128 : (i + 1) * 128])


def reduce_kernel(me, got, pieces, out_share):
    n_ctx, n_fs = got.shape[:2]
    dq = out_share.shape[2]
    width = 3 * dq + 128
    for f in range(n_fs):
        total = got[0, f].astype(F32)
        for c in range(1, n_ctx):
            total = total + got[c, f].astype(F32)
        total = total.astype(BF)
        diff = me[0] ^ f
        at = (diff % 2) * 2 + diff // 2
        pieces[at, :, 0:width] = total[:, 0:width]
        pieces[at, :, width:] = total[:, width + dq :]
        out_share[f] = total[:, width : width + dq]


def expand_kernel(place, *refs):
    firsts, seconds = refs[:4], refs[4:8]
    qkv, out, up, down, l1g, l1b, l2g, l2b, common, common_again, qb, f1b, lines = refs[8:]
    n_ctx = lines.shape[0]
    dq = out.shape[0]
    ff = down.shape[1]
    rows = dq // n_ctx
    me, xl, z, y = (place[i] for i in range(4))
    width = 3 * dq + 128 + dq
    for p in range(4):
        for b in range(4):
            for e in range(2):
                c = (xl ^ e) * 16 + ((z - p) % 4) * 4 + (y - b) % 4
                at = pl.ds(pl.multiple_of(c * rows, rows), rows)
                v = firsts[p][b * 2 + e].astype(F32)
                for f in range(4):
                    part = v[f * rows : (f + 1) * rows]
                    for kind in range(3):
                        qkv[at, (kind * 4 + f) * dq : (kind * 4 + f + 1) * dq] = part[:, kind * dq : (kind + 1) * dq]
                    lines[c, f : f + 1, :] = part[0:1, 3 * dq : 3 * dq + 128]
                    out[at, f * dq : (f + 1) * dq] = part[:, 3 * dq + 128 : width]
                half = 2 * rows
                low = pl.ds(pl.multiple_of(c * 4 * rows, 4 * rows), half)
                for i in range(2):
                    down[low, i * 512 : (i + 1) * 512] = v[i * half : (i + 1) * half, width:]
                c = (xl ^ e) * 16 + ((z - b) % 4) * 4 + (y - p) % 4
                at = pl.ds(pl.multiple_of(c * rows, rows), rows)
                v = seconds[p][b * 2 + e].astype(F32)
                for f in range(4):
                    up[at, f * ff : (f + 1) * ff] = v[f * rows : (f + 1) * rows, 0:ff]
                high = pl.ds(pl.multiple_of(c * 4 * rows + half, half), half)
                for i in range(2):
                    down[high, i * 512 : (i + 1) * 512] = v[i * half : (i + 1) * half, ff:]

    def line(b, f):
        return lines[b, pl.ds(f, 1), :]

    for i, ref in enumerate((l1g, l1b, l2g, l2b)):
        for half in range(2):
            total = line(2 * i + half, 0)
            for f in range(1, 4):
                total = total + line(2 * i + half, f)
            ref[half * 128 : (half + 1) * 128] = total.reshape(128)
    for half in range(2):
        v = line(8 + half, me).reshape(128)
        common[half * 128 : (half + 1) * 128] = v
        common_again[half * 128 : (half + 1) * 128] = v
    for i in range(3):
        b = 3 * me + i
        for half in range(2):
            at = (2 * i + half) * 128
            qb[at : at + 128] = line(10 + 2 * (b // 4) + half, b % 4).reshape(128)
    for i in range(8):
        f1b[i * 128 : (i + 1) * 128] = line(16 + i, me).reshape(128)


def pick(stacked, index):
    return lax.dynamic_index_in_dim(stacked, index, 0, keepdims=False)


def on_device(
    hidden_in,
    positions,
    out_grad,
    ln1_gain,
    ln1_bias,
    qkv_weight,
    qkv_bias,
    out_weight,
    out_bias,
    ln2_gain,
    ln2_bias,
    fc1_weight,
    fc1_bias,
    fc2_weight,
    fc2_bias,
):
    n_fs = 4
    n_ctx = 32
    ctx = lax.axis_index("ctx")
    me = lax.axis_index("fsdp")
    t = hidden_in.shape[1]
    d = hidden_in.shape[2]
    dq = d // n_fs
    ff = fc1_weight.shape[1] // n_fs
    tok = n_fs * t
    rows = dq // n_ctx
    me_one = me.astype(jnp.int32).reshape(1)

    flip = (positions[0, 0] // RUN) % 2 == 1

    def turned(v):
        return jnp.where(flip, jnp.concatenate([v[RUN:], v[:RUN]], 0), v)

    x_msg, cot_msg = whole_call(
        message_kernel,
        (shaped((t + 16, d), BF), shaped((t, d), BF)),
        1,
        (positions[0], hidden_in[0], out_grad[0], ln1_gain, ln1_bias, ln2_gain, ln2_bias, out_bias, fc2_bias, qkv_bias),
        "message",
    )
    x_xh = swap_xh(x_msg)
    cot_xh = swap_xh(cot_msg)
    x_all = [x_msg, x_xh, swap_core(x_msg), swap_core(x_xh)]
    cot_all = [cot_msg, cot_xh, swap_core(cot_msg), swap_core(cot_xh)]

    (qkv_columns,) = whole_call(columns_kernel, (shaped((n_fs, dq, 3 * dq), BF),), 0, (qkv_weight,), "columns")
    w_qkv = lax.all_to_all(qkv_columns, "fsdp", 0, 0).reshape(d, 3 * dq)

    def up_columns(diff):
        return lax.dynamic_slice(fc1_weight, (0, (me ^ diff) * ff), (dq, ff))

    def cross(v, diff):
        return lax.ppermute(v, ("ctx", "fsdp"), [(i, i ^ (16 * n_fs + diff)) for i in range(n_ctx * n_fs)])

    up_parts = lax.optimization_barrier((w_qkv,) + tuple(up_columns(i) for i in range(4)))
    w_qkv = up_parts[0]
    up_rel = [up_parts[1], cross(up_parts[3], 2), swap_core(up_parts[2]), cross(up_parts[4], 3)]

    def rel_of(owner):
        diff = jnp.bitwise_xor(me, owner)
        return (diff % 2) * 2 + diff // 2

    half = ROT // 2
    lane = jnp.arange(2 * HD) % HD
    turning = lane < ROT
    frequency = jnp.where(turning, 10000.0 ** (-2.0 * (lane % half).astype(F32) / ROT), 0.0)
    back = ctx % 2 == 1
    tables = []
    for even_run, odd_run in (
        (2 * ctx, 2 * ctx + 1),
        (jnp.where(back, 2 * n_ctx - 1 - ctx, ctx), jnp.where(back, ctx, 2 * n_ctx - 1 - ctx)),
    ):
        places = jnp.concatenate([even_run * RUN + jnp.arange(RUN), odd_run * RUN + jnp.arange(RUN)])
        phases = places.astype(F32)[:, None] * frequency[None, :]
        sines = jnp.sin(phases)
        tables += [jnp.cos(phases), jnp.where(lane < half, -sines, 0.0), jnp.where((lane >= half) & turning, sines, 0.0)]
    tables = jnp.stack(tables)

    send, attn_in, mlp_in, xhat, cot, short_all, flags = whole_call(
        project_kernel,
        (
            shaped((n_ctx, t + RUN, 2 * HD), BF),
            shaped((tok, d), BF),
            shaped((tok, d), BF),
            shaped((tok, d), F32),
            shaped((tok, d), BF),
            shaped((16, d), F32),
            shaped((n_fs, 8, 128), F32),
        ),
        1,
        (me_one, *x_all, *cot_all, w_qkv, out_weight, tables),
        "project",
        flops=2 * tok * d * 4 * dq,
    )
    gain_one, gain_two = short_all[0:1], short_all[2:3]
    both_bias = short_all[4:5] + short_all[5:6]
    folded = (flags[:, 0, 0] > 0.5).astype(jnp.int32)

    my_folded = pick(folded, ctx // 8)
    scal = jnp.stack([my_folded, ctx % 2]).astype(jnp.int32)
    up_rel = jnp.stack(up_rel)
    w_up = jnp.concatenate([pick(up_rel, rel_of(o)) for o in range(n_fs)], 0)
    recv = lax.all_to_all(send, "ctx", 0, 0)

    pre_act = mm(mlp_in, w_up) + fc1_bias.astype(F32)[None]
    act_float, pull_act = jax.vjp(lambda v: jax.nn.gelu(v, approximate=False), pre_act)
    activated = act_float.astype(BF)
    d_pre = pull_act(contract_cols(cot, fc2_weight))[0].astype(BF)
    fc2_grad = contract_rows(activated, cot).astype(BF)
    fc1_grad = contract_rows(mlp_in, d_pre).astype(BF)
    xl, z, y = ctx // 16, (ctx // 4) % 4, ctx % 4
    spot = {"xl": xl, "z": z, "y": y}

    def shift(v, axis, by):
        size, stride = {"y": (4, 1), "z": (4, 4), "xl": (2, 16)}[axis]
        perm = []
        for i in range(n_ctx):
            p = (i // stride) % size
            perm.append((i, i + ((p + by) % size - p) * stride))
        return lax.ppermute(v, "ctx", perm)

    recv, fc2_grad, scal = lax.optimization_barrier((recv, fc2_grad, scal))
    down_got = lax.all_to_all(fc2_grad.reshape(n_ctx, ff // n_ctx, d), "ctx", 0, 0)

    grads = attention(scal, recv)
    grads, down_got = lax.optimization_barrier((grads, down_got))
    home = lax.all_to_all(grads, "ctx", 0, 0)
    down_share = jnp.sum(down_got.astype(F32), 0).astype(BF)

    mlp_part = mm(activated, fc2_weight)
    d_norm_two = contract_cols(d_pre, w_up)
    early = jnp.stack(
        [
            jnp.sum(d_norm_two * xhat, 0),
            jnp.sum(d_norm_two, 0),
            jnp.sum(cot.astype(F32), 0),
            jnp.sum(d_pre, 0, dtype=F32),
        ]
    )
    early, down_share = lax.optimization_barrier((early, down_share))

    payload, d_norm_one, head_out, _ = whole_call(
        finish_kernel,
        (
            shaped((n_ctx, n_fs, rows, 4 * dq + 128 + ff), BF),
            shaped((tok, d), F32),
            shaped((tok, dq), BF),
            shaped((tok, 3 * dq), BF),
        ),
        1,
        (folded, home, tables, attn_in, cot, w_qkv, xhat, early, fc1_grad.reshape(n_fs, n_ctx, rows, ff)),
        "finish",
        flops=2 * tok * d * 7 * dq,
    )
    got = lax.all_to_all(payload, "ctx", 0, 0)

    def scatter_fsdp(parts):
        parts = parts.reshape(2, 2, t, d)
        here = parts[0] + swap_core(parts[1].astype(BF)).astype(F32)
        return here[0] + swap_xh(here[1].astype(BF)).astype(F32)

    block = scatter_fsdp(mlp_part + mm(head_out, out_weight))

    u = scatter_fsdp(d_norm_one * gain_one + d_norm_two * gain_two)
    width = 3 * dq + 128
    pieces, out_share = whole_call(
        reduce_kernel,
        (shaped((n_fs, rows, width + ff), BF), shaped((n_fs, rows, dq), BF)),
        1,
        (me_one, got),
        "reduce",
    )
    from_core = swap_core(pieces[2:])
    from_xh = swap_xh(jnp.stack([pieces[1], from_core[1]]))
    rel = jnp.stack([pieces[0], from_xh[0], from_core[0], from_xh[1]])
    owned = jnp.stack([pick(rel, rel_of(o)) for o in range(n_fs)])
    first = jnp.concatenate([owned[..., :width], out_share], 2).reshape(n_fs * rows, width + dq)
    second = owned[..., width:].reshape(n_fs * rows, ff)
    down_halves = down_share.reshape(2, 2 * rows, 2, d // 2).transpose(0, 2, 1, 3).reshape(2, 4 * rows, d // 2)
    first = jnp.concatenate([first, down_halves[0]], 1)
    second = jnp.concatenate([second, down_halves[1]], 1)

    def joined(parts):
        v = jnp.concatenate([p[None] for p in parts], 0)
        return v.reshape((-1,) + v.shape[2:])

    def around(v, axis):
        return [v] + [shift(v, axis, s) for s in range(1, 4)]

    both = jnp.concatenate([first, second], 1)
    both, block, u = lax.optimization_barrier((both, block, u))
    both = jnp.stack([both, shift(both, "xl", 1)])
    cut = first.shape[1]
    near = (around(both[..., :cut], "y"), around(both[..., cut:], "z"))
    near = lax.optimization_barrier(near)
    firsts = around(joined(near[0]), "z")
    seconds = around(joined(near[1]), "y")

    place = jnp.stack([me, xl, z, y]).astype(jnp.int32)
    grads_out = whole_call(
        expand_kernel,
        (shaped((dq, 3 * d), F32), shaped((dq, d), F32), shaped((dq, n_fs * ff), F32), shaped((ff, d), F32))
        + (shaped((dq,), F32),) * 6
        + (shaped((3 * dq,), F32), shaped((ff,), F32), shaped((n_ctx, n_fs, 128), F32)),
        1,
        (place, *firsts, *seconds),
        "expand",
    )
    qkv_out, out_out, fc1_out, fc2_out, l1g, l1b, l2g, l2b, out_bias_out, fc2_bias_out, qkv_bias_out, fc1_bias_out, _ = (
        grads_out
    )

    x_float = x_msg[:t].astype(F32)
    block_out = turned((x_float + block + both_bias).astype(BF))
    centred = x_float - jnp.mean(x_float, axis=-1, keepdims=True)
    rstd_own = lax.rsqrt(jnp.mean(centred * centred, axis=-1, keepdims=True) + NORM_EPS)
    xhat_own = centred * rstd_own
    dx = rstd_own * (
        u - jnp.mean(u, axis=-1, keepdims=True) - xhat_own * jnp.mean(u * xhat_own, axis=-1, keepdims=True)
    )
    input_grad = turned((cot_msg.astype(F32) + dx).astype(BF))

    return (
        block_out[None],
        input_grad[None],
        l1g,
        l1b,
        qkv_out,
        qkv_bias_out,
        out_out,
        out_bias_out,
        l2g,
        l2b,
        fc1_out,
        fc1_bias_out,
        fc2_out,
        fc2_bias_out,
    )


def solution(mesh):
    token = P("fsdp", "ctx", None)
    placed = (
        token,
        P("fsdp", "ctx"),
        token,
        P("fsdp"),
        P("fsdp"),
        P("fsdp", None),
        P("fsdp"),
        P("fsdp", None),
        P("fsdp"),
        P("fsdp"),
        P("fsdp"),
        P("fsdp", None),
        P("fsdp"),
        P("fsdp", None),
        P("fsdp"),
    )
    return jax.shard_map(
        on_device,
        mesh=mesh,
        in_specs=placed,
        out_specs=(
            token,
            token,
            P("fsdp"),
            P("fsdp"),
            P("fsdp", None),
            P("fsdp"),
            P("fsdp", None),
            P("fsdp"),
            P("fsdp"),
            P("fsdp"),
            P("fsdp", None),
            P("fsdp"),
            P("fsdp", None),
            P("fsdp"),
        ),
        check_vma=False,
    )
```

```python
import functools

import jax
import jax.numpy as jnp
from jax import lax
from jax.experimental import pallas as pl
from jax.experimental.pallas import tpu as pltpu
from jax.sharding import PartitionSpec as P

H = 16
HD = 64
ROT = 16
RUN = 64
RUNS = 64
NORM_EPS = 1e-05
BF = jnp.bfloat16
F32 = jnp.float32
NEG = -1e30

QT = 512
KT = 1024


def mm(a, b):
    return jnp.dot(a, b, preferred_element_type=F32)


def contract_rows(a, b):
    return lax.dot_general(a, b, (((0,), (0,)), ((), ())), preferred_element_type=F32)


def contract_cols(a, b):
    return lax.dot_general(a, b, (((1,), (1,)), ((), ())), preferred_element_type=F32)


def swap_xh(v):
    return lax.ppermute(v, "fsdp", [(i, i ^ 2) for i in range(4)])


def swap_core(v):
    return lax.ppermute(v, "fsdp", [(i, i ^ 1) for i in range(4)])


def attention_kernel(scal, recv, out, kv, qx, yx, dkv, oq, sbuf, dbuf):
    folded = scal[0]
    odd = scal[1]
    lane = lax.broadcasted_iota(jnp.int32, (RUN, 2 * HD), 1)
    low_half = lane < HD
    n_src = recv.shape[0]
    tiles = qx.shape[0]
    per_tile = QT // RUN

    def runs(c):
        turned = jnp.logical_and(folded == 1, c % 2 == 1)
        even = jnp.where(folded == 1, jnp.where(turned, 2 * n_src - 1 - c, c), 2 * c)
        other = jnp.where(folded == 1, jnp.where(turned, c, 2 * n_src - 1 - c), 2 * c + 1)
        return even, other

    def sort_in(c, carry):
        even, other = runs(c)
        kv[pl.ds(pl.multiple_of(even * RUN, RUN), RUN), :] = recv[c, 0:RUN, :]
        kv[pl.ds(pl.multiple_of(other * RUN, RUN), RUN), :] = recv[c, RUN : 2 * RUN, :]
        rank = jnp.where(odd == 1, other, even) // 2
        tile = rank // per_tile
        place = pl.multiple_of((rank % per_tile) * RUN, RUN)
        qd = recv[c, 2 * RUN : 3 * RUN, :]
        zero = jnp.zeros_like(qd)
        q_only = jnp.where(low_half, qd, zero)
        d_only = jnp.where(low_half, zero, qd)
        qx[tile, pl.ds(place, RUN), :] = q_only
        qx[tile, pl.ds(QT + place, RUN), :] = d_only
        yx[tile, pl.ds(place, RUN), :] = d_only
        yx[tile, pl.ds(QT + place, RUN), :] = q_only
        return carry

    lax.fori_loop(0, n_src, sort_in, 0)
    dkv[...] = jnp.zeros_like(dkv)

    row = lax.broadcasted_iota(jnp.int32, (QT, KT), 0)
    col = lax.broadcasted_iota(jnp.int32, (QT, KT), 1)
    row_place = (2 * (row // RUN) + odd) * RUN + row % RUN
    allowed = col <= row_place

    def fold(v, op):
        parts = [v[:, i * 128 : (i + 1) * 128] for i in range(KT // 128)]
        total = parts[0]
        for part in parts[1:]:
            total = op(total, part)
        return total

    def tile_step(j, carry):
        x = qx[j]
        y = yx[j]

        def products(k):
            keys = kv[pl.ds(pl.multiple_of(k * KT, KT), KT), :]
            both = contract_cols(x, keys)
            return both[:QT], both[QT:]

        def pass_one(k, top):
            s, d = products(k)
            sbuf[k] = s
            dbuf[k] = d
            return jnp.maximum(top, fold(s, jnp.maximum))

        top = lax.fori_loop(0, j, pass_one, jnp.full((QT, 128), NEG, F32), unroll=2 if j else 1)
        s, d = products(j)
        s = jnp.where(allowed, s, NEG)
        sbuf[j] = s
        dbuf[j] = d
        top = jnp.maximum(top, fold(s, jnp.maximum))
        top = jnp.max(top, axis=1, keepdims=True)

        def pass_two(k, sums):
            total, weighted = sums
            e = jnp.exp(sbuf[k] - top)
            sbuf[k] = e
            return total + fold(e, jnp.add), weighted + fold(e * dbuf[k], jnp.add)

        zero = jnp.zeros((QT, 128), F32)
        total, weighted = lax.fori_loop(0, j + 1, pass_two, (zero, zero), unroll=2)
        scale = 1.0 / jnp.sum(total, axis=1, keepdims=True)
        delta = jnp.sum(weighted, axis=1, keepdims=True) * scale

        def pass_three(k, acc):
            rows = pl.ds(pl.multiple_of(k * KT, KT), KT)
            p = sbuf[k] * scale
            ds = p * (dbuf[k] - delta)
            a = jnp.concatenate([p.astype(BF), ds.astype(BF)], axis=0)
            dkv[rows, :] += contract_rows(a, y)
            return acc + mm(a, kv[rows, :])

        acc = lax.fori_loop(0, j + 1, pass_three, jnp.zeros((2 * QT, 2 * HD), F32), unroll=2)
        wide = lax.broadcasted_iota(jnp.int32, (QT, 2 * HD), 1) < HD
        oq[pl.ds(j * QT, QT), :] = jnp.where(wide, acc[QT:], acc[:QT]).astype(BF)
        return carry

    for j in range(tiles):
        tile_step(j, 0)

    def sort_out(c, carry):
        even, other = runs(c)
        out[c, 0:RUN, :] = dkv[pl.ds(pl.multiple_of(even * RUN, RUN), RUN), :].astype(BF)
        out[c, RUN : 2 * RUN, :] = dkv[pl.ds(pl.multiple_of(other * RUN, RUN), RUN), :].astype(BF)
        rank = jnp.where(odd == 1, other, even) // 2
        out[c, 2 * RUN : 3 * RUN, :] = oq[pl.ds(pl.multiple_of(rank * RUN, RUN), RUN), :]
        return carry

    lax.fori_loop(0, n_src, sort_out, 0)


def attention(scal, recv):
    n_src = recv.shape[0]
    keys = n_src * 2 * RUN
    queries = n_src * RUN
    tiles = queries // QT
    return pl.pallas_call(
        attention_kernel,
        out_shape=jax.ShapeDtypeStruct(recv.shape, BF),
        in_specs=[pl.BlockSpec(memory_space=pltpu.SMEM), pl.BlockSpec(memory_space=pltpu.VMEM)],
        out_specs=pl.BlockSpec(memory_space=pltpu.VMEM),
        scratch_shapes=[
            pltpu.VMEM((keys, 2 * HD), BF),
            pltpu.VMEM((tiles, 2 * QT, 2 * HD), BF),
            pltpu.VMEM((tiles, 2 * QT, 2 * HD), BF),
            pltpu.VMEM((keys, 2 * HD), F32),
            pltpu.VMEM((queries, 2 * HD), BF),
            pltpu.VMEM((keys // KT, QT, KT), F32),
            pltpu.VMEM((keys // KT, QT, KT), F32),
        ],
        compiler_params=pltpu.CompilerParams(vmem_limit_bytes=60 * 1024 * 1024),
        cost_estimate=pl.CostEstimate(
            flops=14 * HD * queries * keys // 2,
            bytes_accessed=4 * recv.size,
            transcendentals=queries * keys // 2,
        ),
        name="attention",
    )(scal, recv)


def full_spec(v):
    zeros = (0,) * len(v.shape)
    return pl.BlockSpec(v.shape, lambda i: zeros)


def whole_call(body, out_shape, n_smem, args, name, flops=0):
    smem = [pl.BlockSpec(memory_space=pltpu.SMEM)] * n_smem
    return pl.pallas_call(
        body,
        grid=(1,),
        out_shape=out_shape,
        in_specs=smem + [full_spec(v) for v in args[n_smem:]],
        out_specs=jax.tree.map(full_spec, out_shape),
        compiler_params=pltpu.CompilerParams(vmem_limit_bytes=60 * 1024 * 1024),
        cost_estimate=pl.CostEstimate(
            flops=flops,
            bytes_accessed=sum(v.size * v.dtype.itemsize for v in args)
            + sum(v.size * v.dtype.itemsize for v in jax.tree.leaves(out_shape)),
            transcendentals=0,
        ),
        name=name,
    )(*args)


def shaped(shape, dtype):
    return jax.ShapeDtypeStruct(shape, dtype)


def message_kernel(places, x, g, l1g, l1b, l2g, l2b, ob, f2b, qb, x_out, g_out):
    run = places[0] // RUN
    flip = run % 2 == 1
    t, d = x.shape

    @pl.when(flip)
    def _():
        for src, dst in ((x, x_out), (g, g_out)):
            dst[0:RUN, :] = src[RUN:t, :]
            dst[RUN:t, :] = src[0:RUN, :]

    @pl.when(jnp.logical_not(flip))
    def _():
        x_out[0:t, :] = x[...]
        g_out[...] = g[...]

    n = l1g.shape[0]
    both = run + places[RUN] // RUN
    row = lax.broadcasted_iota(jnp.int32, (16, n), 0)
    short = jnp.where(jnp.logical_and(row == 9, both == RUNS - 1), 1.0, 0.0)
    lines = [ref[...].astype(F32).reshape(1, n) for ref in (l1g, l1b, l2g, l2b, ob, f2b)]
    bias = qb[...].astype(F32).reshape(1, 3 * n)
    lines += [bias[:, i * n : (i + 1) * n] for i in range(3)]
    for i, line in enumerate(lines):
        short = jnp.where(row == i, line, short)
    x_out[t:, 0:n] = short.astype(BF)
    x_out[t:, n:] = jnp.zeros((16, d - n), BF)


def columns_kernel(w, out):
    n_fs, _, width = out.shape
    part = width // 3
    for g in range(n_fs):
        for k in range(3):
            out[g, :, k * part : (k + 1) * part] = w[:, (k * n_fs + g) * part : (k * n_fs + g + 1) * part]


def project_kernel(me, x0, x1, x2, x3, g0, g1, g2, g3, w, wo, tables, send, attn_in, mlp_in, xhat, cot, short_out, flags):
    t = g0.shape[0]
    d = g0.shape[1]
    dq = w.shape[1] // 3
    n_fs = d // dq
    blocks = (x0, x1, x2, x3)
    cots = (g0, g1, g2, g3)
    f = me[0]
    shorts = [ref[t : t + 16, :].astype(F32) for ref in blocks]
    owners = [f, f ^ 2, f ^ 1, f ^ 3]
    by_owner = []
    for o in range(n_fs):
        total = shorts[0]
        for r in range(1, n_fs):
            total = jnp.where(owners[r] == o, shorts[r], total)
        by_owner.append(total[:, :dq])
    short = jnp.concatenate(by_owner, axis=1)
    short_out[...] = short
    for r in range(n_fs):
        flags[r] = jnp.broadcast_to(shorts[r][9:10, 0:128], (8, 128))
    gain_one, shift_one, gain_two, shift_two = (short[i : i + 1] for i in range(4))
    biases = []
    for kind in range(3):
        total = jnp.zeros((1, dq), F32)
        for b in range(3 * n_fs):
            o, i = divmod(b, 3)
            total = jnp.where(kind * n_fs + f == b, by_owner[o][6 + i : 7 + i], total)
        biases.append(total)

    for r in range(n_fs):
        rows = slice(r * t, (r + 1) * t)
        v = blocks[r][0:t, :].astype(F32)
        centred = v - jnp.mean(v, axis=1, keepdims=True)
        variance = jnp.mean(centred * centred, axis=1, keepdims=True)
        hat = centred * lax.rsqrt(variance + NORM_EPS)
        xhat[rows, :] = hat
        attn_in[rows, :] = (hat * gain_one + shift_one).astype(BF)
        mlp_in[rows, :] = (hat * gain_two + shift_two).astype(BF)
        cot[rows, :] = cots[r][...]

    a = attn_in[...]
    q_all = mm(a, w[:, :dq]) + biases[0]
    k_all = mm(a, w[:, dq : 2 * dq]) + biases[1]
    v_all = mm(a, w[:, 2 * dq :]) + biases[2]
    dh_all = contract_cols(cot[...], wo[...])
    low = lax.broadcasted_iota(jnp.int32, (t, 2 * HD), 1) < HD
    for r in range(n_fs):
        rows = slice(r * t, (r + 1) * t)
        is_folded = shorts[r][9:10, 0:1] > 0.5
        cos, up, down = (jnp.where(is_folded, tables[3 + i], tables[i]) for i in range(3))

        def turn(v):
            return v * cos + pltpu.roll(v, 2 * HD - ROT // 2, 1) * up + pltpu.roll(v, ROT // 2, 1) * down

        for b in range(dq // (2 * HD)):
            cols = slice(b * 2 * HD, (b + 1) * 2 * HD)
            q = turn(q_all[rows, cols]) * (HD ** (-0.5))
            k = turn(k_all[rows, cols])
            v = v_all[rows, cols]
            dh = dh_all[rows, cols]
            for side in range(2):
                if side == 0:
                    kv = jnp.where(low, k, pltpu.roll(v, HD, 1)).astype(BF)
                    qd = jnp.where(low, q, pltpu.roll(dh, HD, 1)).astype(BF)
                else:
                    kv = jnp.where(low, pltpu.roll(k, HD, 1), v).astype(BF)
                    qd = jnp.where(low, pltpu.roll(q, HD, 1), dh).astype(BF)
                at = r * 8 + (2 * b + side) * 2
                for half in range(2):
                    send[at + half, 0:t, :] = kv
                    send[at + half, t : t + RUN, :] = qd[half * RUN : (half + 1) * RUN]


def finish_kernel(folded, home, tables, attn_in, cot, w, xhat, early, fc1, payload, d_norm, head_out, d_proj):
    t = home.shape[1] - RUN
    dq = head_out.shape[1]
    n_fs = home.shape[0] // 8
    low = lax.broadcasted_iota(jnp.int32, (t, 2 * HD), 1) < HD
    for r in range(n_fs):
        rows = slice(r * t, (r + 1) * t)
        is_folded = folded[r] == 1
        cos, up, down = (jnp.where(is_folded, tables[3 + i], tables[i]) for i in range(3))

        def turn_back(v):
            return v * cos - (pltpu.roll(v, 2 * HD - ROT // 2, 1) * up + pltpu.roll(v, ROT // 2, 1) * down)

        for b in range(dq // (2 * HD)):
            cols = slice(b * 2 * HD, (b + 1) * 2 * HD)
            dkv, qo = [], []
            for side in range(2):
                at = r * 8 + (2 * b + side) * 2
                dkv.append(home[at, 0:t, :].astype(F32) + home[at + 1, 0:t, :].astype(F32))
                qo.append(jnp.concatenate([home[at, t : t + RUN, :], home[at + 1, t : t + RUN, :]], 0).astype(F32))
            d_q = jnp.where(low, qo[0], pltpu.roll(qo[1], HD, 1))
            o = jnp.where(low, pltpu.roll(qo[0], HD, 1), qo[1])
            d_k = jnp.where(low, dkv[0], pltpu.roll(dkv[1], HD, 1))
            d_v = jnp.where(low, pltpu.roll(dkv[0], HD, 1), dkv[1])
            head_out[rows, cols] = o.astype(BF)
            d_proj[rows, cols] = (turn_back(d_q) * (HD ** (-0.5))).astype(BF)
            d_proj[rows, dq + b * 2 * HD : dq + (b + 1) * 2 * HD] = turn_back(d_k).astype(BF)
            d_proj[rows, 2 * dq + b * 2 * HD : 2 * dq + (b + 1) * 2 * HD] = d_v.astype(BF)

    n_ctx, _, rows, _ = payload.shape
    d = attn_in.shape[1]
    width = d_proj.shape[1]
    dp = d_proj[...]
    c = contract_cols(dp, w[...])
    d_norm[...] = c
    gain = jnp.sum(c * xhat[...], axis=0, keepdims=True)
    shift = jnp.sum(c, axis=0, keepdims=True)
    bias = jnp.sum(dp.astype(F32), axis=0, keepdims=True)
    last = width + 128
    payload[:, :, :, width:last] = jnp.zeros((n_ctx, n_fs, rows, 128), BF)
    first = lax.broadcasted_iota(jnp.int32, (rows, 128), 0) == 0

    def put(b, f, v):
        payload[b, f, :, width:last] = jnp.where(first, v, 0.0).astype(BF)

    for f in range(n_fs):
        grad = contract_rows(attn_in[:, f * dq : (f + 1) * dq], dp)
        payload[:, f, :, 0:width] = grad.reshape(n_ctx, rows, width).astype(BF)
        grad = contract_rows(head_out[...], cot[:, f * dq : (f + 1) * dq])
        payload[:, f, :, last : last + dq] = grad.reshape(n_ctx, rows, dq).astype(BF)
        payload[:, f, :, last + dq :] = fc1[f]
        mine = [gain, shift, early[0:1, :], early[1:2, :], early[2:3, :]]
        for i, v in enumerate(mine):
            for half in range(2):
                at = f * dq + half * 128
                put(2 * i + half, f, v[:, at : at + 128])
        for i in range(6):
            put(10 + i, f, bias[:, i * 128 : (i + 1) * 128])
        for i in range(8):
            put(16 + i, f, early[3:4, i * 128 : (i + 1) * 128])


def reduce_kernel(me, got, mine, theirs, out_share):
    n_ctx, n_fs = got.shape[:2]
    dq = out_share.shape[2]
    width = 3 * dq + 128
    for f in range(n_fs):
        total = got[0, f].astype(F32)
        for c in range(1, n_ctx):
            total = total + got[c, f].astype(F32)
        total = total.astype(BF)
        diff = me[0] ^ f

        def put(pieces, at, total=total):
            pieces[at, :, 0:width] = total[:, 0:width]
            pieces[at, :, width:] = total[:, width + dq :]

        pl.when(diff % 2 == 0)(functools.partial(put, mine, diff // 2))
        pl.when(diff % 2 == 1)(functools.partial(put, theirs, diff // 2))
        out_share[f] = total[:, width : width + dq]


def arrange_kernel(me, keep, a, b, c, extra, extra_xl, first, second):
    dq = 256
    width = 3 * dq + 128
    for e, sources, more in (
        (0, (keep[0], keep[1], a[0], a[1]), extra),
        (1, (b[0], b[1], c[0], c[1]), extra_xl),
    ):
        sources = [v.astype(F32) for v in sources]
        lines = []
        for o in range(4):
            total = sources[0]
            for k in range(1, 4):
                total = jnp.where((me[0] ^ k) == o, sources[k], total)
            lines.append(total)
        owned = jnp.concatenate(lines, 0)
        more = more[...].astype(F32)
        at = width + dq
        first[e, :, 0:width] = owned[:, 0:width].astype(BF)
        first[e, :, width:at] = more[:, 0:dq].astype(BF)
        first[e, :, at:] = more[:, dq : dq + 512].astype(BF)
        second[e, :, 0 : 4 * dq] = owned[:, width:].astype(BF)
        second[e, :, 4 * dq :] = more[:, dq + 512 :].astype(BF)


def expand_kernel(place, *refs):
    firsts, seconds = refs[:4], refs[4:8]
    qkv, out, up, down, l1g, l1b, l2g, l2b, common, common_again, qb, f1b, lines = refs[8:]
    n_ctx = lines.shape[0]
    dq = out.shape[0]
    ff = down.shape[1]
    rows = dq // n_ctx
    me, xl, z, y = (place[i] for i in range(4))
    width = 3 * dq + 128 + dq
    for p in range(4):
        for b in range(4):
            for e in range(2):
                c = (xl ^ e) * 16 + ((z - p) % 4) * 4 + (y - b) % 4
                at = pl.ds(pl.multiple_of(c * rows, rows), rows)
                v = firsts[p][b * 2 + e].astype(F32)
                for f in range(4):
                    part = v[f * rows : (f + 1) * rows]
                    for kind in range(3):
                        qkv[at, (kind * 4 + f) * dq : (kind * 4 + f + 1) * dq] = part[:, kind * dq : (kind + 1) * dq]
                    lines[c, f : f + 1, :] = part[0:1, 3 * dq : 3 * dq + 128]
                    out[at, f * dq : (f + 1) * dq] = part[:, 3 * dq + 128 : width]
                half = 2 * rows
                low = pl.ds(pl.multiple_of(c * 4 * rows, 4 * rows), half)
                for i in range(2):
                    down[low, i * 512 : (i + 1) * 512] = v[i * half : (i + 1) * half, width:]
                c = (xl ^ e) * 16 + ((z - b) % 4) * 4 + (y - p) % 4
                at = pl.ds(pl.multiple_of(c * rows, rows), rows)
                v = seconds[p][b * 2 + e].astype(F32)
                for f in range(4):
                    up[at, f * ff : (f + 1) * ff] = v[f * rows : (f + 1) * rows, 0:ff]
                high = pl.ds(pl.multiple_of(c * 4 * rows + half, half), half)
                for i in range(2):
                    down[high, i * 512 : (i + 1) * 512] = v[i * half : (i + 1) * half, ff:]

    def line(b, f):
        return lines[b, pl.ds(f, 1), :]

    for i, ref in enumerate((l1g, l1b, l2g, l2b)):
        for half in range(2):
            total = line(2 * i + half, 0)
            for f in range(1, 4):
                total = total + line(2 * i + half, f)
            ref[half * 128 : (half + 1) * 128] = total.reshape(128)
    for half in range(2):
        v = line(8 + half, me).reshape(128)
        common[half * 128 : (half + 1) * 128] = v
        common_again[half * 128 : (half + 1) * 128] = v
    for i in range(3):
        b = 3 * me + i
        for half in range(2):
            at = (2 * i + half) * 128
            qb[at : at + 128] = line(10 + 2 * (b // 4) + half, b % 4).reshape(128)
    for i in range(8):
        f1b[i * 128 : (i + 1) * 128] = line(16 + i, me).reshape(128)


def pick(stacked, index):
    return lax.dynamic_index_in_dim(stacked, index, 0, keepdims=False)


def on_device(
    hidden_in,
    positions,
    out_grad,
    ln1_gain,
    ln1_bias,
    qkv_weight,
    qkv_bias,
    out_weight,
    out_bias,
    ln2_gain,
    ln2_bias,
    fc1_weight,
    fc1_bias,
    fc2_weight,
    fc2_bias,
):
    n_fs = 4
    n_ctx = 32
    ctx = lax.axis_index("ctx")
    me = lax.axis_index("fsdp")
    t = hidden_in.shape[1]
    d = hidden_in.shape[2]
    dq = d // n_fs
    ff = fc1_weight.shape[1] // n_fs
    tok = n_fs * t
    rows = dq // n_ctx
    me_one = me.astype(jnp.int32).reshape(1)

    flip = (positions[0, 0] // RUN) % 2 == 1

    def turned(v):
        return jnp.where(flip, jnp.concatenate([v[RUN:], v[:RUN]], 0), v)

    x_msg, cot_msg = whole_call(
        message_kernel,
        (shaped((t + 16, d), BF), shaped((t, d), BF)),
        1,
        (positions[0], hidden_in[0], out_grad[0], ln1_gain, ln1_bias, ln2_gain, ln2_bias, out_bias, fc2_bias, qkv_bias),
        "message",
    )
    x_xh = swap_xh(x_msg)
    cot_xh = swap_xh(cot_msg)
    x_all = [x_msg, x_xh, swap_core(x_msg), swap_core(x_xh)]
    cot_all = [cot_msg, cot_xh, swap_core(cot_msg), swap_core(cot_xh)]

    (qkv_columns,) = whole_call(columns_kernel, (shaped((n_fs, dq, 3 * dq), BF),), 0, (qkv_weight,), "columns")
    w_qkv = lax.all_to_all(qkv_columns, "fsdp", 0, 0).reshape(d, 3 * dq)

    def up_columns(diff):
        return lax.dynamic_slice(fc1_weight, (0, (me ^ diff) * ff), (dq, ff))

    def cross(v, diff):
        return lax.ppermute(v, ("ctx", "fsdp"), [(i, i ^ (16 * n_fs + diff)) for i in range(n_ctx * n_fs)])

    up_parts = lax.optimization_barrier((w_qkv,) + tuple(up_columns(i) for i in range(4)))
    w_qkv = up_parts[0]
    up_rel = [up_parts[1], cross(up_parts[3], 2), swap_core(up_parts[2]), cross(up_parts[4], 3)]

    def rel_of(owner):
        diff = jnp.bitwise_xor(me, owner)
        return (diff % 2) * 2 + diff // 2

    half = ROT // 2
    lane = jnp.arange(2 * HD) % HD
    turning = lane < ROT
    frequency = jnp.where(turning, 10000.0 ** (-2.0 * (lane % half).astype(F32) / ROT), 0.0)
    back = ctx % 2 == 1
    tables = []
    for even_run, odd_run in (
        (2 * ctx, 2 * ctx + 1),
        (jnp.where(back, 2 * n_ctx - 1 - ctx, ctx), jnp.where(back, ctx, 2 * n_ctx - 1 - ctx)),
    ):
        places = jnp.concatenate([even_run * RUN + jnp.arange(RUN), odd_run * RUN + jnp.arange(RUN)])
        phases = places.astype(F32)[:, None] * frequency[None, :]
        sines = jnp.sin(phases)
        tables += [jnp.cos(phases), jnp.where(lane < half, -sines, 0.0), jnp.where((lane >= half) & turning, sines, 0.0)]
    tables = jnp.stack(tables)

    send, attn_in, mlp_in, xhat, cot, short_all, flags = whole_call(
        project_kernel,
        (
            shaped((n_ctx, t + RUN, 2 * HD), BF),
            shaped((tok, d), BF),
            shaped((tok, d), BF),
            shaped((tok, d), F32),
            shaped((tok, d), BF),
            shaped((16, d), F32),
            shaped((n_fs, 8, 128), F32),
        ),
        1,
        (me_one, *x_all, *cot_all, w_qkv, out_weight, tables),
        "project",
        flops=2 * tok * d * 4 * dq,
    )
    gain_one, gain_two = short_all[0:1], short_all[2:3]
    both_bias = short_all[4:5] + short_all[5:6]
    folded = (flags[:, 0, 0] > 0.5).astype(jnp.int32)

    my_folded = pick(folded, ctx // 8)
    scal = jnp.stack([my_folded, ctx % 2]).astype(jnp.int32)
    up_rel = jnp.stack(up_rel)
    w_up = jnp.concatenate([pick(up_rel, rel_of(o)) for o in range(n_fs)], 0)
    recv = lax.all_to_all(send, "ctx", 0, 0)

    pre_act = mm(mlp_in, w_up) + fc1_bias.astype(F32)[None]
    act_float, pull_act = jax.vjp(lambda v: jax.nn.gelu(v, approximate=False), pre_act)
    activated = act_float.astype(BF)
    d_pre = pull_act(contract_cols(cot, fc2_weight))[0].astype(BF)
    fc2_grad = contract_rows(activated, cot).astype(BF)
    fc1_grad = contract_rows(mlp_in, d_pre).astype(BF)
    xl, z, y = ctx // 16, (ctx // 4) % 4, ctx % 4
    spot = {"xl": xl, "z": z, "y": y}

    def shift(v, axis, by):
        size, stride = {"y": (4, 1), "z": (4, 4), "xl": (2, 16)}[axis]
        perm = []
        for i in range(n_ctx):
            p = (i // stride) % size
            perm.append((i, i + ((p + by) % size - p) * stride))
        return lax.ppermute(v, "ctx", perm)

    recv, fc2_grad, scal = lax.optimization_barrier((recv, fc2_grad, scal))
    down_got = lax.all_to_all(fc2_grad.reshape(n_ctx, ff // n_ctx, d), "ctx", 0, 0)

    grads = attention(scal, recv)
    grads, down_got = lax.optimization_barrier((grads, down_got))
    home = lax.all_to_all(grads, "ctx", 0, 0)
    down_share = jnp.sum(down_got.astype(F32), 0).astype(BF)

    mlp_part = mm(activated, fc2_weight)
    d_norm_two = contract_cols(d_pre, w_up)
    early = jnp.stack(
        [
            jnp.sum(d_norm_two * xhat, 0),
            jnp.sum(d_norm_two, 0),
            jnp.sum(cot.astype(F32), 0),
            jnp.sum(d_pre, 0, dtype=F32),
        ]
    )
    early, down_share = lax.optimization_barrier((early, down_share))

    payload, d_norm_one, head_out, _ = whole_call(
        finish_kernel,
        (
            shaped((n_ctx, n_fs, rows, 4 * dq + 128 + ff), BF),
            shaped((tok, d), F32),
            shaped((tok, dq), BF),
            shaped((tok, 3 * dq), BF),
        ),
        1,
        (folded, home, tables, attn_in, cot, w_qkv, xhat, early, fc1_grad.reshape(n_fs, n_ctx, rows, ff)),
        "finish",
        flops=2 * tok * d * 7 * dq,
    )
    got = lax.all_to_all(payload, "ctx", 0, 0)

    def scatter_fsdp(parts):
        parts = parts.reshape(2, 2, t, d)
        here = parts[0] + swap_core(parts[1].astype(BF)).astype(F32)
        return here[0] + swap_xh(here[1].astype(BF)).astype(F32)

    block = scatter_fsdp(mlp_part + mm(head_out, out_weight))

    u = scatter_fsdp(d_norm_one * gain_one + d_norm_two * gain_two)
    width = 3 * dq + 128
    mine, theirs, out_share = whole_call(
        reduce_kernel,
        (shaped((2, rows, width + ff), BF), shaped((2, rows, width + ff), BF), shaped((n_fs, rows, dq), BF)),
        1,
        (me_one, got),
        "reduce",
    )
    from_core = swap_core(theirs)
    keep = jnp.stack([mine[0], from_core[0]])
    away = jnp.stack([mine[1], from_core[1]])
    down_halves = down_share.reshape(2, 2 * rows, 2, d // 2).transpose(0, 2, 1, 3).reshape(2, 4 * rows, d // 2)
    extra = jnp.concatenate([out_share.reshape(n_fs * rows, dq), down_halves[0], down_halves[1]], 1)
    first, second = whole_call(
        arrange_kernel,
        (shaped((2, n_fs * rows, width + dq + d // 2), BF), shaped((2, n_fs * rows, ff + d // 2), BF)),
        1,
        (
            me_one,
            keep,
            swap_xh(away),
            shift(keep, "xl", 1),
            cross(away, 2),
            extra,
            shift(extra, "xl", 1),
        ),
        "arrange",
    )

    def joined(parts):
        v = jnp.concatenate([p[None] for p in parts], 0)
        return v.reshape((-1,) + v.shape[2:])

    def around(v, axis):
        return [v] + [shift(v, axis, s) for s in range(1, 4)]

    first, second, block, u = lax.optimization_barrier((first, second, block, u))
    near = (around(first, "y"), around(second, "z"))
    near = lax.optimization_barrier(near)
    firsts = around(joined(near[0]), "z")
    seconds = around(joined(near[1]), "y")

    place = jnp.stack([me, xl, z, y]).astype(jnp.int32)
    grads_out = whole_call(
        expand_kernel,
        (shaped((dq, 3 * d), F32), shaped((dq, d), F32), shaped((dq, n_fs * ff), F32), shaped((ff, d), F32))
        + (shaped((dq,), F32),) * 6
        + (shaped((3 * dq,), F32), shaped((ff,), F32), shaped((n_ctx, n_fs, 128), F32)),
        1,
        (place, *firsts, *seconds),
        "expand",
    )
    qkv_out, out_out, fc1_out, fc2_out, l1g, l1b, l2g, l2b, out_bias_out, fc2_bias_out, qkv_bias_out, fc1_bias_out, _ = (
        grads_out
    )

    x_float = x_msg[:t].astype(F32)
    block_out = turned((x_float + block + both_bias).astype(BF))
    centred = x_float - jnp.mean(x_float, axis=-1, keepdims=True)
    rstd_own = lax.rsqrt(jnp.mean(centred * centred, axis=-1, keepdims=True) + NORM_EPS)
    xhat_own = centred * rstd_own
    dx = rstd_own * (
        u - jnp.mean(u, axis=-1, keepdims=True) - xhat_own * jnp.mean(u * xhat_own, axis=-1, keepdims=True)
    )
    input_grad = turned((cot_msg.astype(F32) + dx).astype(BF))

    return (
        block_out[None],
        input_grad[None],
        l1g,
        l1b,
        qkv_out,
        qkv_bias_out,
        out_out,
        out_bias_out,
        l2g,
        l2b,
        fc1_out,
        fc1_bias_out,
        fc2_out,
        fc2_bias_out,
    )


def solution(mesh):
    token = P("fsdp", "ctx", None)
    placed = (
        token,
        P("fsdp", "ctx"),
        token,
        P("fsdp"),
        P("fsdp"),
        P("fsdp", None),
        P("fsdp"),
        P("fsdp", None),
        P("fsdp"),
        P("fsdp"),
        P("fsdp"),
        P("fsdp", None),
        P("fsdp"),
        P("fsdp", None),
        P("fsdp"),
    )
    return jax.shard_map(
        on_device,
        mesh=mesh,
        in_specs=placed,
        out_specs=(
            token,
            token,
            P("fsdp"),
            P("fsdp"),
            P("fsdp", None),
            P("fsdp"),
            P("fsdp", None),
            P("fsdp"),
            P("fsdp"),
            P("fsdp"),
            P("fsdp", None),
            P("fsdp"),
            P("fsdp", None),
            P("fsdp"),
        ),
        check_vma=False,
    )
```

```python
import functools

import jax
import jax.numpy as jnp
from jax import lax
from jax.experimental import pallas as pl
from jax.experimental.pallas import tpu as pltpu
from jax.sharding import PartitionSpec as P

H = 16
HD = 64
ROT = 16
RUN = 64
RUNS = 64
NORM_EPS = 1e-05
BF = jnp.bfloat16
F32 = jnp.float32
NEG = -1e30

QT = 512
KT = 1024


def mm(a, b):
    return jnp.dot(a, b, preferred_element_type=F32)


def contract_rows(a, b):
    return lax.dot_general(a, b, (((0,), (0,)), ((), ())), preferred_element_type=F32)


def contract_cols(a, b):
    return lax.dot_general(a, b, (((1,), (1,)), ((), ())), preferred_element_type=F32)


def swap_xh(v):
    return lax.ppermute(v, "fsdp", [(i, i ^ 2) for i in range(4)])


def swap_core(v):
    return lax.ppermute(v, "fsdp", [(i, i ^ 1) for i in range(4)])


def attention_kernel(scal, recv, out, kv, qx, yx, dkv, oq, sbuf, dbuf):
    folded = scal[0]
    odd = scal[1]
    lane = lax.broadcasted_iota(jnp.int32, (RUN, 2 * HD), 1)
    low_half = lane < HD
    n_src = recv.shape[0]
    tiles = qx.shape[0]
    per_tile = QT // RUN

    def runs(c):
        turned = jnp.logical_and(folded == 1, c % 2 == 1)
        even = jnp.where(folded == 1, jnp.where(turned, 2 * n_src - 1 - c, c), 2 * c)
        other = jnp.where(folded == 1, jnp.where(turned, c, 2 * n_src - 1 - c), 2 * c + 1)
        return even, other

    def sort_in(c, carry):
        even, other = runs(c)
        kv[pl.ds(pl.multiple_of(even * RUN, RUN), RUN), :] = recv[c, 0:RUN, :]
        kv[pl.ds(pl.multiple_of(other * RUN, RUN), RUN), :] = recv[c, RUN : 2 * RUN, :]
        rank = jnp.where(odd == 1, other, even) // 2
        tile = rank // per_tile
        place = pl.multiple_of((rank % per_tile) * RUN, RUN)
        qd = recv[c, 2 * RUN : 3 * RUN, :]
        zero = jnp.zeros_like(qd)
        q_only = jnp.where(low_half, qd, zero)
        d_only = jnp.where(low_half, zero, qd)
        qx[tile, pl.ds(place, RUN), :] = q_only
        qx[tile, pl.ds(QT + place, RUN), :] = d_only
        yx[tile, pl.ds(place, RUN), :] = d_only
        yx[tile, pl.ds(QT + place, RUN), :] = q_only
        return carry

    lax.fori_loop(0, n_src, sort_in, 0)
    dkv[...] = jnp.zeros_like(dkv)

    row = lax.broadcasted_iota(jnp.int32, (QT, KT), 0)
    col = lax.broadcasted_iota(jnp.int32, (QT, KT), 1)
    row_place = (2 * (row // RUN) + odd) * RUN + row % RUN
    allowed = col <= row_place

    def fold(v, op):
        parts = [v[:, i * 128 : (i + 1) * 128] for i in range(KT // 128)]
        total = parts[0]
        for part in parts[1:]:
            total = op(total, part)
        return total

    def tile_step(j, carry):
        x = qx[j]
        y = yx[j]

        def products(k):
            keys = kv[pl.ds(pl.multiple_of(k * KT, KT), KT), :]
            both = contract_cols(x, keys)
            return both[:QT], both[QT:]

        def pass_one(k, top):
            s, d = products(k)
            sbuf[k] = s
            dbuf[k] = d
            return jnp.maximum(top, fold(s, jnp.maximum))

        top = lax.fori_loop(0, j, pass_one, jnp.full((QT, 128), NEG, F32), unroll=2 if j else 1)
        s, d = products(j)
        s = jnp.where(allowed, s, NEG)
        sbuf[j] = s
        dbuf[j] = d
        top = jnp.maximum(top, fold(s, jnp.maximum))
        top = jnp.max(top, axis=1, keepdims=True)

        def pass_two(k, sums):
            total, weighted = sums
            e = jnp.exp(sbuf[k] - top)
            sbuf[k] = e
            return total + fold(e, jnp.add), weighted + fold(e * dbuf[k], jnp.add)

        zero = jnp.zeros((QT, 128), F32)
        total, weighted = lax.fori_loop(0, j + 1, pass_two, (zero, zero), unroll=2)
        scale = 1.0 / jnp.sum(total, axis=1, keepdims=True)
        delta = jnp.sum(weighted, axis=1, keepdims=True) * scale

        def pass_three(k, acc):
            rows = pl.ds(pl.multiple_of(k * KT, KT), KT)
            p = sbuf[k] * scale
            ds = p * (dbuf[k] - delta)
            a = jnp.concatenate([p.astype(BF), ds.astype(BF)], axis=0)
            dkv[rows, :] += contract_rows(a, y)
            return acc + mm(a, kv[rows, :])

        acc = lax.fori_loop(0, j + 1, pass_three, jnp.zeros((2 * QT, 2 * HD), F32), unroll=2)
        wide = lax.broadcasted_iota(jnp.int32, (QT, 2 * HD), 1) < HD
        oq[pl.ds(j * QT, QT), :] = jnp.where(wide, acc[QT:], acc[:QT]).astype(BF)
        return carry

    for j in range(tiles):
        tile_step(j, 0)

    def sort_out(c, carry):
        even, other = runs(c)
        out[c, 0:RUN, :] = dkv[pl.ds(pl.multiple_of(even * RUN, RUN), RUN), :].astype(BF)
        out[c, RUN : 2 * RUN, :] = dkv[pl.ds(pl.multiple_of(other * RUN, RUN), RUN), :].astype(BF)
        rank = jnp.where(odd == 1, other, even) // 2
        out[c, 2 * RUN : 3 * RUN, :] = oq[pl.ds(pl.multiple_of(rank * RUN, RUN), RUN), :]
        return carry

    lax.fori_loop(0, n_src, sort_out, 0)


def attention(scal, recv):
    n_src = recv.shape[0]
    keys = n_src * 2 * RUN
    queries = n_src * RUN
    tiles = queries // QT
    return pl.pallas_call(
        attention_kernel,
        out_shape=jax.ShapeDtypeStruct(recv.shape, BF),
        in_specs=[pl.BlockSpec(memory_space=pltpu.SMEM), pl.BlockSpec(memory_space=pltpu.VMEM)],
        out_specs=pl.BlockSpec(memory_space=pltpu.VMEM),
        scratch_shapes=[
            pltpu.VMEM((keys, 2 * HD), BF),
            pltpu.VMEM((tiles, 2 * QT, 2 * HD), BF),
            pltpu.VMEM((tiles, 2 * QT, 2 * HD), BF),
            pltpu.VMEM((keys, 2 * HD), F32),
            pltpu.VMEM((queries, 2 * HD), BF),
            pltpu.VMEM((keys // KT, QT, KT), F32),
            pltpu.VMEM((keys // KT, QT, KT), F32),
        ],
        compiler_params=pltpu.CompilerParams(vmem_limit_bytes=60 * 1024 * 1024),
        cost_estimate=pl.CostEstimate(
            flops=14 * HD * queries * keys // 2,
            bytes_accessed=4 * recv.size,
            transcendentals=queries * keys // 2,
        ),
        name="attention",
    )(scal, recv)


def full_spec(v):
    zeros = (0,) * len(v.shape)
    return pl.BlockSpec(v.shape, lambda i: zeros)


def whole_call(body, out_shape, n_smem, args, name, flops=0):
    smem = [pl.BlockSpec(memory_space=pltpu.SMEM)] * n_smem
    return pl.pallas_call(
        body,
        grid=(1,),
        out_shape=out_shape,
        in_specs=smem + [full_spec(v) for v in args[n_smem:]],
        out_specs=jax.tree.map(full_spec, out_shape),
        compiler_params=pltpu.CompilerParams(vmem_limit_bytes=60 * 1024 * 1024),
        cost_estimate=pl.CostEstimate(
            flops=flops,
            bytes_accessed=sum(v.size * v.dtype.itemsize for v in args)
            + sum(v.size * v.dtype.itemsize for v in jax.tree.leaves(out_shape)),
            transcendentals=0,
        ),
        name=name,
    )(*args)


def shaped(shape, dtype):
    return jax.ShapeDtypeStruct(shape, dtype)


def message_kernel(places, x, g, l1g, l1b, l2g, l2b, ob, f2b, qb, x_out, g_out):
    run = places[0] // RUN
    flip = run % 2 == 1
    t, d = x.shape

    @pl.when(flip)
    def _():
        for src, dst in ((x, x_out), (g, g_out)):
            dst[0:RUN, :] = src[RUN:t, :]
            dst[RUN:t, :] = src[0:RUN, :]

    @pl.when(jnp.logical_not(flip))
    def _():
        x_out[0:t, :] = x[...]
        g_out[...] = g[...]

    n = l1g.shape[0]
    both = run + places[RUN] // RUN
    row = lax.broadcasted_iota(jnp.int32, (16, n), 0)
    short = jnp.where(jnp.logical_and(row == 9, both == RUNS - 1), 1.0, 0.0)
    lines = [ref[...].astype(F32).reshape(1, n) for ref in (l1g, l1b, l2g, l2b, ob, f2b)]
    bias = qb[...].astype(F32).reshape(1, 3 * n)
    lines += [bias[:, i * n : (i + 1) * n] for i in range(3)]
    for i, line in enumerate(lines):
        short = jnp.where(row == i, line, short)
    x_out[t:, 0:n] = short.astype(BF)
    x_out[t:, n:] = jnp.zeros((16, d - n), BF)


def columns_kernel(w, out):
    n_fs, _, width = out.shape
    part = width // 3
    for g in range(n_fs):
        for k in range(3):
            out[g, :, k * part : (k + 1) * part] = w[:, (k * n_fs + g) * part : (k * n_fs + g + 1) * part]


def prepare_kernel(me, x0, x1, x2, x3, g0, g1, g2, g3, wo, attn_in, mlp_in, xhat, cot, short_out, flags, dh, bias):
    t = g0.shape[0]
    d = g0.shape[1]
    dq = wo.shape[0]
    n_fs = d // dq
    blocks = (x0, x1, x2, x3)
    cots = (g0, g1, g2, g3)
    f = me[0]
    shorts = [ref[t : t + 16, :].astype(F32) for ref in blocks]
    owners = [f, f ^ 2, f ^ 1, f ^ 3]
    by_owner = []
    for o in range(n_fs):
        total = shorts[0]
        for r in range(1, n_fs):
            total = jnp.where(owners[r] == o, shorts[r], total)
        by_owner.append(total[:, :dq])
    short = jnp.concatenate(by_owner, axis=1)
    short_out[...] = short
    for r in range(n_fs):
        flags[r] = jnp.broadcast_to(shorts[r][9:10, 0:128], (8, 128))
    gain_one, shift_one, gain_two, shift_two = (short[i : i + 1] for i in range(4))
    bias[...] = jnp.zeros((8, dq), F32)
    for kind in range(3):
        total = jnp.zeros((1, dq), F32)
        for b in range(3 * n_fs):
            o, i = divmod(b, 3)
            total = jnp.where(kind * n_fs + f == b, by_owner[o][6 + i : 7 + i], total)
        bias[kind : kind + 1, :] = total

    for r in range(n_fs):
        rows = slice(r * t, (r + 1) * t)
        v = blocks[r][0:t, :].astype(F32)
        centred = v - jnp.mean(v, axis=1, keepdims=True)
        variance = jnp.mean(centred * centred, axis=1, keepdims=True)
        hat = centred * lax.rsqrt(variance + NORM_EPS)
        xhat[rows, :] = hat
        attn_in[rows, :] = (hat * gain_one + shift_one).astype(BF)
        mlp_in[rows, :] = (hat * gain_two + shift_two).astype(BF)
        cot[rows, :] = cots[r][...]

    dh[...] = contract_cols(cot[...], wo[...])


def project_kernel(attn_in, w, dh, bias, flags, tables, send):
    n_fs = flags.shape[0]
    t = attn_in.shape[0] // n_fs
    dq = dh.shape[1]
    a = attn_in[...]
    q_all = mm(a, w[:, :dq]) + bias[0:1, :]
    k_all = mm(a, w[:, dq : 2 * dq]) + bias[1:2, :]
    v_all = mm(a, w[:, 2 * dq :]) + bias[2:3, :]
    dh_all = dh[...]
    low = lax.broadcasted_iota(jnp.int32, (t, 2 * HD), 1) < HD
    for r in range(n_fs):
        rows = slice(r * t, (r + 1) * t)
        is_folded = flags[r][0:1, 0:1] > 0.5
        cos, up, down = (jnp.where(is_folded, tables[3 + i], tables[i]) for i in range(3))

        def turn(v):
            return v * cos + pltpu.roll(v, 2 * HD - ROT // 2, 1) * up + pltpu.roll(v, ROT // 2, 1) * down

        for b in range(dq // (2 * HD)):
            cols = slice(b * 2 * HD, (b + 1) * 2 * HD)
            q = turn(q_all[rows, cols]) * (HD ** (-0.5))
            k = turn(k_all[rows, cols])
            v = v_all[rows, cols]
            dh = dh_all[rows, cols]
            for side in range(2):
                if side == 0:
                    kv = jnp.where(low, k, pltpu.roll(v, HD, 1)).astype(BF)
                    qd = jnp.where(low, q, pltpu.roll(dh, HD, 1)).astype(BF)
                else:
                    kv = jnp.where(low, pltpu.roll(k, HD, 1), v).astype(BF)
                    qd = jnp.where(low, pltpu.roll(q, HD, 1), dh).astype(BF)
                at = r * 8 + (2 * b + side) * 2
                for half in range(2):
                    send[at + half, 0:t, :] = kv
                    send[at + half, t : t + RUN, :] = qd[half * RUN : (half + 1) * RUN]


def finish_kernel(folded, home, tables, attn_in, cot, w, xhat, early, fc1, payload, d_norm, head_out, d_proj):
    t = home.shape[1] - RUN
    dq = head_out.shape[1]
    n_fs = home.shape[0] // 8
    low = lax.broadcasted_iota(jnp.int32, (t, 2 * HD), 1) < HD
    for r in range(n_fs):
        rows = slice(r * t, (r + 1) * t)
        is_folded = folded[r] == 1
        cos, up, down = (jnp.where(is_folded, tables[3 + i], tables[i]) for i in range(3))

        def turn_back(v):
            return v * cos - (pltpu.roll(v, 2 * HD - ROT // 2, 1) * up + pltpu.roll(v, ROT // 2, 1) * down)

        for b in range(dq // (2 * HD)):
            cols = slice(b * 2 * HD, (b + 1) * 2 * HD)
            dkv, qo = [], []
            for side in range(2):
                at = r * 8 + (2 * b + side) * 2
                dkv.append(home[at, 0:t, :].astype(F32) + home[at + 1, 0:t, :].astype(F32))
                qo.append(jnp.concatenate([home[at, t : t + RUN, :], home[at + 1, t : t + RUN, :]], 0).astype(F32))
            d_q = jnp.where(low, qo[0], pltpu.roll(qo[1], HD, 1))
            o = jnp.where(low, pltpu.roll(qo[0], HD, 1), qo[1])
            d_k = jnp.where(low, dkv[0], pltpu.roll(dkv[1], HD, 1))
            d_v = jnp.where(low, pltpu.roll(dkv[0], HD, 1), dkv[1])
            head_out[rows, cols] = o.astype(BF)
            d_proj[rows, cols] = (turn_back(d_q) * (HD ** (-0.5))).astype(BF)
            d_proj[rows, dq + b * 2 * HD : dq + (b + 1) * 2 * HD] = turn_back(d_k).astype(BF)
            d_proj[rows, 2 * dq + b * 2 * HD : 2 * dq + (b + 1) * 2 * HD] = d_v.astype(BF)

    n_ctx, _, rows, _ = payload.shape
    d = attn_in.shape[1]
    width = d_proj.shape[1]
    dp = d_proj[...]
    c = contract_cols(dp, w[...])
    d_norm[...] = c
    gain = jnp.sum(c * xhat[...], axis=0, keepdims=True)
    shift = jnp.sum(c, axis=0, keepdims=True)
    bias = jnp.sum(dp.astype(F32), axis=0, keepdims=True)
    last = width + 128
    payload[:, :, :, width:last] = jnp.zeros((n_ctx, n_fs, rows, 128), BF)
    first = lax.broadcasted_iota(jnp.int32, (rows, 128), 0) == 0

    def put(b, f, v):
        payload[b, f, :, width:last] = jnp.where(first, v, 0.0).astype(BF)

    for f in range(n_fs):
        grad = contract_rows(attn_in[:, f * dq : (f + 1) * dq], dp)
        payload[:, f, :, 0:width] = grad.reshape(n_ctx, rows, width).astype(BF)
        grad = contract_rows(head_out[...], cot[:, f * dq : (f + 1) * dq])
        payload[:, f, :, last : last + dq] = grad.reshape(n_ctx, rows, dq).astype(BF)
        payload[:, f, :, last + dq :] = fc1[f]
        mine = [gain, shift, early[0:1, :], early[1:2, :], early[2:3, :]]
        for i, v in enumerate(mine):
            for half in range(2):
                at = f * dq + half * 128
                put(2 * i + half, f, v[:, at : at + 128])
        for i in range(6):
            put(10 + i, f, bias[:, i * 128 : (i + 1) * 128])
        for i in range(8):
            put(16 + i, f, early[3:4, i * 128 : (i + 1) * 128])


def reduce_kernel(me, got, mine, theirs, out_share):
    n_ctx, n_fs = got.shape[:2]
    dq = out_share.shape[2]
    width = 3 * dq + 128
    for f in range(n_fs):
        total = got[0, f].astype(F32)
        for c in range(1, n_ctx):
            total = total + got[c, f].astype(F32)
        total = total.astype(BF)
        diff = me[0] ^ f

        def put(pieces, at, total=total):
            pieces[at, :, 0:width] = total[:, 0:width]
            pieces[at, :, width:] = total[:, width + dq :]

        pl.when(diff % 2 == 0)(functools.partial(put, mine, diff // 2))
        pl.when(diff % 2 == 1)(functools.partial(put, theirs, diff // 2))
        out_share[f] = total[:, width : width + dq]


def arrange_kernel(me, keep, a, b, c, extra, extra_xl, first, second):
    dq = 256
    width = 3 * dq + 128
    for e, sources, more in (
        (0, (keep[0], keep[1], a[0], a[1]), extra),
        (1, (b[0], b[1], c[0], c[1]), extra_xl),
    ):
        sources = [v.astype(F32) for v in sources]
        lines = []
        for o in range(4):
            total = sources[0]
            for k in range(1, 4):
                total = jnp.where((me[0] ^ k) == o, sources[k], total)
            lines.append(total)
        owned = jnp.concatenate(lines, 0)
        more = more[...].astype(F32)
        at = width + dq
        first[e, :, 0:width] = owned[:, 0:width].astype(BF)
        first[e, :, width:at] = more[:, 0:dq].astype(BF)
        first[e, :, at:] = more[:, dq : dq + 512].astype(BF)
        second[e, :, 0 : 4 * dq] = owned[:, width:].astype(BF)
        second[e, :, 4 * dq :] = more[:, dq + 512 :].astype(BF)


def expand_kernel(place, *refs):
    firsts, seconds = refs[:5], refs[5:10]
    qkv, out, up, down, l1g, l1b, l2g, l2b, common, common_again, qb, f1b, lines = refs[10:]

    def block(parts, p, i):
        if p == 2:
            return parts[2][i] if i < 4 else parts[3][i - 4]
        return parts[(0, 1, 2, 4)[p]][i]

    n_ctx = lines.shape[0]
    dq = out.shape[0]
    ff = down.shape[1]
    rows = dq // n_ctx
    me, xl, z, y = (place[i] for i in range(4))
    width = 3 * dq + 128 + dq
    for p in range(4):
        for b in range(4):
            for e in range(2):
                c = (xl ^ e) * 16 + ((z - p) % 4) * 4 + (y - b) % 4
                at = pl.ds(pl.multiple_of(c * rows, rows), rows)
                v = block(firsts, p, b * 2 + e).astype(F32)
                for f in range(4):
                    part = v[f * rows : (f + 1) * rows]
                    for kind in range(3):
                        qkv[at, (kind * 4 + f) * dq : (kind * 4 + f + 1) * dq] = part[:, kind * dq : (kind + 1) * dq]
                    lines[c, f : f + 1, :] = part[0:1, 3 * dq : 3 * dq + 128]
                    out[at, f * dq : (f + 1) * dq] = part[:, 3 * dq + 128 : width]
                half = 2 * rows
                low = pl.ds(pl.multiple_of(c * 4 * rows, 4 * rows), half)
                for i in range(2):
                    down[low, i * 512 : (i + 1) * 512] = v[i * half : (i + 1) * half, width:]
                c = (xl ^ e) * 16 + ((z - b) % 4) * 4 + (y - p) % 4
                at = pl.ds(pl.multiple_of(c * rows, rows), rows)
                v = block(seconds, p, b * 2 + e).astype(F32)
                for f in range(4):
                    up[at, f * ff : (f + 1) * ff] = v[f * rows : (f + 1) * rows, 0:ff]
                high = pl.ds(pl.multiple_of(c * 4 * rows + half, half), half)
                for i in range(2):
                    down[high, i * 512 : (i + 1) * 512] = v[i * half : (i + 1) * half, ff:]

    def line(b, f):
        return lines[b, pl.ds(f, 1), :]

    for i, ref in enumerate((l1g, l1b, l2g, l2b)):
        for half in range(2):
            total = line(2 * i + half, 0)
            for f in range(1, 4):
                total = total + line(2 * i + half, f)
            ref[half * 128 : (half + 1) * 128] = total.reshape(128)
    for half in range(2):
        v = line(8 + half, me).reshape(128)
        common[half * 128 : (half + 1) * 128] = v
        common_again[half * 128 : (half + 1) * 128] = v
    for i in range(3):
        b = 3 * me + i
        for half in range(2):
            at = (2 * i + half) * 128
            qb[at : at + 128] = line(10 + 2 * (b // 4) + half, b % 4).reshape(128)
    for i in range(8):
        f1b[i * 128 : (i + 1) * 128] = line(16 + i, me).reshape(128)


def pick(stacked, index):
    return lax.dynamic_index_in_dim(stacked, index, 0, keepdims=False)


def on_device(
    hidden_in,
    positions,
    out_grad,
    ln1_gain,
    ln1_bias,
    qkv_weight,
    qkv_bias,
    out_weight,
    out_bias,
    ln2_gain,
    ln2_bias,
    fc1_weight,
    fc1_bias,
    fc2_weight,
    fc2_bias,
):
    n_fs = 4
    n_ctx = 32
    ctx = lax.axis_index("ctx")
    me = lax.axis_index("fsdp")
    t = hidden_in.shape[1]
    d = hidden_in.shape[2]
    dq = d // n_fs
    ff = fc1_weight.shape[1] // n_fs
    tok = n_fs * t
    rows = dq // n_ctx
    me_one = me.astype(jnp.int32).reshape(1)

    flip = (positions[0, 0] // RUN) % 2 == 1

    def turned(v):
        return jnp.where(flip, jnp.concatenate([v[RUN:], v[:RUN]], 0), v)

    x_msg, cot_msg = whole_call(
        message_kernel,
        (shaped((t + 16, d), BF), shaped((t, d), BF)),
        1,
        (positions[0], hidden_in[0], out_grad[0], ln1_gain, ln1_bias, ln2_gain, ln2_bias, out_bias, fc2_bias, qkv_bias),
        "message",
    )
    x_xh = swap_xh(x_msg)
    cot_xh = swap_xh(cot_msg)
    x_all = [x_msg, x_xh, swap_core(x_msg), swap_core(x_xh)]
    cot_all = [cot_msg, cot_xh, swap_core(cot_msg), swap_core(cot_xh)]

    (qkv_columns,) = whole_call(columns_kernel, (shaped((n_fs, dq, 3 * dq), BF),), 0, (qkv_weight,), "columns")
    w_qkv = lax.all_to_all(qkv_columns, "fsdp", 0, 0).reshape(d, 3 * dq)

    def up_columns(diff):
        return lax.dynamic_slice(fc1_weight, (0, (me ^ diff) * ff), (dq, ff))

    def cross(v, diff):
        return lax.ppermute(v, ("ctx", "fsdp"), [(i, i ^ (16 * n_fs + diff)) for i in range(n_ctx * n_fs)])

    up_parts = lax.optimization_barrier((w_qkv,) + tuple(up_columns(i) for i in range(4)))
    w_qkv = up_parts[0]
    up_rel = [up_parts[1], cross(up_parts[3], 2), swap_core(up_parts[2]), cross(up_parts[4], 3)]

    def rel_of(owner):
        diff = jnp.bitwise_xor(me, owner)
        return (diff % 2) * 2 + diff // 2

    half = ROT // 2
    lane = jnp.arange(2 * HD) % HD
    turning = lane < ROT
    frequency = jnp.where(turning, 10000.0 ** (-2.0 * (lane % half).astype(F32) / ROT), 0.0)
    back = ctx % 2 == 1
    tables = []
    for even_run, odd_run in (
        (2 * ctx, 2 * ctx + 1),
        (jnp.where(back, 2 * n_ctx - 1 - ctx, ctx), jnp.where(back, ctx, 2 * n_ctx - 1 - ctx)),
    ):
        places = jnp.concatenate([even_run * RUN + jnp.arange(RUN), odd_run * RUN + jnp.arange(RUN)])
        phases = places.astype(F32)[:, None] * frequency[None, :]
        sines = jnp.sin(phases)
        tables += [jnp.cos(phases), jnp.where(lane < half, -sines, 0.0), jnp.where((lane >= half) & turning, sines, 0.0)]
    tables = jnp.stack(tables)

    attn_in, mlp_in, xhat, cot, short_all, flags, d_heads, bias = whole_call(
        prepare_kernel,
        (
            shaped((tok, d), BF),
            shaped((tok, d), BF),
            shaped((tok, d), F32),
            shaped((tok, d), BF),
            shaped((16, d), F32),
            shaped((n_fs, 8, 128), F32),
            shaped((tok, dq), F32),
            shaped((8, dq), F32),
        ),
        1,
        (me_one, *x_all, *cot_all, out_weight),
        "prepare",
        flops=2 * tok * d * dq,
    )
    (send,) = whole_call(
        project_kernel,
        (shaped((n_ctx, t + RUN, 2 * HD), BF),),
        0,
        (attn_in, w_qkv, d_heads, bias, flags, tables),
        "project",
        flops=2 * tok * d * 3 * dq,
    )
    gain_one, gain_two = short_all[0:1], short_all[2:3]
    both_bias = short_all[4:5] + short_all[5:6]
    folded = (flags[:, 0, 0] > 0.5).astype(jnp.int32)

    my_folded = pick(folded, ctx // 8)
    scal = jnp.stack([my_folded, ctx % 2]).astype(jnp.int32)
    up_rel = jnp.stack(up_rel)
    w_up = jnp.concatenate([pick(up_rel, rel_of(o)) for o in range(n_fs)], 0)
    recv = lax.all_to_all(send, "ctx", 0, 0)

    pre_act = mm(mlp_in, w_up) + fc1_bias.astype(F32)[None]
    act_float, pull_act = jax.vjp(lambda v: jax.nn.gelu(v, approximate=False), pre_act)
    activated = act_float.astype(BF)
    d_pre = pull_act(contract_cols(cot, fc2_weight))[0].astype(BF)
    fc2_grad = contract_rows(activated, cot).astype(BF)
    fc1_grad = contract_rows(mlp_in, d_pre).astype(BF)
    xl, z, y = ctx // 16, (ctx // 4) % 4, ctx % 4
    spot = {"xl": xl, "z": z, "y": y}

    def shift(v, axis, by):
        size, stride = {"y": (4, 1), "z": (4, 4), "xl": (2, 16)}[axis]
        perm = []
        for i in range(n_ctx):
            p = (i // stride) % size
            perm.append((i, i + ((p + by) % size - p) * stride))
        return lax.ppermute(v, "ctx", perm)

    recv, fc2_grad, scal = lax.optimization_barrier((recv, fc2_grad, scal))
    down_got = lax.all_to_all(fc2_grad.reshape(n_ctx, ff // n_ctx, d), "ctx", 0, 0)

    grads = attention(scal, recv)
    grads, down_got = lax.optimization_barrier((grads, down_got))
    home = lax.all_to_all(grads, "ctx", 0, 0)
    down_share = jnp.sum(down_got.astype(F32), 0).astype(BF)

    mlp_part = mm(activated, fc2_weight)
    d_norm_two = contract_cols(d_pre, w_up)
    early = jnp.stack(
        [
            jnp.sum(d_norm_two * xhat, 0),
            jnp.sum(d_norm_two, 0),
            jnp.sum(cot.astype(F32), 0),
            jnp.sum(d_pre, 0, dtype=F32),
        ]
    )
    early, down_share = lax.optimization_barrier((early, down_share))

    payload, d_norm_one, head_out, _ = whole_call(
        finish_kernel,
        (
            shaped((n_ctx, n_fs, rows, 4 * dq + 128 + ff), BF),
            shaped((tok, d), F32),
            shaped((tok, dq), BF),
            shaped((tok, 3 * dq), BF),
        ),
        1,
        (folded, home, tables, attn_in, cot, w_qkv, xhat, early, fc1_grad.reshape(n_fs, n_ctx, rows, ff)),
        "finish",
        flops=2 * tok * d * 7 * dq,
    )
    got = lax.all_to_all(payload, "ctx", 0, 0)

    def scatter_fsdp(parts):
        parts = parts.reshape(2, 2, t, d)
        here = parts[0] + swap_core(parts[1].astype(BF)).astype(F32)
        return here[0] + swap_xh(here[1].astype(BF)).astype(F32)

    block = scatter_fsdp(mlp_part + mm(head_out, out_weight))

    u = scatter_fsdp(d_norm_one * gain_one + d_norm_two * gain_two)
    width = 3 * dq + 128
    mine, theirs, out_share = whole_call(
        reduce_kernel,
        (shaped((2, rows, width + ff), BF), shaped((2, rows, width + ff), BF), shaped((n_fs, rows, dq), BF)),
        1,
        (me_one, got),
        "reduce",
    )
    from_core = swap_core(theirs)
    from_core, out_share = lax.optimization_barrier((from_core, out_share))
    keep = jnp.stack([mine[0], from_core[0]])
    away = jnp.stack([mine[1], from_core[1]])
    down_halves = down_share.reshape(2, 2 * rows, 2, d // 2).transpose(0, 2, 1, 3).reshape(2, 4 * rows, d // 2)
    extra = jnp.concatenate([out_share.reshape(n_fs * rows, dq), down_halves[0], down_halves[1]], 1)
    first, second = whole_call(
        arrange_kernel,
        (shaped((2, n_fs * rows, width + dq + d // 2), BF), shaped((2, n_fs * rows, ff + d // 2), BF)),
        1,
        (
            me_one,
            keep,
            swap_xh(away),
            shift(keep, "xl", 1),
            cross(away, 2),
            extra,
            shift(extra, "xl", 1),
        ),
        "arrange",
    )

    def joined(parts):
        v = jnp.concatenate([p[None] for p in parts], 0)
        return v.reshape((-1,) + v.shape[2:])

    def around(v, axis):
        return [v] + [shift(v, axis, s) for s in range(1, 4)]

    near = (around(first, "y"), around(second, "z"))
    near, block, u = lax.optimization_barrier((near, block, u))

    def both_ways(v, axis):
        ahead, behind = shift(v, axis, 1), shift(v, axis, 3)
        half = v.shape[0] // 2
        return [v, ahead, shift(ahead[:half], axis, 1), shift(behind[half:], axis, 3), behind]

    firsts = both_ways(joined(near[0]), "z")
    seconds = both_ways(joined(near[1]), "y")

    place = jnp.stack([me, xl, z, y]).astype(jnp.int32)
    grads_out = whole_call(
        expand_kernel,
        (shaped((dq, 3 * d), F32), shaped((dq, d), F32), shaped((dq, n_fs * ff), F32), shaped((ff, d), F32))
        + (shaped((dq,), F32),) * 6
        + (shaped((3 * dq,), F32), shaped((ff,), F32), shaped((n_ctx, n_fs, 128), F32)),
        1,
        (place, *firsts, *seconds),
        "expand",
    )
    qkv_out, out_out, fc1_out, fc2_out, l1g, l1b, l2g, l2b, out_bias_out, fc2_bias_out, qkv_bias_out, fc1_bias_out, _ = (
        grads_out
    )

    x_float = x_msg[:t].astype(F32)
    block_out = turned((x_float + block + both_bias).astype(BF))
    centred = x_float - jnp.mean(x_float, axis=-1, keepdims=True)
    rstd_own = lax.rsqrt(jnp.mean(centred * centred, axis=-1, keepdims=True) + NORM_EPS)
    xhat_own = centred * rstd_own
    dx = rstd_own * (
        u - jnp.mean(u, axis=-1, keepdims=True) - xhat_own * jnp.mean(u * xhat_own, axis=-1, keepdims=True)
    )
    input_grad = turned((cot_msg.astype(F32) + dx).astype(BF))

    return (
        block_out[None],
        input_grad[None],
        l1g,
        l1b,
        qkv_out,
        qkv_bias_out,
        out_out,
        out_bias_out,
        l2g,
        l2b,
        fc1_out,
        fc1_bias_out,
        fc2_out,
        fc2_bias_out,
    )


def solution(mesh):
    token = P("fsdp", "ctx", None)
    placed = (
        token,
        P("fsdp", "ctx"),
        token,
        P("fsdp"),
        P("fsdp"),
        P("fsdp", None),
        P("fsdp"),
        P("fsdp", None),
        P("fsdp"),
        P("fsdp"),
        P("fsdp"),
        P("fsdp", None),
        P("fsdp"),
        P("fsdp", None),
        P("fsdp"),
    )
    return jax.shard_map(
        on_device,
        mesh=mesh,
        in_specs=placed,
        out_specs=(
            token,
            token,
            P("fsdp"),
            P("fsdp"),
            P("fsdp", None),
            P("fsdp"),
            P("fsdp", None),
            P("fsdp"),
            P("fsdp"),
            P("fsdp"),
            P("fsdp", None),
            P("fsdp"),
            P("fsdp", None),
            P("fsdp"),
        ),
        check_vma=False,
    )
```

```python
import functools

import jax
import jax.numpy as jnp
from jax import lax
from jax.experimental import pallas as pl
from jax.experimental.pallas import tpu as pltpu
from jax.sharding import PartitionSpec as P

H = 16
HD = 64
ROT = 16
RUN = 64
RUNS = 64
NORM_EPS = 1e-05
BF = jnp.bfloat16
F32 = jnp.float32
NEG = -1e30

QT = 512
KT = 1024


def mm(a, b):
    return jnp.dot(a, b, preferred_element_type=F32)


def contract_rows(a, b):
    return lax.dot_general(a, b, (((0,), (0,)), ((), ())), preferred_element_type=F32)


def contract_cols(a, b):
    return lax.dot_general(a, b, (((1,), (1,)), ((), ())), preferred_element_type=F32)


def swap_xh(v):
    return lax.ppermute(v, "fsdp", [(i, i ^ 2) for i in range(4)])


def swap_core(v):
    return lax.ppermute(v, "fsdp", [(i, i ^ 1) for i in range(4)])


def attention_kernel(scal, recv, out, kv, qx, yx, dkv, oq, sbuf, dbuf):
    folded = scal[0]
    odd = scal[1]
    lane = lax.broadcasted_iota(jnp.int32, (RUN, 2 * HD), 1)
    low_half = lane < HD
    n_src = recv.shape[0]
    tiles = qx.shape[0]
    per_tile = QT // RUN

    def runs(c):
        turned = jnp.logical_and(folded == 1, c % 2 == 1)
        even = jnp.where(folded == 1, jnp.where(turned, 2 * n_src - 1 - c, c), 2 * c)
        other = jnp.where(folded == 1, jnp.where(turned, c, 2 * n_src - 1 - c), 2 * c + 1)
        return even, other

    def sort_in(c, carry):
        even, other = runs(c)
        kv[pl.ds(pl.multiple_of(even * RUN, RUN), RUN), :] = recv[c, 0:RUN, :]
        kv[pl.ds(pl.multiple_of(other * RUN, RUN), RUN), :] = recv[c, RUN : 2 * RUN, :]
        rank = jnp.where(odd == 1, other, even) // 2
        tile = rank // per_tile
        place = pl.multiple_of((rank % per_tile) * RUN, RUN)
        qd = recv[c, 2 * RUN : 3 * RUN, :]
        zero = jnp.zeros_like(qd)
        q_only = jnp.where(low_half, qd, zero)
        d_only = jnp.where(low_half, zero, qd)
        qx[tile, pl.ds(place, RUN), :] = q_only
        qx[tile, pl.ds(QT + place, RUN), :] = d_only
        yx[tile, pl.ds(place, RUN), :] = d_only
        yx[tile, pl.ds(QT + place, RUN), :] = q_only
        return carry

    lax.fori_loop(0, n_src, sort_in, 0)
    dkv[...] = jnp.zeros_like(dkv)

    row = lax.broadcasted_iota(jnp.int32, (QT, KT), 0)
    col = lax.broadcasted_iota(jnp.int32, (QT, KT), 1)
    row_place = (2 * (row // RUN) + odd) * RUN + row % RUN
    allowed = col <= row_place

    def fold(v, op):
        parts = [v[:, i * 128 : (i + 1) * 128] for i in range(KT // 128)]
        total = parts[0]
        for part in parts[1:]:
            total = op(total, part)
        return total

    def tile_step(j, carry):
        x = qx[j]
        y = yx[j]

        def products(k):
            keys = kv[pl.ds(pl.multiple_of(k * KT, KT), KT), :]
            both = contract_cols(x, keys)
            return both[:QT], both[QT:]

        def pass_one(k, top):
            s, d = products(k)
            sbuf[k] = s
            dbuf[k] = d
            return jnp.maximum(top, fold(s, jnp.maximum))

        top = lax.fori_loop(0, j, pass_one, jnp.full((QT, 128), NEG, F32), unroll=2 if j else 1)
        s, d = products(j)
        s = jnp.where(allowed, s, NEG)
        sbuf[j] = s
        dbuf[j] = d
        top = jnp.maximum(top, fold(s, jnp.maximum))
        top = jnp.max(top, axis=1, keepdims=True)

        def pass_two(k, sums):
            total, weighted = sums
            e = jnp.exp(sbuf[k] - top)
            sbuf[k] = e
            return total + fold(e, jnp.add), weighted + fold(e * dbuf[k], jnp.add)

        zero = jnp.zeros((QT, 128), F32)
        total, weighted = lax.fori_loop(0, j + 1, pass_two, (zero, zero), unroll=2)
        scale = 1.0 / jnp.sum(total, axis=1, keepdims=True)
        delta = jnp.sum(weighted, axis=1, keepdims=True) * scale

        def pass_three(k, acc):
            rows = pl.ds(pl.multiple_of(k * KT, KT), KT)
            p = sbuf[k] * scale
            ds = p * (dbuf[k] - delta)
            a = jnp.concatenate([p.astype(BF), ds.astype(BF)], axis=0)
            dkv[rows, :] += contract_rows(a, y)
            return acc + mm(a, kv[rows, :])

        acc = lax.fori_loop(0, j + 1, pass_three, jnp.zeros((2 * QT, 2 * HD), F32), unroll=2)
        wide = lax.broadcasted_iota(jnp.int32, (QT, 2 * HD), 1) < HD
        oq[pl.ds(j * QT, QT), :] = jnp.where(wide, acc[QT:], acc[:QT]).astype(BF)
        return carry

    for j in range(tiles):
        tile_step(j, 0)

    def sort_out(c, carry):
        even, other = runs(c)
        out[c, 0:RUN, :] = dkv[pl.ds(pl.multiple_of(even * RUN, RUN), RUN), :].astype(BF)
        out[c, RUN : 2 * RUN, :] = dkv[pl.ds(pl.multiple_of(other * RUN, RUN), RUN), :].astype(BF)
        rank = jnp.where(odd == 1, other, even) // 2
        out[c, 2 * RUN : 3 * RUN, :] = oq[pl.ds(pl.multiple_of(rank * RUN, RUN), RUN), :]
        return carry

    lax.fori_loop(0, n_src, sort_out, 0)


def attention(scal, recv):
    n_src = recv.shape[0]
    keys = n_src * 2 * RUN
    queries = n_src * RUN
    tiles = queries // QT
    return pl.pallas_call(
        attention_kernel,
        out_shape=jax.ShapeDtypeStruct(recv.shape, BF),
        in_specs=[pl.BlockSpec(memory_space=pltpu.SMEM), pl.BlockSpec(memory_space=pltpu.VMEM)],
        out_specs=pl.BlockSpec(memory_space=pltpu.VMEM),
        scratch_shapes=[
            pltpu.VMEM((keys, 2 * HD), BF),
            pltpu.VMEM((tiles, 2 * QT, 2 * HD), BF),
            pltpu.VMEM((tiles, 2 * QT, 2 * HD), BF),
            pltpu.VMEM((keys, 2 * HD), F32),
            pltpu.VMEM((queries, 2 * HD), BF),
            pltpu.VMEM((keys // KT, QT, KT), F32),
            pltpu.VMEM((keys // KT, QT, KT), F32),
        ],
        compiler_params=pltpu.CompilerParams(vmem_limit_bytes=60 * 1024 * 1024),
        cost_estimate=pl.CostEstimate(
            flops=14 * HD * queries * keys // 2,
            bytes_accessed=4 * recv.size,
            transcendentals=queries * keys // 2,
        ),
        name="attention",
    )(scal, recv)


def full_spec(v):
    zeros = (0,) * len(v.shape)
    return pl.BlockSpec(v.shape, lambda i: zeros)


def whole_call(body, out_shape, n_smem, args, name, flops=0):
    smem = [pl.BlockSpec(memory_space=pltpu.SMEM)] * n_smem
    return pl.pallas_call(
        body,
        grid=(1,),
        out_shape=out_shape,
        in_specs=smem + [full_spec(v) for v in args[n_smem:]],
        out_specs=jax.tree.map(full_spec, out_shape),
        compiler_params=pltpu.CompilerParams(vmem_limit_bytes=60 * 1024 * 1024),
        cost_estimate=pl.CostEstimate(
            flops=flops,
            bytes_accessed=sum(v.size * v.dtype.itemsize for v in args)
            + sum(v.size * v.dtype.itemsize for v in jax.tree.leaves(out_shape)),
            transcendentals=0,
        ),
        name=name,
    )(*args)


def shaped(shape, dtype):
    return jax.ShapeDtypeStruct(shape, dtype)


def message_kernel(places, x, g, l1g, l1b, l2g, l2b, ob, f2b, qb, x_out, g_out):
    run = places[0] // RUN
    flip = run % 2 == 1
    t, d = x.shape

    @pl.when(flip)
    def _():
        for src, dst in ((x, x_out), (g, g_out)):
            dst[0:RUN, :] = src[RUN:t, :]
            dst[RUN:t, :] = src[0:RUN, :]

    @pl.when(jnp.logical_not(flip))
    def _():
        x_out[0:t, :] = x[...]
        g_out[...] = g[...]

    n = l1g.shape[0]
    both = run + places[RUN] // RUN
    row = lax.broadcasted_iota(jnp.int32, (16, n), 0)
    short = jnp.where(jnp.logical_and(row == 9, both == RUNS - 1), 1.0, 0.0)
    lines = [ref[...].astype(F32).reshape(1, n) for ref in (l1g, l1b, l2g, l2b, ob, f2b)]
    bias = qb[...].astype(F32).reshape(1, 3 * n)
    lines += [bias[:, i * n : (i + 1) * n] for i in range(3)]
    for i, line in enumerate(lines):
        short = jnp.where(row == i, line, short)
    x_out[t:, 0:n] = short.astype(BF)
    x_out[t:, n:] = jnp.zeros((16, d - n), BF)


def columns_kernel(w, out):
    n_fs, _, width = out.shape
    part = width // 3
    for g in range(n_fs):
        for k in range(3):
            out[g, :, k * part : (k + 1) * part] = w[:, (k * n_fs + g) * part : (k * n_fs + g + 1) * part]


def project_kernel(me, x0, x1, x2, x3, g0, g1, g2, g3, w, wo, tables, send, attn_in, mlp_in, xhat, cot, short_out, flags):
    t = g0.shape[0]
    d = g0.shape[1]
    dq = w.shape[1] // 3
    n_fs = d // dq
    blocks = (x0, x1, x2, x3)
    cots = (g0, g1, g2, g3)
    f = me[0]
    shorts = [ref[t : t + 16, :].astype(F32) for ref in blocks]
    owners = [f, f ^ 2, f ^ 1, f ^ 3]
    by_owner = []
    for o in range(n_fs):
        total = shorts[0]
        for r in range(1, n_fs):
            total = jnp.where(owners[r] == o, shorts[r], total)
        by_owner.append(total[:, :dq])
    short = jnp.concatenate(by_owner, axis=1)
    short_out[...] = short
    for r in range(n_fs):
        flags[r] = jnp.broadcast_to(shorts[r][9:10, 0:128], (8, 128))
    gain_one, shift_one, gain_two, shift_two = (short[i : i + 1] for i in range(4))
    biases = []
    for kind in range(3):
        total = jnp.zeros((1, dq), F32)
        for b in range(3 * n_fs):
            o, i = divmod(b, 3)
            total = jnp.where(kind * n_fs + f == b, by_owner[o][6 + i : 7 + i], total)
        biases.append(total)

    for r in range(n_fs):
        rows = slice(r * t, (r + 1) * t)
        v = blocks[r][0:t, :].astype(F32)
        centred = v - jnp.mean(v, axis=1, keepdims=True)
        variance = jnp.mean(centred * centred, axis=1, keepdims=True)
        hat = centred * lax.rsqrt(variance + NORM_EPS)
        xhat[rows, :] = hat
        attn_in[rows, :] = (hat * gain_one + shift_one).astype(BF)
        mlp_in[rows, :] = (hat * gain_two + shift_two).astype(BF)
        cot[rows, :] = cots[r][...]

    a = attn_in[...]
    q_all = mm(a, w[:, :dq]) + biases[0]
    k_all = mm(a, w[:, dq : 2 * dq]) + biases[1]
    v_all = mm(a, w[:, 2 * dq :]) + biases[2]
    dh_all = contract_cols(cot[...], wo[...])
    low = lax.broadcasted_iota(jnp.int32, (t, 2 * HD), 1) < HD
    for r in range(n_fs):
        rows = slice(r * t, (r + 1) * t)
        is_folded = shorts[r][9:10, 0:1] > 0.5
        cos, up, down = (jnp.where(is_folded, tables[3 + i], tables[i]) for i in range(3))

        def turn(v):
            return v * cos + pltpu.roll(v, 2 * HD - ROT // 2, 1) * up + pltpu.roll(v, ROT // 2, 1) * down

        for b in range(dq // (2 * HD)):
            cols = slice(b * 2 * HD, (b + 1) * 2 * HD)
            q = turn(q_all[rows, cols]) * (HD ** (-0.5))
            k = turn(k_all[rows, cols])
            v = v_all[rows, cols]
            dh = dh_all[rows, cols]
            for side in range(2):
                if side == 0:
                    kv = jnp.where(low, k, pltpu.roll(v, HD, 1)).astype(BF)
                    qd = jnp.where(low, q, pltpu.roll(dh, HD, 1)).astype(BF)
                else:
                    kv = jnp.where(low, pltpu.roll(k, HD, 1), v).astype(BF)
                    qd = jnp.where(low, pltpu.roll(q, HD, 1), dh).astype(BF)
                at = r * 8 + (2 * b + side) * 2
                for half in range(2):
                    send[at + half, 0:t, :] = kv
                    send[at + half, t : t + RUN, :] = qd[half * RUN : (half + 1) * RUN]


def finish_kernel(folded, home, tables, attn_in, cot, w, xhat, early, fc1, payload, d_norm, head_out, d_proj):
    t = home.shape[1] - RUN
    dq = head_out.shape[1]
    n_fs = home.shape[0] // 8
    low = lax.broadcasted_iota(jnp.int32, (t, 2 * HD), 1) < HD
    for r in range(n_fs):
        rows = slice(r * t, (r + 1) * t)
        is_folded = folded[r] == 1
        cos, up, down = (jnp.where(is_folded, tables[3 + i], tables[i]) for i in range(3))

        def turn_back(v):
            return v * cos - (pltpu.roll(v, 2 * HD - ROT // 2, 1) * up + pltpu.roll(v, ROT // 2, 1) * down)

        for b in range(dq // (2 * HD)):
            cols = slice(b * 2 * HD, (b + 1) * 2 * HD)
            dkv, qo = [], []
            for side in range(2):
                at = r * 8 + (2 * b + side) * 2
                dkv.append(home[at, 0:t, :].astype(F32) + home[at + 1, 0:t, :].astype(F32))
                qo.append(jnp.concatenate([home[at, t : t + RUN, :], home[at + 1, t : t + RUN, :]], 0).astype(F32))
            d_q = jnp.where(low, qo[0], pltpu.roll(qo[1], HD, 1))
            o = jnp.where(low, pltpu.roll(qo[0], HD, 1), qo[1])
            d_k = jnp.where(low, dkv[0], pltpu.roll(dkv[1], HD, 1))
            d_v = jnp.where(low, pltpu.roll(dkv[0], HD, 1), dkv[1])
            head_out[rows, cols] = o.astype(BF)
            d_proj[rows, cols] = (turn_back(d_q) * (HD ** (-0.5))).astype(BF)
            d_proj[rows, dq + b * 2 * HD : dq + (b + 1) * 2 * HD] = turn_back(d_k).astype(BF)
            d_proj[rows, 2 * dq + b * 2 * HD : 2 * dq + (b + 1) * 2 * HD] = d_v.astype(BF)

    n_ctx, _, rows, _ = payload.shape
    d = attn_in.shape[1]
    width = d_proj.shape[1]
    dp = d_proj[...]
    c = contract_cols(dp, w[...])
    d_norm[...] = c
    gain = jnp.sum(c * xhat[...], axis=0, keepdims=True)
    shift = jnp.sum(c, axis=0, keepdims=True)
    bias = jnp.sum(dp.astype(F32), axis=0, keepdims=True)
    last = width + 128
    payload[:, :, :, width:last] = jnp.zeros((n_ctx, n_fs, rows, 128), BF)
    first = lax.broadcasted_iota(jnp.int32, (rows, 128), 0) == 0

    def put(b, f, v):
        payload[b, f, :, width:last] = jnp.where(first, v, 0.0).astype(BF)

    for f in range(n_fs):
        grad = contract_rows(attn_in[:, f * dq : (f + 1) * dq], dp)
        payload[:, f, :, 0:width] = grad.reshape(n_ctx, rows, width).astype(BF)
        grad = contract_rows(head_out[...], cot[:, f * dq : (f + 1) * dq])
        payload[:, f, :, last : last + dq] = grad.reshape(n_ctx, rows, dq).astype(BF)
        payload[:, f, :, last + dq :] = fc1[f]
        mine = [gain, shift, early[0:1, :], early[1:2, :], early[2:3, :]]
        for i, v in enumerate(mine):
            for half in range(2):
                at = f * dq + half * 128
                put(2 * i + half, f, v[:, at : at + 128])
        for i in range(6):
            put(10 + i, f, bias[:, i * 128 : (i + 1) * 128])
        for i in range(8):
            put(16 + i, f, early[3:4, i * 128 : (i + 1) * 128])


def reduce_kernel(me, got, mine, theirs, out_share):
    n_ctx, n_fs = got.shape[:2]
    dq = out_share.shape[2]
    width = 3 * dq + 128
    for f in range(n_fs):
        total = got[0, f].astype(F32)
        for c in range(1, n_ctx):
            total = total + got[c, f].astype(F32)
        total = total.astype(BF)
        diff = me[0] ^ f

        def put(pieces, at, total=total):
            pieces[at, :, 0:width] = total[:, 0:width]
            pieces[at, :, width:] = total[:, width + dq :]

        pl.when(diff % 2 == 0)(functools.partial(put, mine, diff // 2))
        pl.when(diff % 2 == 1)(functools.partial(put, theirs, diff // 2))
        out_share[f] = total[:, width : width + dq]


def arrange_kernel(me, keep, a, b, c, extra, extra_xl, first, second):
    dq = 256
    width = 3 * dq + 128
    for e, sources, more in (
        (0, (keep[0], keep[1], a[0], a[1]), extra),
        (1, (b[0], b[1], c[0], c[1]), extra_xl),
    ):
        sources = [v.astype(F32) for v in sources]
        lines = []
        for o in range(4):
            total = sources[0]
            for k in range(1, 4):
                total = jnp.where((me[0] ^ k) == o, sources[k], total)
            lines.append(total)
        owned = jnp.concatenate(lines, 0)
        more = more[...].astype(F32)
        at = width + dq
        first[e, :, 0:width] = owned[:, 0:width].astype(BF)
        first[e, :, width:at] = more[:, 0:dq].astype(BF)
        first[e, :, at:] = more[:, dq : dq + 512].astype(BF)
        second[e, :, 0 : 4 * dq] = owned[:, width:].astype(BF)
        second[e, :, 4 * dq :] = more[:, dq + 512 :].astype(BF)


def expand_kernel(place, *refs):
    firsts, seconds = refs[:5], refs[5:10]
    qkv, out, up, down, l1g, l1b, l2g, l2b, common, common_again, qb, f1b, lines = refs[10:]

    def block(parts, p, i):
        if p == 2:
            return parts[2][i] if i < 4 else parts[3][i - 4]
        return parts[(0, 1, 2, 4)[p]][i]

    n_ctx = lines.shape[0]
    dq = out.shape[0]
    ff = down.shape[1]
    rows = dq // n_ctx
    me, xl, z, y = (place[i] for i in range(4))
    width = 3 * dq + 128 + dq
    for p in range(4):
        for b in range(4):
            for e in range(2):
                c = (xl ^ e) * 16 + ((z - p) % 4) * 4 + (y - b) % 4
                at = pl.ds(pl.multiple_of(c * rows, rows), rows)
                v = block(firsts, p, b * 2 + e).astype(F32)
                for f in range(4):
                    part = v[f * rows : (f + 1) * rows]
                    for kind in range(3):
                        qkv[at, (kind * 4 + f) * dq : (kind * 4 + f + 1) * dq] = part[:, kind * dq : (kind + 1) * dq]
                    lines[c, f : f + 1, :] = part[0:1, 3 * dq : 3 * dq + 128]
                    out[at, f * dq : (f + 1) * dq] = part[:, 3 * dq + 128 : width]
                half = 2 * rows
                low = pl.ds(pl.multiple_of(c * 4 * rows, 4 * rows), half)
                for i in range(2):
                    down[low, i * 512 : (i + 1) * 512] = v[i * half : (i + 1) * half, width:]
                c = (xl ^ e) * 16 + ((z - b) % 4) * 4 + (y - p) % 4
                at = pl.ds(pl.multiple_of(c * rows, rows), rows)
                v = block(seconds, p, b * 2 + e).astype(F32)
                for f in range(4):
                    up[at, f * ff : (f + 1) * ff] = v[f * rows : (f + 1) * rows, 0:ff]
                high = pl.ds(pl.multiple_of(c * 4 * rows + half, half), half)
                for i in range(2):
                    down[high, i * 512 : (i + 1) * 512] = v[i * half : (i + 1) * half, ff:]

    def line(b, f):
        return lines[b, pl.ds(f, 1), :]

    for i, ref in enumerate((l1g, l1b, l2g, l2b)):
        for half in range(2):
            total = line(2 * i + half, 0)
            for f in range(1, 4):
                total = total + line(2 * i + half, f)
            ref[half * 128 : (half + 1) * 128] = total.reshape(128)
    for half in range(2):
        v = line(8 + half, me).reshape(128)
        common[half * 128 : (half + 1) * 128] = v
        common_again[half * 128 : (half + 1) * 128] = v
    for i in range(3):
        b = 3 * me + i
        for half in range(2):
            at = (2 * i + half) * 128
            qb[at : at + 128] = line(10 + 2 * (b // 4) + half, b % 4).reshape(128)
    for i in range(8):
        f1b[i * 128 : (i + 1) * 128] = line(16 + i, me).reshape(128)


def pick(stacked, index):
    return lax.dynamic_index_in_dim(stacked, index, 0, keepdims=False)


def on_device(
    hidden_in,
    positions,
    out_grad,
    ln1_gain,
    ln1_bias,
    qkv_weight,
    qkv_bias,
    out_weight,
    out_bias,
    ln2_gain,
    ln2_bias,
    fc1_weight,
    fc1_bias,
    fc2_weight,
    fc2_bias,
):
    n_fs = 4
    n_ctx = 32
    ctx = lax.axis_index("ctx")
    me = lax.axis_index("fsdp")
    t = hidden_in.shape[1]
    d = hidden_in.shape[2]
    dq = d // n_fs
    ff = fc1_weight.shape[1] // n_fs
    tok = n_fs * t
    rows = dq // n_ctx
    me_one = me.astype(jnp.int32).reshape(1)

    flip = (positions[0, 0] // RUN) % 2 == 1

    def turned(v):
        return jnp.where(flip, jnp.concatenate([v[RUN:], v[:RUN]], 0), v)

    x_msg, cot_msg = whole_call(
        message_kernel,
        (shaped((t + 16, d), BF), shaped((t, d), BF)),
        1,
        (positions[0], hidden_in[0], out_grad[0], ln1_gain, ln1_bias, ln2_gain, ln2_bias, out_bias, fc2_bias, qkv_bias),
        "message",
    )
    x_xh = swap_xh(x_msg)
    cot_xh = swap_xh(cot_msg)
    x_all = [x_msg, x_xh, swap_core(x_msg), swap_core(x_xh)]
    cot_all = [cot_msg, cot_xh, swap_core(cot_msg), swap_core(cot_xh)]

    (qkv_columns,) = whole_call(columns_kernel, (shaped((n_fs, dq, 3 * dq), BF),), 0, (qkv_weight,), "columns")
    w_qkv = lax.all_to_all(qkv_columns, "fsdp", 0, 0).reshape(d, 3 * dq)

    def up_columns(diff):
        return lax.dynamic_slice(fc1_weight, (0, (me ^ diff) * ff), (dq, ff))

    def cross(v, diff):
        return lax.ppermute(v, ("ctx", "fsdp"), [(i, i ^ (16 * n_fs + diff)) for i in range(n_ctx * n_fs)])

    up_parts = lax.optimization_barrier((w_qkv,) + tuple(up_columns(i) for i in range(4)))
    w_qkv = up_parts[0]
    up_rel = [up_parts[1], cross(up_parts[3], 2), swap_core(up_parts[2]), cross(up_parts[4], 3)]

    def rel_of(owner):
        diff = jnp.bitwise_xor(me, owner)
        return (diff % 2) * 2 + diff // 2

    half = ROT // 2
    lane = jnp.arange(2 * HD) % HD
    turning = lane < ROT
    frequency = jnp.where(turning, 10000.0 ** (-2.0 * (lane % half).astype(F32) / ROT), 0.0)
    back = ctx % 2 == 1
    tables = []
    for even_run, odd_run in (
        (2 * ctx, 2 * ctx + 1),
        (jnp.where(back, 2 * n_ctx - 1 - ctx, ctx), jnp.where(back, ctx, 2 * n_ctx - 1 - ctx)),
    ):
        places = jnp.concatenate([even_run * RUN + jnp.arange(RUN), odd_run * RUN + jnp.arange(RUN)])
        phases = places.astype(F32)[:, None] * frequency[None, :]
        sines = jnp.sin(phases)
        tables += [jnp.cos(phases), jnp.where(lane < half, -sines, 0.0), jnp.where((lane >= half) & turning, sines, 0.0)]
    tables = jnp.stack(tables)

    send, attn_in, mlp_in, xhat, cot, short_all, flags = whole_call(
        project_kernel,
        (
            shaped((n_ctx, t + RUN, 2 * HD), BF),
            shaped((tok, d), BF),
            shaped((tok, d), BF),
            shaped((tok, d), F32),
            shaped((tok, d), BF),
            shaped((16, d), F32),
            shaped((n_fs, 8, 128), F32),
        ),
        1,
        (me_one, *x_all, *cot_all, w_qkv, out_weight, tables),
        "project",
        flops=2 * tok * d * 4 * dq,
    )
    gain_one, gain_two = short_all[0:1], short_all[2:3]
    both_bias = short_all[4:5] + short_all[5:6]
    folded = (flags[:, 0, 0] > 0.5).astype(jnp.int32)

    my_folded = pick(folded, ctx // 8)
    scal = jnp.stack([my_folded, ctx % 2]).astype(jnp.int32)
    up_rel = jnp.stack(up_rel)
    w_up = jnp.concatenate([pick(up_rel, rel_of(o)) for o in range(n_fs)], 0)
    recv = lax.all_to_all(send, "ctx", 0, 0)

    pre_act = mm(mlp_in, w_up) + fc1_bias.astype(F32)[None]
    act_float, pull_act = jax.vjp(lambda v: jax.nn.gelu(v, approximate=False), pre_act)
    activated = act_float.astype(BF)
    d_pre = pull_act(contract_cols(cot, fc2_weight))[0].astype(BF)
    fc2_grad = contract_rows(activated, cot).astype(BF)
    fc1_grad = contract_rows(mlp_in, d_pre).astype(BF)
    xl, z, y = ctx // 16, (ctx // 4) % 4, ctx % 4
    spot = {"xl": xl, "z": z, "y": y}

    def shift(v, axis, by):
        size, stride = {"y": (4, 1), "z": (4, 4), "xl": (2, 16)}[axis]
        perm = []
        for i in range(n_ctx):
            p = (i // stride) % size
            perm.append((i, i + ((p + by) % size - p) * stride))
        return lax.ppermute(v, "ctx", perm)

    recv, fc2_grad, scal = lax.optimization_barrier((recv, fc2_grad, scal))
    down_got = lax.all_to_all(fc2_grad.reshape(n_ctx, ff // n_ctx, d), "ctx", 0, 0)

    grads = attention(scal, recv)
    grads, down_got = lax.optimization_barrier((grads, down_got))
    home = lax.all_to_all(grads, "ctx", 0, 0)
    down_share = jnp.sum(down_got.astype(F32), 0).astype(BF)

    mlp_part = mm(activated, fc2_weight)
    d_norm_two = contract_cols(d_pre, w_up)
    early = jnp.stack(
        [
            jnp.sum(d_norm_two * xhat, 0),
            jnp.sum(d_norm_two, 0),
            jnp.sum(cot.astype(F32), 0),
            jnp.sum(d_pre, 0, dtype=F32),
        ]
    )
    early, down_share = lax.optimization_barrier((early, down_share))

    payload, d_norm_one, head_out, _ = whole_call(
        finish_kernel,
        (
            shaped((n_ctx, n_fs, rows, 4 * dq + 128 + ff), BF),
            shaped((tok, d), F32),
            shaped((tok, dq), BF),
            shaped((tok, 3 * dq), BF),
        ),
        1,
        (folded, home, tables, attn_in, cot, w_qkv, xhat, early, fc1_grad.reshape(n_fs, n_ctx, rows, ff)),
        "finish",
        flops=2 * tok * d * 7 * dq,
    )
    got = lax.all_to_all(payload, "ctx", 0, 0)

    def scatter_fsdp(parts):
        parts = parts.reshape(2, 2, t, d)
        here = parts[0] + swap_core(parts[1].astype(BF)).astype(F32)
        return here[0] + swap_xh(here[1].astype(BF)).astype(F32)

    block = scatter_fsdp(mlp_part + mm(head_out, out_weight))

    u = scatter_fsdp(d_norm_one * gain_one + d_norm_two * gain_two)
    width = 3 * dq + 128
    mine, theirs, out_share = whole_call(
        reduce_kernel,
        (shaped((2, rows, width + ff), BF), shaped((2, rows, width + ff), BF), shaped((n_fs, rows, dq), BF)),
        1,
        (me_one, got),
        "reduce",
    )
    from_core = swap_core(theirs)
    from_core, out_share = lax.optimization_barrier((from_core, out_share))
    keep = jnp.stack([mine[0], from_core[0]])
    away = jnp.stack([mine[1], from_core[1]])
    down_halves = down_share.reshape(2, 2 * rows, 2, d // 2).transpose(0, 2, 1, 3).reshape(2, 4 * rows, d // 2)
    extra = jnp.concatenate([out_share.reshape(n_fs * rows, dq), down_halves[0], down_halves[1]], 1)
    first, second = whole_call(
        arrange_kernel,
        (shaped((2, n_fs * rows, width + dq + d // 2), BF), shaped((2, n_fs * rows, ff + d // 2), BF)),
        1,
        (
            me_one,
            keep,
            swap_xh(away),
            shift(keep, "xl", 1),
            cross(away, 2),
            extra,
            shift(extra, "xl", 1),
        ),
        "arrange",
    )

    def joined(parts):
        v = jnp.concatenate([p[None] for p in parts], 0)
        return v.reshape((-1,) + v.shape[2:])

    def around(v, axis):
        return [v] + [shift(v, axis, s) for s in range(1, 4)]

    near = (around(first, "y"), around(second, "z"))
    near, block, u = lax.optimization_barrier((near, block, u))

    def both_ways(v, axis):
        ahead, behind = shift(v, axis, 1), shift(v, axis, 3)
        half = v.shape[0] // 2
        return [v, ahead, shift(ahead[:half], axis, 1), shift(behind[half:], axis, 3), behind]

    firsts = both_ways(joined(near[0]), "z")
    seconds = both_ways(joined(near[1]), "y")

    place = jnp.stack([me, xl, z, y]).astype(jnp.int32)
    grads_out = whole_call(
        expand_kernel,
        (shaped((dq, 3 * d), F32), shaped((dq, d), F32), shaped((dq, n_fs * ff), F32), shaped((ff, d), F32))
        + (shaped((dq,), F32),) * 6
        + (shaped((3 * dq,), F32), shaped((ff,), F32), shaped((n_ctx, n_fs, 128), F32)),
        1,
        (place, *firsts, *seconds),
        "expand",
    )
    qkv_out, out_out, fc1_out, fc2_out, l1g, l1b, l2g, l2b, out_bias_out, fc2_bias_out, qkv_bias_out, fc1_bias_out, _ = (
        grads_out
    )

    x_float = x_msg[:t].astype(F32)
    block_out = turned((x_float + block + both_bias).astype(BF))
    centred = x_float - jnp.mean(x_float, axis=-1, keepdims=True)
    rstd_own = lax.rsqrt(jnp.mean(centred * centred, axis=-1, keepdims=True) + NORM_EPS)
    xhat_own = centred * rstd_own
    dx = rstd_own * (
        u - jnp.mean(u, axis=-1, keepdims=True) - xhat_own * jnp.mean(u * xhat_own, axis=-1, keepdims=True)
    )
    input_grad = turned((cot_msg.astype(F32) + dx).astype(BF))

    return (
        block_out[None],
        input_grad[None],
        l1g,
        l1b,
        qkv_out,
        qkv_bias_out,
        out_out,
        out_bias_out,
        l2g,
        l2b,
        fc1_out,
        fc1_bias_out,
        fc2_out,
        fc2_bias_out,
    )


def solution(mesh):
    token = P("fsdp", "ctx", None)
    placed = (
        token,
        P("fsdp", "ctx"),
        token,
        P("fsdp"),
        P("fsdp"),
        P("fsdp", None),
        P("fsdp"),
        P("fsdp", None),
        P("fsdp"),
        P("fsdp"),
        P("fsdp"),
        P("fsdp", None),
        P("fsdp"),
        P("fsdp", None),
        P("fsdp"),
    )
    return jax.shard_map(
        on_device,
        mesh=mesh,
        in_specs=placed,
        out_specs=(
            token,
            token,
            P("fsdp"),
            P("fsdp"),
            P("fsdp", None),
            P("fsdp"),
            P("fsdp", None),
            P("fsdp"),
            P("fsdp"),
            P("fsdp"),
            P("fsdp", None),
            P("fsdp"),
            P("fsdp", None),
            P("fsdp"),
        ),
        check_vma=False,
    )
```
